32 devices in a mesh: nbhd: 8 (over y, x, core), sub: 4 (over z).
Axes of the slice: x: 2, y: 2, z: 4, core: 2. Of those that a mesh axis runs over, the one named last changes fastest.
Arguments:
- snap_init: bfloat16 [8, 16, 16, 96, 128], P('nbhd', 'sub'), may hold values from -8 to 8
- channel_map: int32 [8, 16, 16, 96], P('nbhd', 'sub'), may hold values from 0 to 3
- yface_vals: bfloat16 [8, 96, 128], P('nbhd'), may hold values from -6 to 6
- zface_vals: bfloat16 [8, 16, 128], P('nbhd'), may hold values from -6 to 6
- face_of: int32 [8, 128], P('nbhd'), may hold values from 0 to 3
- start_block: float32 [8, 128, 32], P('nbhd'), may hold values from -6 to 6
- correlation: int32 [8, 8], replicated, may hold values 0 or 1
Outputs:
- owner_basis: bfloat16 [8, 4, 8, 32, 768], P('nbhd', 'sub')
The draws below stay inside these ranges and needn't reach their ends.
All inputs are finite; a program needn't handle non-finite values.
Results may differ from the reference program's by a relative error of at most 0.0072.
Values may be sent and summed in bfloat16 or wider, within the bound.
No kernel may reach another device: no remote copies, remote signals or barrier semaphores. Data moves between devices by JAX's collectives and lax.ppermute only.
A program may use at most 128 MiB of HBM per device.

```python
import math
import jax
import jax.numpy as jnp
from jax import lax

NY = 16
NZ = 96
NSNAP = 128
MODES = 32
SWEEPS = 3
ITERS = 4
NBHDS = 8
NXR = 16
PIECE = 768


def sine_profile(count, waves):
    position = jnp.arange(1, count + 1, dtype=jnp.float32) / (count + 1.0)
    return jnp.sin(math.pi * position[None, :, None] * waves[:, None, :])


def draw_snap_init(key, part):
    shape = (NBHDS, NXR, NY, NZ, NSNAP)
    keys = jax.random.split(key, 6)
    wave_x = jax.random.randint(keys[0], (NBHDS, NSNAP), 1, 7).astype(jnp.float32)
    wave_y = jax.random.randint(keys[1], (NBHDS, NSNAP), 1, 6).astype(jnp.float32)
    wave_z = jax.random.randint(keys[2], (NBHDS, NSNAP), 1, 7).astype(jnp.float32)
    along_x = sine_profile(NXR, wave_x)[:, :, None, None, :]
    along_y = sine_profile(NY, wave_y)[:, None, :, None, :]
    along_z = sine_profile(NZ, wave_z)[:, None, None, :, :]
    smooth = along_x * along_y * along_z
    rough_share = jnp.exp(jax.random.uniform(keys[3], (NBHDS, 1, 1, 1, NSNAP), jnp.float32, math.log(0.1), math.log(0.7)))
    scales = jnp.exp(jax.random.uniform(keys[4], (NBHDS, 1, 1, 1, NSNAP), jnp.float32, math.log(0.3), math.log(3.0)))
    local = jax.random.normal(keys[5], shape, jnp.float32)
    field = smooth + rough_share * local
    return jnp.clip(field * scales, -8.0, 8.0).astype(jnp.bfloat16)


def plant(values, stream_key, least, high):
    place = [jax.random.randint(jax.random.fold_in(stream_key, axis), (), 0, length) for axis, length in enumerate(values.shape)]
    widest = values.shape.index(max(values.shape))
    beside = place[:widest] + [(place[widest] + 1) % values.shape[widest]] + place[widest + 1:]
    return values.at[tuple(place)].set(least).at[tuple(beside)].set(high)


def shard_levels(rng, shape, cuts, smallest, high):
    def one(axis_at, blocks):
        heights = jax.random.uniform(jax.random.fold_in(jax.random.fold_in(rng, 6), axis_at), (blocks,), jnp.float32, smallest / len(cuts), high / len(cuts))
        return jnp.repeat(jnp.exp(heights), shape[axis_at] // blocks).reshape((-1,) + (1,) * (len(shape) - axis_at - 1))

    gain = one(*cuts[0])
    for cut in cuts[1:]:
        gain = gain * one(*cut)
    return gain


def scatter_about(own_key, shape, scale, bound, shards=(), kind=jnp.bfloat16):
    level = shard_levels(own_key, shape, shards, -0.22, 0.18) if shards else 1.0
    result = jax.random.normal(own_key, shape, jnp.float32) * scale * level
    return jnp.minimum(jnp.maximum(result, -bound), bound).astype(kind)


def setup_inputs(seed: int = 0) -> dict:
    seeds = jax.random.split(jax.random.key(seed), 8)
    snap_init = draw_snap_init(jax.random.fold_in(seeds[7], 71), 0)
    channel_map = plant(jax.random.randint(seeds[1], (NBHDS, NXR, NY, NZ), 0, 4), jax.random.fold_in(seeds[1], 1), 0, 3).astype(jnp.int32)
    yface_vals = scatter_about(seeds[2], (NBHDS, NZ, NSNAP), 1.0, 6.0, ((0, 8),))
    zface_vals = scatter_about(seeds[3], (NBHDS, NY, NSNAP), 1.0, 6.0, ((0, 8),))
    face_of = plant(jax.random.randint(seeds[4], (NBHDS, NSNAP), 0, 4), jax.random.fold_in(seeds[4], 1), 0, 3).astype(jnp.int32)
    start_block = scatter_about(seeds[5], (NBHDS, NSNAP, MODES), 1.0, 6.0, ((0, 8),), jnp.float32)
    correlation = plant((jax.random.randint(seeds[6], (NBHDS, NBHDS), 0, 2) < 1).astype(jnp.int32), jax.random.fold_in(seeds[6], 1), 0, 1)
    return {"snap_init": snap_init, "channel_map": channel_map, "yface_vals": yface_vals, "zface_vals": zface_vals, "face_of": face_of, "start_block": start_block, "correlation": correlation}


def harmonic(left_k, right_k):
    return 2.0 * left_k * right_k / (left_k + right_k)

def face_terms(field_ext, kappa_ext, first_plane, plane_count, ghosts):
    length = field_ext.shape[0]
    plane_ids = first_plane + jnp.arange(length, dtype=jnp.int32)
    inside = (plane_ids >= 0) & (plane_ids < plane_count)
    kappa = jnp.where(inside[:, None, None], kappa_ext, jnp.float32(1.0))
    centre = kappa[1:-1]
    x_lower = jnp.where(inside[:-2, None, None], harmonic(centre, kappa[:-2]), centre)
    x_upper = jnp.where(inside[2:, None, None], harmonic(centre, kappa[2:]), centre)
    y_inner = harmonic(centre[:, 1:], centre[:, :-1])
    y_lower = jnp.concatenate([centre[:, :1], y_inner], axis=1)
    y_upper = jnp.concatenate([y_inner, centre[:, -1:]], axis=1)
    z_inner = harmonic(centre[:, :, 1:], centre[:, :, :-1])
    z_lower = jnp.concatenate([centre[:, :, :1], z_inner], axis=2)
    z_upper = jnp.concatenate([z_inner, centre[:, :, -1:]], axis=2)
    middle = field_ext[1:-1].astype(jnp.float32)
    count, rows_y, rows_z, width = middle.shape
    ghost_ylo, ghost_yhi, ghost_zlo, ghost_zhi = ghosts
    below_y = jnp.concatenate([jnp.broadcast_to(ghost_ylo, (count, 1, rows_z, width)), middle[:, :-1]], axis=1)
    above_y = jnp.concatenate([middle[:, 1:], jnp.broadcast_to(ghost_yhi, (count, 1, rows_z, width))], axis=1)
    below_z = jnp.concatenate([jnp.broadcast_to(ghost_zlo[:, None, :], (count, rows_y, 1, width)), middle[:, :, :-1]], axis=2)
    above_z = jnp.concatenate([middle[:, :, 1:], jnp.broadcast_to(ghost_zhi[:, None, :], (count, rows_y, 1, width))], axis=2)
    numer = x_lower[..., None] * field_ext[:-2].astype(jnp.float32) + x_upper[..., None] * field_ext[2:].astype(jnp.float32) + y_lower[..., None] * below_y + y_upper[..., None] * above_y + z_lower[..., None] * below_z + z_upper[..., None] * above_z
    denom = x_lower + x_upper + y_lower + y_upper + z_lower + z_upper
    return (numer, denom, middle, inside[1:-1])

def relax(field_ext, kappa_ext, first_plane, plane_count, ghosts):
    numer, denom, middle, inside = face_terms(field_ext, kappa_ext, first_plane, plane_count, ghosts)
    updated = numer / denom[..., None]
    return jnp.where(inside[:, None, None, None], updated, jnp.float32(0.0)).astype(jnp.bfloat16)

def stiffness(field_ext, kappa_ext, first_plane, plane_count):
    rows_y, rows_z, width = (field_ext.shape[1], field_ext.shape[2], field_ext.shape[3])
    zero_y = jnp.zeros((rows_z, width), jnp.float32)
    zero_z = jnp.zeros((rows_y, width), jnp.float32)
    numer, denom, middle, inside = face_terms(field_ext, kappa_ext, first_plane, plane_count, (zero_y, zero_y, zero_z, zero_z))
    return (denom[..., None] * middle - numer).astype(jnp.bfloat16)

def make_ghosts(y_values, z_values, face_ids):
    y_float = y_values.astype(jnp.float32)
    z_float = z_values.astype(jnp.float32)
    picks = [(face_ids == side).astype(jnp.float32)[None, :] for side in range(4)]
    return (y_float * picks[0], y_float * picks[1], z_float * picks[2], z_float * picks[3])

def gram_terms(snapshots, kappa, stiff_apply):
    width = snapshots.shape[-1]
    flat = snapshots.reshape(-1, width)
    weighted = (flat * (kappa.reshape(-1, 1) / 16.0)).astype(jnp.bfloat16)
    stiff_flat = stiff_apply.reshape(-1, width)
    dims = (((0,), (0,)), ((), ()))
    mass_part = lax.dot_general(flat.astype(jnp.float32), weighted.astype(jnp.float32), dims, preferred_element_type=jnp.float32)
    stiff_part = lax.dot_general(flat.astype(jnp.float32), stiff_flat.astype(jnp.float32), dims, preferred_element_type=jnp.float32)
    return (mass_part, stiff_part)

def subspace(mass_sum, stiff_sum, start, cell_count):
    highest = lax.Precision.HIGHEST
    mass_gram = mass_sum / cell_count
    stiff_gram = (stiff_sum + stiff_sum.T) * (0.5 / cell_count)
    factor = jnp.linalg.cholesky(stiff_gram)
    mode_block = start
    for step in range(ITERS):
        right_side = jnp.dot(mass_gram, mode_block, precision=highest)
        solved = jax.scipy.linalg.cho_solve((factor, True), right_side)
        inner = jnp.dot(solved.T, jnp.dot(mass_gram, solved, precision=highest), precision=highest)
        inner = 0.5 * (inner + inner.T)
        lower = jnp.linalg.cholesky(inner)
        mode_block = jax.scipy.linalg.solve_triangular(lower, solved.T, lower=True).T
    return mode_block

def reference(snap_init, channel_map, yface_vals, zface_vals, face_of, start_block, correlation):

    def single(items):
        init, cmap, y_values, z_values, face_ids, start = items
        plane_count = init.shape[0]
        kappa = jnp.exp2(2.0 * cmap.astype(jnp.float32))
        ghosts = make_ghosts(y_values, z_values, face_ids)
        kappa_ext = jnp.pad(kappa, ((1, 1), (0, 0), (0, 0)))
        pad_spec = ((1, 1), (0, 0), (0, 0), (0, 0))
        state = init
        for sweep_no in range(SWEEPS):
            state = relax(jnp.pad(state, pad_spec), kappa_ext, -1, plane_count, ghosts)
        stiff_apply = stiffness(jnp.pad(state, pad_spec), kappa_ext, -1, plane_count)
        mass_part, stiff_part = gram_terms(state, kappa, stiff_apply)
        cell_count = float(plane_count * state.shape[1] * state.shape[2])
        mode_block = subspace(mass_part, stiff_part, start, cell_count)
        blocks = state.reshape(-1, NBHDS, PIECE, state.shape[-1]).astype(jnp.float32)
        modes_low = mode_block.astype(jnp.bfloat16).astype(jnp.float32)
        basis = jnp.einsum('gpcs,sm->gpmc', blocks, modes_low)
        return basis.astype(jnp.bfloat16)
    built = lax.map(single, (snap_init, channel_map, yface_vals, zface_vals, face_of, start_block))
    mask = correlation.T.astype(jnp.bfloat16)
    return jnp.transpose(built, (2, 1, 0, 3, 4)) * mask[:, None, :, None, None]
```

```python
import functools

import jax
import jax.numpy as jnp
from jax import lax
from jax.experimental import pallas as pl
from jax.experimental.pallas import tpu as pltpu
from jax.sharding import PartitionSpec as P

SWEEPS = 3
ITERS = 4


def with_halo(cells, sides, width):
    for axis, dim in sides:
        count = lax.axis_size(axis)
        ends = count - 1
        head = lax.slice_in_dim(cells, 0, width, axis=dim)
        tail = lax.slice_in_dim(cells, cells.shape[dim] - width, cells.shape[dim], axis=dim)
        cells = jnp.concatenate(
            [
                lax.ppermute(tail, axis, [(i, (i + 1) % count) for i in range(ends)]),
                cells,
                lax.ppermute(head, axis, [((i + 1) % count, i) for i in range(ends)]),
            ],
            axis=dim,
        )
    return cells


def harmonic(left_k, right_k):
    return 2.0 * left_k * right_k / (left_k + right_k)


def face_terms(field_ext, kappa_ext, first_plane, plane_count, ghosts):
    length = field_ext.shape[0]
    plane_ids = first_plane + jnp.arange(length, dtype=jnp.int32)
    inside = (plane_ids >= 0) & (plane_ids < plane_count)
    kappa = jnp.where(inside[:, None, None], kappa_ext, jnp.float32(1.0))
    centre = kappa[1:-1]
    x_lower = jnp.where(inside[:-2, None, None], harmonic(centre, kappa[:-2]), centre)
    x_upper = jnp.where(inside[2:, None, None], harmonic(centre, kappa[2:]), centre)
    y_inner = harmonic(centre[:, 1:], centre[:, :-1])
    y_lower = jnp.concatenate([centre[:, :1], y_inner], axis=1)
    y_upper = jnp.concatenate([y_inner, centre[:, -1:]], axis=1)
    z_inner = harmonic(centre[:, :, 1:], centre[:, :, :-1])
    z_lower = jnp.concatenate([centre[:, :, :1], z_inner], axis=2)
    z_upper = jnp.concatenate([z_inner, centre[:, :, -1:]], axis=2)
    middle = field_ext[1:-1].astype(jnp.float32)
    count, rows_y, rows_z, width = middle.shape
    ghost_ylo, ghost_yhi, ghost_zlo, ghost_zhi = ghosts
    below_y = jnp.concatenate(
        [jnp.broadcast_to(ghost_ylo, (count, 1, rows_z, width)), middle[:, :-1]], axis=1
    )
    above_y = jnp.concatenate(
        [middle[:, 1:], jnp.broadcast_to(ghost_yhi, (count, 1, rows_z, width))], axis=1
    )
    below_z = jnp.concatenate(
        [jnp.broadcast_to(ghost_zlo[:, None, :], (count, rows_y, 1, width)), middle[:, :, :-1]],
        axis=2,
    )
    above_z = jnp.concatenate(
        [middle[:, :, 1:], jnp.broadcast_to(ghost_zhi[:, None, :], (count, rows_y, 1, width))],
        axis=2,
    )
    numer = (
        x_lower[..., None] * field_ext[:-2].astype(jnp.float32)
        + x_upper[..., None] * field_ext[2:].astype(jnp.float32)
        + y_lower[..., None] * below_y
        + y_upper[..., None] * above_y
        + z_lower[..., None] * below_z
        + z_upper[..., None] * above_z
    )
    denom = x_lower + x_upper + y_lower + y_upper + z_lower + z_upper
    return (numer, denom, middle, inside[1:-1])


def relax(field_ext, kappa_ext, first_plane, plane_count, ghosts):
    numer, denom, middle, inside = face_terms(
        field_ext, kappa_ext, first_plane, plane_count, ghosts
    )
    updated = numer / denom[..., None]
    return jnp.where(inside[:, None, None, None], updated, jnp.float32(0.0)).astype(jnp.bfloat16)


def stiffness(field_ext, kappa_ext, first_plane, plane_count):
    rows_y, rows_z, width = (field_ext.shape[1], field_ext.shape[2], field_ext.shape[3])
    zero_y = jnp.zeros((rows_z, width), jnp.float32)
    zero_z = jnp.zeros((rows_y, width), jnp.float32)
    numer, denom, middle, inside = face_terms(
        field_ext, kappa_ext, first_plane, plane_count, (zero_y, zero_y, zero_z, zero_z)
    )
    return (denom[..., None] * middle - numer).astype(jnp.bfloat16)


def make_ghosts(y_values, z_values, face_ids):
    y_float = y_values.astype(jnp.float32)
    z_float = z_values.astype(jnp.float32)
    picks = [(face_ids == side).astype(jnp.float32)[None, :] for side in range(4)]
    return (y_float * picks[0], y_float * picks[1], z_float * picks[2], z_float * picks[3])


def gram_terms(snapshots, kappa, stiff_apply):
    width = snapshots.shape[-1]
    flat = snapshots.reshape(-1, width)
    weighted = (flat * (kappa.reshape(-1, 1) / 16.0)).astype(jnp.bfloat16)
    stiff_flat = stiff_apply.reshape(-1, width)
    dims = (((0,), (0,)), ((), ()))
    mass_part = lax.dot_general(flat, weighted, dims, preferred_element_type=jnp.float32)
    stiff_part = lax.dot_general(flat, stiff_flat, dims, preferred_element_type=jnp.float32)
    return (mass_part, stiff_part)


def lane_copy(tile, lane):
    return jnp.broadcast_to(tile[:, lane : lane + 1], (8, 128))


def row_copy(tile, row):
    return jnp.broadcast_to(tile[row : row + 1, :], (8, tile.shape[1]))


def solve_spd(left, right):
    size = left.shape[0]
    count = size // 8
    sub = lax.broadcasted_iota(jnp.int32, (8, 128), 0)
    lhs = [left[8 * t : 8 * t + 8] for t in range(count)]
    rhs = [right[8 * t : 8 * t + 8] for t in range(count)]
    for k in range(count):
        cols = [lane_copy(lhs[k], 8 * k + j) for j in range(8)]
        panel_l, panel_r = lhs[k], rhs[k]
        for j in range(8):
            recip = 1.0 / row_copy(cols[j], j)
            here = sub == j
            mult = jnp.where(here, recip, -cols[j] * recip)
            for l in range(j + 1, 8):
                cols[l] = jnp.where(here, 0.0, cols[l]) + mult * row_copy(cols[l], j)
            panel_l = jnp.where(here, 0.0, panel_l) + mult * row_copy(panel_l, j)
            panel_r = jnp.where(here, 0.0, panel_r) + mult * row_copy(panel_r, j)
        rows_l = [row_copy(panel_l, j) for j in range(8)]
        rows_r = [row_copy(panel_r, j) for j in range(8)]
        order = list(range(k + 1, count)) + list(range(k))
        for t in order:
            tile_cols = [lane_copy(lhs[t], 8 * k + j) for j in range(8)]
            if k + 1 < count:
                lhs[t] = lhs[t] - tree([tile_cols[j] * rows_l[j] for j in range(8)])
            rhs[t] = rhs[t] - tree([tile_cols[j] * rows_r[j] for j in range(8)])
        lhs[k], rhs[k] = panel_l, panel_r
    return jnp.concatenate(rhs, axis=0)


def tree(terms):
    while len(terms) > 1:
        terms = [a + b for a, b in zip(terms[::2], terms[1::2])] + terms[len(terms) & ~1 :]
    return terms[0]


def whiten(inner, block):
    size = inner.shape[0]
    count = size // 8
    sub = lax.broadcasted_iota(jnp.int32, (8, 128), 0)
    lhs = [inner[8 * t : 8 * t + 8] for t in range(count)]
    rhs = [block[8 * t : 8 * t + 8] for t in range(count)]
    done = []
    for k in range(count):
        live = range(k, count)
        cols = {t: [lane_copy(lhs[t], 8 * k + j) for j in range(8)] for t in live}
        scale = None
        for j in range(8):
            pivot = row_copy(cols[k][j], j)
            recip = 1.0 / pivot
            root = lax.rsqrt(pivot)
            scale = root if scale is None else jnp.where(sub >= j, root, scale)
            head = {l: row_copy(cols[k][l], j) for l in range(j + 1, 8)}
            row_l, row_r = row_copy(lhs[k], j), row_copy(rhs[k], j)
            for t in live:
                mult = cols[t][j] * recip
                if t == k:
                    mult = jnp.where(sub > j, mult, 0.0)
                for l in range(j + 1, 8):
                    cols[t][l] = cols[t][l] - mult * head[l]
                lhs[t] = lhs[t] - mult[:, : row_l.shape[1]] * row_l
                rhs[t] = rhs[t] - mult * row_r
        done.append(rhs[k] * scale)
    return jnp.concatenate(done, axis=0)


def dot(a, b, dims):
    return lax.dot_general(
        a, b, (dims, ((), ())), precision=lax.Precision.HIGHEST, preferred_element_type=jnp.float32
    )


def modes_kernel(cell_count, *refs):
    *part_refs, start_ref, snap_ref, out_ref = refs
    mass = part_refs[0][0]
    stiff = part_refs[0][1]
    for part in part_refs[1:]:
        mass = mass + part[0]
        stiff = stiff + part[1]
    mass = mass * (1.0 / cell_count)
    stiff = (stiff + stiff.T) * (0.5 / cell_count)
    step = solve_spd(stiff, mass)
    form = dot(step, dot(mass, step, ((1,), (0,))), ((0,), (0,)))
    block = start_ref[...]
    for _ in range(ITERS):
        weighted = dot(block, form, ((1,), (0,)))
        solved = dot(block, step, ((1,), (1,)))
        inner = dot(weighted, block, ((1,), (1,)))
        block = whiten(inner, solved)
    modes = block.astype(jnp.bfloat16)
    for piece in range(out_ref.shape[0]):
        out_ref[piece] = lax.dot_general(
            modes, snap_ref[piece], (((1,), (1,)), ((), ())), preferred_element_type=jnp.float32
        ).astype(jnp.bfloat16)


def on_device(snap_init, channel_map, yface_vals, zface_vals, face_of, start_block, correlation):
    initial = snap_init[0]
    class_map = channel_map[0]
    planes = initial.shape[0]
    plane_count = planes * lax.axis_size("sub")
    base_plane = lax.axis_index("sub") * planes
    ghosts = make_ghosts(yface_vals[0], zface_vals[0], face_of[0])
    class_ext = with_halo(class_map, (("sub", 0),), 1)
    kappa_edge = jnp.exp2(2.0 * class_ext.astype(jnp.float32))
    state = initial
    for sweep_no in range(SWEEPS):
        padded = with_halo(state, (("sub", 0),), 1)
        state = relax(padded, kappa_edge, base_plane - 1, plane_count, ghosts)
    field_edge = with_halo(state, (("sub", 0),), 1)
    snapshots = field_edge[1:-1]
    kappa_local = kappa_edge[1:-1]
    stiff_apply = stiffness(field_edge, kappa_edge, base_plane - 1, plane_count)
    mass_part, stiff_part = gram_terms(snapshots, kappa_local, stiff_apply)
    own = jnp.stack([mass_part, stiff_part])
    subs = lax.axis_size("sub")
    parts = [own] + [
        lax.ppermute(own, "sub", [(i, (i + shift) % subs) for i in range(subs)])
        for shift in range(1, subs)
    ]
    cell_count = float(plane_count * snapshots.shape[1] * snapshots.shape[2])
    owner_count = lax.axis_size("nbhd")
    width = snapshots.shape[-1]
    piece_cells = snapshots.size // width // owner_count
    blocks = snapshots.reshape(owner_count, piece_cells, width)
    modes = start_block.shape[-1]
    pieces = pl.pallas_call(
        functools.partial(modes_kernel, cell_count),
        out_shape=jax.ShapeDtypeStruct((owner_count, modes, piece_cells), jnp.bfloat16),
        compiler_params=pltpu.CompilerParams(vmem_limit_bytes=32 * 2**20),
    )(*parts, start_block[0].T, blocks)
    received = lax.all_to_all(pieces, "nbhd", split_axis=0, concat_axis=0, tiled=True)
    column = lax.dynamic_slice_in_dim(correlation, lax.axis_index("nbhd"), 1, axis=1)[:, 0]
    result = received * column.astype(jnp.bfloat16)[:, None, None]
    return result[None, None]


def solution(mesh):
    return jax.shard_map(
        on_device,
        mesh=mesh,
        in_specs=(
            P("nbhd", "sub", None, None, None),
            P("nbhd", "sub", None, None),
            P("nbhd", None, None),
            P("nbhd", None, None),
            P("nbhd", None),
            P("nbhd", None, None),
            P(),
        ),
        out_specs=P("nbhd", "sub", None, None, None),
        check_vma=False,
    )
```

```python
import functools

import jax
import jax.numpy as jnp
from jax import lax
from jax.experimental import pallas as pl
from jax.experimental.pallas import tpu as pltpu
from jax.sharding import PartitionSpec as P

SWEEPS = 3
ITERS = 4


def harmonic(left_k, right_k):
    return 2.0 * left_k * right_k / (left_k + right_k)


def coefficients(classes, planes, first, last):
    kappa = jnp.exp2(2.0 * classes.astype(jnp.float32))
    length = classes.shape[0]
    depth = (length - planes) // 2
    place = jnp.arange(length, dtype=jnp.int32)[:, None, None]
    outside = (first & (place < depth)) | (last & (place >= depth + planes))
    x_face = harmonic(kappa[1:], kappa[:-1])
    x_face = jnp.where(outside[:-1], kappa[1:], jnp.where(outside[1:], kappa[:-1], x_face))
    centre = kappa[1:-1]
    y_face = harmonic(centre[:, 1:], centre[:, :-1])
    y_face = jnp.concatenate([centre[:, :1], y_face, centre[:, -1:]], axis=1)
    z_face = harmonic(centre[:, :, 1:], centre[:, :, :-1])
    z_face = jnp.concatenate([centre[:, :, :1], z_face, centre[:, :, -1:]], axis=2)
    denom = (
        x_face[:-1]
        + x_face[1:]
        + y_face[:, :-1]
        + y_face[:, 1:]
        + z_face[:, :, :-1]
        + z_face[:, :, 1:]
    )
    scale = jnp.where(outside[1:-1], 0.0, 1.0 / denom)
    z_face = jnp.pad(z_face, ((0, 0), (0, 0), (0, 7)))
    mass = kappa[depth : depth + planes] * (1.0 / 16.0)
    return [jnp.swapaxes(item, 1, 2) for item in (x_face, y_face, z_face, scale, mass)]


def relax_kernel(
    own,
    low,
    high,
    x_col,
    y_col,
    z_col,
    scale_col,
    mass_col,
    y_vals,
    z_vals,
    face_ids,
    snap,
    gram,
    state,
    x_face,
    y_face,
    z_face,
    scale,
    ghost,
    both,
):
    planes, rows_y, rows_z, width = own.shape
    length = state.shape[0]
    inner = pl.ds(8, rows_z)

    def fill(src, base):
        def body(p, carry):
            for y in range(rows_y):
                state[base + p, y, inner] = src[p, y].astype(jnp.float32)
            return carry

        lax.fori_loop(0, planes, body, 0)

    fill(low, 0)
    fill(own, planes)
    fill(high, 2 * planes)
    ids = face_ids[...]
    picks = [(ids == side).astype(jnp.float32) for side in range(4)]
    ghost[0] = y_vals[...].astype(jnp.float32) * picks[0]
    ghost[1] = y_vals[...].astype(jnp.float32) * picks[1]
    z_low = z_vals[...].astype(jnp.float32) * picks[2]
    z_high = z_vals[...].astype(jnp.float32) * picks[3]

    def edges(p, carry):
        for y in range(rows_y):
            state[p, y, pl.ds(7, 1)] = z_low[y : y + 1]
            state[p, y, pl.ds(8 + rows_z, 1)] = z_high[y : y + 1]
        return carry

    lax.fori_loop(0, length, edges, 0)

    def spread(dst, src):
        def body(p, carry):
            columns = src[p]
            for y in range(dst.shape[1]):
                dst[p, y] = jnp.broadcast_to(columns[:, y : y + 1], (columns.shape[0], width))
            return carry

        lax.fori_loop(0, dst.shape[0], body, 0)

    spread(x_face, x_col)
    spread(y_face, y_col)
    spread(z_face, z_col)
    spread(scale, scale_col)

    for sweep in range(1, SWEEPS + 1):

        def body(e, carry, sweep=sweep):
            slot = e - sweep + 1
            for y in range(rows_y):
                below = ghost[0] if y == 0 else state[slot, y - 1, inner]
                above = ghost[1] if y == rows_y - 1 else state[slot, y + 1, inner]
                numer = (
                    x_face[e - 1, y] * state[slot - 1, y, inner]
                    + x_face[e, y] * state[slot + 1, y, inner]
                    + y_face[e - 1, y] * below
                    + y_face[e - 1, y + 1] * above
                    + z_face[e - 1, y, pl.ds(0, rows_z)] * state[slot, y, pl.ds(7, rows_z)]
                    + z_face[e - 1, y, pl.ds(1, rows_z)] * state[slot, y, pl.ds(9, rows_z)]
                )
                fresh = (numer * scale[e - 1, y]).astype(jnp.bfloat16)
                state[slot - 1, y, inner] = fresh.astype(jnp.float32)
            return carry

        lax.fori_loop(sweep, length - sweep, body, 0)

    for p in range(planes):
        e = planes + p
        slot = e - SWEEPS
        mass = mass_col[p]
        for y in range(rows_y):
            state[slot, y, pl.ds(7, 1)] = jnp.zeros((1, width), jnp.float32)
            state[slot, y, pl.ds(8 + rows_z, 1)] = jnp.zeros((1, width), jnp.float32)
        for y in range(rows_y):
            rows = pl.ds(y * rows_z, rows_z)
            middle = state[slot, y, inner]
            faces = [
                x_face[e - 1, y],
                x_face[e, y],
                y_face[e - 1, y],
                y_face[e - 1, y + 1],
                z_face[e - 1, y, pl.ds(0, rows_z)],
                z_face[e - 1, y, pl.ds(1, rows_z)],
            ]
            numer = faces[0] * state[slot - 1, y, inner] + faces[1] * state[slot + 1, y, inner]
            if y > 0:
                numer = numer + faces[2] * state[slot, y - 1, inner]
            if y < rows_y - 1:
                numer = numer + faces[3] * state[slot, y + 1, inner]
            numer = (
                numer
                + faces[4] * state[slot, y, pl.ds(7, rows_z)]
                + faces[5] * state[slot, y, pl.ds(9, rows_z)]
            )
            denom = faces[0] + faces[1] + faces[2] + faces[3] + faces[4] + faces[5]
            snap[p, rows] = middle.astype(jnp.bfloat16)
            both[rows, pl.ds(0, width)] = (
                middle * jnp.broadcast_to(mass[:, y : y + 1], (rows_z, width))
            ).astype(jnp.bfloat16)
            both[rows, pl.ds(width, width)] = (denom * middle - numer).astype(jnp.bfloat16)
        part = lax.dot_general(
            snap[p], both[...], (((0,), (0,)), ((), ())), preferred_element_type=jnp.float32
        )
        for item in range(2):
            piece = part[:, item * width : (item + 1) * width]
            gram[item] = piece if p == 0 else gram[item] + piece


def shift_planes(array, up):
    count = lax.axis_size("sub")
    pairs = [(i, i + 1) for i in range(count - 1)]
    if not up:
        pairs = [(j, i) for i, j in pairs]
    return lax.ppermute(array, "sub", pairs)


def relax(initial, classes, y_vals, z_vals, face_ids):
    planes, rows_y, rows_z, width = initial.shape
    index = lax.axis_index("sub")
    subs = lax.axis_size("sub")
    packed = classes.astype(jnp.bfloat16)
    class_low = shift_planes(packed, True)
    class_high = shift_planes(packed, False)
    low = shift_planes(initial, True)
    high = shift_planes(initial, False)
    extended = jnp.concatenate([class_low, packed, class_high], axis=0)
    columns = coefficients(extended, planes, index == 0, index == subs - 1)
    length = 3 * planes
    scratch = [
        (length, rows_y, rows_z + 16),
        (length - 1, rows_y, rows_z),
        (length - 2, rows_y + 1, rows_z),
        (length - 2, rows_y, rows_z + 8),
        (length - 2, rows_y, rows_z),
        (2, rows_z),
    ]
    return pl.pallas_call(
        relax_kernel,
        out_shape=[
            jax.ShapeDtypeStruct((planes, rows_y * rows_z, width), jnp.bfloat16),
            jax.ShapeDtypeStruct((2, width, width), jnp.float32),
        ],
        scratch_shapes=[pltpu.VMEM(shape + (width,), jnp.float32) for shape in scratch]
        + [pltpu.VMEM((rows_y * rows_z, 2 * width), jnp.bfloat16)],
        compiler_params=pltpu.CompilerParams(vmem_limit_bytes=60 * 2**20),
    )(initial, low, high, *columns, y_vals, z_vals, face_ids[None])


def lane_copy(tile, lane):
    return jnp.broadcast_to(tile[:, lane : lane + 1], (8, 128))


def row_copy(tile, row):
    return jnp.broadcast_to(tile[row : row + 1, :], (8, tile.shape[1]))


def solve_spd(left, right):
    size = left.shape[0]
    count = size // 8
    sub = lax.broadcasted_iota(jnp.int32, (8, 128), 0)
    lhs = [left[8 * t : 8 * t + 8] for t in range(count)]
    rhs = [right[8 * t : 8 * t + 8] for t in range(count)]
    for k in range(count):
        cols = [lane_copy(lhs[k], 8 * k + j) for j in range(8)]
        panel_l, panel_r = lhs[k], rhs[k]
        for j in range(8):
            recip = 1.0 / row_copy(cols[j], j)
            here = sub == j
            mult = jnp.where(here, recip, -cols[j] * recip)
            for l in range(j + 1, 8):
                cols[l] = jnp.where(here, 0.0, cols[l]) + mult * row_copy(cols[l], j)
            panel_l = jnp.where(here, 0.0, panel_l) + mult * row_copy(panel_l, j)
            panel_r = jnp.where(here, 0.0, panel_r) + mult * row_copy(panel_r, j)
        rows_l = [row_copy(panel_l, j) for j in range(8)]
        rows_r = [row_copy(panel_r, j) for j in range(8)]
        order = list(range(k + 1, count)) + list(range(k))
        for t in order:
            tile_cols = [lane_copy(lhs[t], 8 * k + j) for j in range(8)]
            if k + 1 < count:
                lhs[t] = lhs[t] - tree([tile_cols[j] * rows_l[j] for j in range(8)])
            rhs[t] = rhs[t] - tree([tile_cols[j] * rows_r[j] for j in range(8)])
        lhs[k], rhs[k] = panel_l, panel_r
    return jnp.concatenate(rhs, axis=0)


def tree(terms):
    while len(terms) > 1:
        terms = [a + b for a, b in zip(terms[::2], terms[1::2])] + terms[len(terms) & ~1 :]
    return terms[0]


def whiten(inner, block):
    size = inner.shape[0]
    count = size // 8
    sub = lax.broadcasted_iota(jnp.int32, (8, 128), 0)
    lhs = [inner[8 * t : 8 * t + 8] for t in range(count)]
    rhs = [block[8 * t : 8 * t + 8] for t in range(count)]
    done = []
    for k in range(count):
        live = range(k, count)
        cols = {t: [lane_copy(lhs[t], 8 * k + j) for j in range(8)] for t in live}
        scale = None
        for j in range(8):
            pivot = row_copy(cols[k][j], j)
            recip = 1.0 / pivot
            root = lax.rsqrt(pivot)
            scale = root if scale is None else jnp.where(sub >= j, root, scale)
            head = {l: row_copy(cols[k][l], j) for l in range(j + 1, 8)}
            row_l, row_r = row_copy(lhs[k], j), row_copy(rhs[k], j)
            for t in live:
                mult = cols[t][j] * recip
                if t == k:
                    mult = jnp.where(sub > j, mult, 0.0)
                for l in range(j + 1, 8):
                    cols[t][l] = cols[t][l] - mult * head[l]
                lhs[t] = lhs[t] - mult[:, : row_l.shape[1]] * row_l
                rhs[t] = rhs[t] - mult * row_r
        done.append(rhs[k] * scale)
    return jnp.concatenate(done, axis=0)


def dot(a, b, dims):
    return lax.dot_general(
        a, b, (dims, ((), ())), precision=lax.Precision.HIGHEST, preferred_element_type=jnp.float32
    )


def modes_kernel(cell_count, *refs):
    *part_refs, start_ref, snap_ref, out_ref = refs
    mass = part_refs[0][0]
    stiff = part_refs[0][1]
    for part in part_refs[1:]:
        mass = mass + part[0]
        stiff = stiff + part[1]
    mass = mass * (1.0 / cell_count)
    stiff = (stiff + stiff.T) * (0.5 / cell_count)
    step = solve_spd(stiff, mass)
    form = dot(step, dot(mass, step, ((1,), (0,))), ((0,), (0,)))
    block = start_ref[...]
    for _ in range(ITERS):
        weighted = dot(block, form, ((1,), (0,)))
        solved = dot(block, step, ((1,), (1,)))
        inner = dot(weighted, block, ((1,), (1,)))
        block = whiten(inner, solved)
    modes = block.astype(jnp.bfloat16)
    for piece in range(out_ref.shape[0]):
        out_ref[piece] = lax.dot_general(
            modes, snap_ref[piece], (((1,), (1,)), ((), ())), preferred_element_type=jnp.float32
        ).astype(jnp.bfloat16)


def on_device(snap_init, channel_map, yface_vals, zface_vals, face_of, start_block, correlation):
    subs = lax.axis_size("sub")
    snapshots, own = relax(
        snap_init[0], channel_map[0], yface_vals[0], zface_vals[0], face_of[0]
    )
    parts = [own] + [
        lax.ppermute(own, "sub", [(i, (i + shift) % subs) for i in range(subs)])
        for shift in range(1, subs)
    ]
    cell_count = float(subs * snapshots.shape[0] * snapshots.shape[1])
    owner_count = lax.axis_size("nbhd")
    width = snapshots.shape[-1]
    piece_cells = snapshots.size // width // owner_count
    blocks = snapshots.reshape(owner_count, piece_cells, width)
    modes = start_block.shape[-1]
    pieces = pl.pallas_call(
        functools.partial(modes_kernel, cell_count),
        out_shape=jax.ShapeDtypeStruct((owner_count, modes, piece_cells), jnp.bfloat16),
        compiler_params=pltpu.CompilerParams(vmem_limit_bytes=32 * 2**20),
    )(*parts, start_block[0].T, blocks)
    received = lax.all_to_all(pieces, "nbhd", split_axis=0, concat_axis=0, tiled=True)
    column = lax.dynamic_slice_in_dim(correlation, lax.axis_index("nbhd"), 1, axis=1)[:, 0]
    result = received * column.astype(jnp.bfloat16)[:, None, None]
    return result[None, None]


def solution(mesh):
    return jax.shard_map(
        on_device,
        mesh=mesh,
        in_specs=(
            P("nbhd", "sub", None, None, None),
            P("nbhd", "sub", None, None),
            P("nbhd", None, None),
            P("nbhd", None, None),
            P("nbhd", None),
            P("nbhd", None, None),
            P(),
        ),
        out_specs=P("nbhd", "sub", None, None, None),
        check_vma=False,
    )
```

```python
import functools

import jax
import jax.numpy as jnp
from jax import lax
from jax.experimental import pallas as pl
from jax.experimental.pallas import tpu as pltpu
from jax.sharding import PartitionSpec as P

SWEEPS = 3
ITERS = 4


def harmonic(left_k, right_k):
    return 2.0 * left_k * right_k / (left_k + right_k)


def coefficients(classes, planes, first, last, lanes):
    kappa = jnp.exp2(2.0 * classes.astype(jnp.float32))
    length, rows_y, rows_z = kappa.shape
    depth = (length - planes) // 2
    place = jnp.arange(length, dtype=jnp.int32)[:, None, None]
    outside = (first & (place < depth)) | (last & (place >= depth + planes))
    x_face = harmonic(kappa[1:], kappa[:-1])
    x_face = jnp.where(outside[:-1], kappa[1:], jnp.where(outside[1:], kappa[:-1], x_face))
    centre = kappa[1:-1]
    y_face = harmonic(centre[:, 1:], centre[:, :-1])
    y_face = jnp.concatenate([centre[:, :1], y_face, centre[:, -1:]], axis=1)
    z_face = harmonic(centre[:, :, 1:], centre[:, :, :-1])
    z_face = jnp.concatenate([centre[:, :, :1], z_face, centre[:, :, -1:]], axis=2)
    faces = [
        x_face[:-1],
        x_face[1:],
        y_face[:, :-1],
        y_face[:, 1:],
        z_face[:, :, :-1],
        z_face[:, :, 1:],
    ]
    denom = faces[0] + faces[1] + faces[2] + faces[3] + faces[4] + faces[5]
    scale = jnp.where(outside[1:-1], 0.0, 1.0 / denom)
    empty = jnp.zeros_like(denom)
    sweep = jnp.stack([face * scale for face in faces] + [empty, empty], axis=2)
    sweep = jnp.pad(sweep, ((1, 1), (0, 0), (0, 0), (0, lanes - rows_z)))
    own = slice(depth - 1, depth - 1 + planes)
    plane = jnp.arange(planes, dtype=jnp.int32)[:, None, None]
    row_y = jnp.arange(rows_y, dtype=jnp.int32)[None, :, None]
    row_z = jnp.arange(rows_z, dtype=jnp.int32)[None, None, :]
    upper_half = row_y >= rows_y // 2
    counted = [
        jnp.where(plane > 0, 1.0, jnp.where(first | ~upper_half, 0.0, 2.0)),
        jnp.where(plane < planes - 1, 1.0, jnp.where(last | upper_half, 0.0, 2.0)),
        jnp.where(row_y > 0, 1.0, 0.0),
        jnp.where(row_y < rows_y - 1, 1.0, 0.0),
        jnp.where(row_z > 0, 1.0, 0.0),
        jnp.where(row_z < rows_z - 1, 1.0, 0.0),
    ]
    rows = [face[own] * share for face, share in zip(faces, counted)]
    rows += [denom[own], kappa[depth : depth + planes] * (1.0 / 16.0)]
    stiff = jnp.pad(jnp.stack(rows, axis=2), ((0, 0), (0, 0), (0, 0), (0, lanes - rows_z)))
    return sweep, stiff


def relax_kernel(
    own,
    low,
    high,
    sweep_rows,
    stiff_rows,
    y_vals,
    z_vals,
    face_ids,
    snap,
    gram,
    state_a,
    state_b,
    pad_rows,
    both,
):
    planes, rows_y, rows_z, width = own.shape
    length = state_a.shape[0]
    lanes = state_a.shape[3]
    half = rows_y // 2
    bf16 = jnp.bfloat16
    row = lax.broadcasted_iota(jnp.int32, (width, width), 0)
    col = lax.broadcasted_iota(jnp.int32, (width, width), 1)
    eye = jnp.where(row == col, 1.0, 0.0).astype(bf16)
    valid = lax.broadcasted_iota(jnp.int32, (width, lanes), 1) < rows_z

    def turn(lines):
        return lax.dot_general(
            eye, lines, (((1,), (1,)), ((), ())), preferred_element_type=jnp.float32
        )

    ids = face_ids[...]
    picks = [(ids == side).astype(jnp.float32) for side in range(4)]
    spare = lanes - rows_z
    place = lax.broadcasted_iota(jnp.int32, (spare, width), 0)
    z_all = z_vals[...].astype(jnp.float32)
    z_low = z_all * picks[2]
    z_high = z_all * picks[3]
    for y in range(rows_y):
        rows = jnp.where(place == 0, z_high[y : y + 1], 0.0)
        pad_rows[y] = jnp.where(place == spare - 1, z_low[y : y + 1], rows).astype(bf16)
    y_all = y_vals[...].astype(jnp.float32)
    blank = jnp.zeros((spare, width), bf16)
    ghost_low = turn(jnp.concatenate([(y_all * picks[0]).astype(bf16), blank], axis=0))
    ghost_high = turn(jnp.concatenate([(y_all * picks[1]).astype(bf16), blank], axis=0))

    def edges(e, carry):
        for state in (state_a, state_b):
            state[e, 0] = ghost_low
            state[e, rows_y + 1] = ghost_high
        return carry

    lax.fori_loop(0, length, edges, 0)

    def fill(get, e, y_from, y_to):
        for y in range(y_from, y_to, 2):
            lines = turn(
                jnp.concatenate([get(y), pad_rows[y], get(y + 1), pad_rows[y + 1]], axis=0)
            )
            state_a[e, y + 1] = lines[:, :lanes]
            state_a[e, y + 2] = lines[:, lanes:]

    def fill_planes(i, carry):
        fill(lambda y: own[i, y], planes + i, 0, rows_y)
        return carry

    def fill_sides(i, carry):
        fill(lambda y: low[half + i * rows_y + y], 1 + i, 0, rows_y)
        fill(lambda y: high[i * rows_y + y], 2 * planes + i, 0, rows_y)
        return carry

    lax.fori_loop(0, planes, fill_planes, 0)
    lax.fori_loop(0, planes - 1, fill_sides, 0)
    fill(lambda y: low[y - half], 0, half, rows_y)
    fill(lambda y: high[(planes - 1) * rows_y + y], length - 1, 0, half)

    def relax_line(src, dst, e, y, keep):
        middle = src[e, y + 1]
        rows = sweep_rows[e, y]
        fresh = (
            rows[0:1] * src[e - 1, y + 1]
            + rows[1:2] * src[e + 1, y + 1]
            + rows[2:3] * src[e, y]
            + rows[3:4] * src[e, y + 2]
            + rows[4:5] * pltpu.roll(middle, 1, 1)
            + rows[5:6] * pltpu.roll(middle, lanes - 1, 1)
        )
        fresh = fresh.astype(bf16).astype(jnp.float32)
        dst[e, y + 1] = jnp.where(valid, fresh, middle) if keep else fresh

    group = 4

    def relax_rows(src, dst, e, y_from, y_to, keep):
        def body(i, carry):
            for j in range(group):
                relax_line(src, dst, e, y_from + i * group + j, keep)
            return carry

        lax.fori_loop(0, (y_to - y_from) // group, body, 0)

    buffers = (state_a, state_b)
    for sweep in range(1, SWEEPS + 1):
        src, dst = buffers[(sweep - 1) % 2], buffers[sweep % 2]
        keep = sweep < SWEEPS

        def body(e, carry, src=src, dst=dst, keep=keep):
            relax_rows(src, dst, e, 0, rows_y, keep)
            return carry

        first = planes - SWEEPS - 1 + sweep
        lax.fori_loop(first + 1, length - 1 - first, body, 0)
        relax_rows(src, dst, first, half, rows_y, keep)
        relax_rows(src, dst, length - 1 - first, 0, half, keep)
    final = buffers[SWEEPS % 2]

    def stiffness(p, total):
        e = planes + p

        def body(y, carry):
            middle = final[e, y + 1]
            rows = stiff_rows[p, y]
            numer = (
                rows[0:1] * final[e - 1, y + 1]
                + rows[1:2] * final[e + 1, y + 1]
                + rows[2:3] * final[e, y]
                + rows[3:4] * final[e, y + 2]
                + rows[4:5] * pltpu.roll(middle, 1, 1)
                + rows[5:6] * pltpu.roll(middle, lanes - 1, 1)
            )
            spot = pl.ds(y * lanes, lanes)
            snap[p, :, spot] = middle.astype(bf16)
            both[pl.ds(0, width), spot] = (rows[7:8] * middle).astype(bf16)
            both[pl.ds(width, width), spot] = (rows[6:7] * middle - numer).astype(bf16)
            return carry

        for y in range(rows_y):
            body(y, 0)
        return total + lax.dot_general(
            snap[p], both[...], (((1,), (1,)), ((), ())), preferred_element_type=jnp.float32
        )

    total = lax.fori_loop(0, planes, stiffness, jnp.zeros((width, 2 * width), jnp.float32))
    mass = total[:, :width]
    stiff = total[:, width:]
    stiff = stiff + stiff.T
    gram[pl.ds(0, width)] = jnp.where(row > col, stiff, mass)
    diagonal = jnp.sum(jnp.where(row == col, stiff, 0.0), axis=0, keepdims=True)
    gram[pl.ds(width, 8)] = jnp.broadcast_to(diagonal, (8, width))


def shift_planes(array, up):
    count = lax.axis_size("sub")
    pairs = [(i, i + 1) for i in range(count - 1)]
    if not up:
        pairs = [(j, i) for i, j in pairs]
    return lax.ppermute(array, "sub", pairs)


def relax(initial, classes, y_vals, z_vals, face_ids):
    planes, rows_y, rows_z, width = initial.shape
    lanes = 128
    index = lax.axis_index("sub")
    subs = lax.axis_size("sub")
    packed = classes.astype(jnp.bfloat16)
    lines = initial.reshape(planes * rows_y, rows_z, width)
    half = rows_y // 2
    low = shift_planes(lines[half:], True)
    high = shift_planes(lines[:-half], False)
    class_low = shift_planes(packed, True)
    class_high = shift_planes(packed, False)
    extended = jnp.concatenate([class_low, packed, class_high], axis=0)
    sweep_rows, stiff_rows = coefficients(extended, planes, index == 0, index == subs - 1, lanes)
    state = pltpu.VMEM((3 * planes, rows_y + 2, width, lanes), jnp.float32)
    return pl.pallas_call(
        relax_kernel,
        out_shape=[
            jax.ShapeDtypeStruct((planes, width, rows_y * lanes), jnp.bfloat16),
            jax.ShapeDtypeStruct((width + 8, width), jnp.float32),
        ],
        scratch_shapes=[
            state,
            state,
            pltpu.VMEM((rows_y, lanes - rows_z, width), jnp.bfloat16),
            pltpu.VMEM((2 * width, rows_y * lanes), jnp.bfloat16),
        ],
        compiler_params=pltpu.CompilerParams(vmem_limit_bytes=56 * 2**20),
    )(initial, low, high, sweep_rows, stiff_rows, y_vals, z_vals, face_ids[None])


def lane_copy(tile, lane):
    return jnp.broadcast_to(tile[:, lane : lane + 1], (8, 128))


def row_copy(tile, row):
    return jnp.broadcast_to(tile[row : row + 1, :], (8, tile.shape[1]))


def solve_spd(left, right):
    size = left.shape[0]
    count = size // 8
    sub = lax.broadcasted_iota(jnp.int32, (8, 128), 0)
    lhs = [left[8 * t : 8 * t + 8] for t in range(count)]
    rhs = [right[8 * t : 8 * t + 8] for t in range(count)]
    for k in range(count):
        cols = [lane_copy(lhs[k], 8 * k + j) for j in range(8)]
        panel_l, panel_r = lhs[k], rhs[k]
        for j in range(8):
            recip = 1.0 / row_copy(cols[j], j)
            here = sub == j
            mult = jnp.where(here, recip, -cols[j] * recip)
            for l in range(j + 1, 8):
                cols[l] = jnp.where(here, 0.0, cols[l]) + mult * row_copy(cols[l], j)
            panel_l = jnp.where(here, 0.0, panel_l) + mult * row_copy(panel_l, j)
            panel_r = jnp.where(here, 0.0, panel_r) + mult * row_copy(panel_r, j)
        rows_l = [row_copy(panel_l, j) for j in range(8)]
        rows_r = [row_copy(panel_r, j) for j in range(8)]
        order = list(range(k + 1, count)) + list(range(k))
        for t in order:
            tile_cols = [lane_copy(lhs[t], 8 * k + j) for j in range(8)]
            if k + 1 < count:
                lhs[t] = lhs[t] - tree([tile_cols[j] * rows_l[j] for j in range(8)])
            rhs[t] = rhs[t] - tree([tile_cols[j] * rows_r[j] for j in range(8)])
        lhs[k], rhs[k] = panel_l, panel_r
    return jnp.concatenate(rhs, axis=0)


def tree(terms):
    while len(terms) > 1:
        terms = [a + b for a, b in zip(terms[::2], terms[1::2])] + terms[len(terms) & ~1 :]
    return terms[0]


def whiten(inner, block):
    size = inner.shape[0]
    count = size // 8
    sub = lax.broadcasted_iota(jnp.int32, (8, 128), 0)
    lhs = [inner[8 * t : 8 * t + 8] for t in range(count)]
    rhs = [block[8 * t : 8 * t + 8] for t in range(count)]
    done = []
    for k in range(count):
        live = range(k, count)
        cols = {t: [lane_copy(lhs[t], 8 * k + j) for j in range(8)] for t in live}
        scale = None
        for j in range(8):
            pivot = row_copy(cols[k][j], j)
            recip = 1.0 / pivot
            root = lax.rsqrt(pivot)
            scale = root if scale is None else jnp.where(sub >= j, root, scale)
            head = {l: row_copy(cols[k][l], j) for l in range(j + 1, 8)}
            row_l, row_r = row_copy(lhs[k], j), row_copy(rhs[k], j)
            for t in live:
                mult = cols[t][j] * recip
                if t == k:
                    mult = jnp.where(sub > j, mult, 0.0)
                for l in range(j + 1, 8):
                    cols[t][l] = cols[t][l] - mult * head[l]
                lhs[t] = lhs[t] - mult[:, : row_l.shape[1]] * row_l
                rhs[t] = rhs[t] - mult * row_r
        done.append(rhs[k] * scale)
    return jnp.concatenate(done, axis=0)


def dot(a, b, dims):
    return lax.dot_general(
        a, b, (dims, ((), ())), precision=lax.Precision.HIGHEST, preferred_element_type=jnp.float32
    )


def modes_kernel(cell_count, rows_z, *refs):
    *part_refs, start_ref, snap_ref, out_ref = refs
    total = part_refs[0][...]
    for part in part_refs[1:]:
        total = total + part[...]
    width = total.shape[1]
    row = lax.broadcasted_iota(jnp.int32, (width, width), 0)
    col = lax.broadcasted_iota(jnp.int32, (width, width), 1)
    packed = total[:width]
    turned = packed.T
    mass = jnp.where(row <= col, packed, turned) * (1.0 / cell_count)
    stiff = jnp.where(row > col, packed, jnp.where(row < col, turned, total[width : width + 1]))
    stiff = stiff * (0.5 / cell_count)
    step = solve_spd(stiff, mass)
    form = dot(step, dot(mass, step, ((1,), (0,))), ((0,), (0,)))
    block = start_ref[...]
    for _ in range(ITERS):
        weighted = dot(block, form, ((1,), (0,)))
        solved = dot(block, step, ((1,), (1,)))
        inner = dot(weighted, block, ((1,), (1,)))
        block = whiten(inner, solved)
    modes = block.astype(jnp.bfloat16)
    planes, _, columns = snap_ref.shape
    lanes = 128
    rows_y = columns // lanes
    piece_rows = planes * rows_y // out_ref.shape[0]
    for p in range(planes):
        basis = jnp.dot(modes, snap_ref[p], preferred_element_type=jnp.float32)
        for y in range(rows_y):
            piece, spot = divmod(p * rows_y + y, piece_rows)
            out_ref[piece, :, pl.ds(spot * rows_z, rows_z)] = basis[
                :, y * lanes : y * lanes + rows_z
            ].astype(jnp.bfloat16)


def on_device(snap_init, channel_map, yface_vals, zface_vals, face_of, start_block, correlation):
    subs = lax.axis_size("sub")
    owner_count = lax.axis_size("nbhd")
    planes, rows_y, rows_z, width = snap_init.shape[1:]
    snapshots, own = relax(
        snap_init[0], channel_map[0], yface_vals[0], zface_vals[0], face_of[0]
    )
    parts = [own] + [
        lax.ppermute(own, "sub", [(i, (i + shift) % subs) for i in range(subs)])
        for shift in range(1, subs)
    ]
    cells = planes * rows_y * rows_z
    modes = start_block.shape[-1]
    pieces = pl.pallas_call(
        functools.partial(modes_kernel, float(subs * cells), rows_z),
        out_shape=jax.ShapeDtypeStruct((owner_count, modes, cells // owner_count), jnp.bfloat16),
        compiler_params=pltpu.CompilerParams(vmem_limit_bytes=32 * 2**20),
    )(*parts, start_block[0].T, snapshots)
    received = lax.all_to_all(pieces, "nbhd", split_axis=0, concat_axis=0, tiled=True)
    column = lax.dynamic_slice_in_dim(correlation, lax.axis_index("nbhd"), 1, axis=1)[:, 0]
    result = received * column.astype(jnp.bfloat16)[:, None, None]
    return result[None, None]


def solution(mesh):
    return jax.shard_map(
        on_device,
        mesh=mesh,
        in_specs=(
            P("nbhd", "sub", None, None, None),
            P("nbhd", "sub", None, None),
            P("nbhd", None, None),
            P("nbhd", None, None),
            P("nbhd", None),
            P("nbhd", None, None),
            P(),
        ),
        out_specs=P("nbhd", "sub", None, None, None),
        check_vma=False,
    )
```

```python
import functools

import jax
import jax.numpy as jnp
from jax import lax
from jax.experimental import pallas as pl
from jax.experimental.pallas import tpu as pltpu
from jax.sharding import PartitionSpec as P

SWEEPS = 3
ITERS = 4


def harmonic(left_k, right_k):
    return 2.0 * left_k * right_k / (left_k + right_k)


def coefficients(classes, planes, first, last, lanes):
    kappa = jnp.exp2(2.0 * classes.astype(jnp.float32))
    length, rows_y, rows_z = kappa.shape
    depth = (length - planes) // 2
    place = jnp.arange(length, dtype=jnp.int32)[:, None, None]
    outside = (first & (place < depth)) | (last & (place >= depth + planes))
    x_face = harmonic(kappa[1:], kappa[:-1])
    x_face = jnp.where(outside[:-1], kappa[1:], jnp.where(outside[1:], kappa[:-1], x_face))
    centre = kappa[1:-1]
    y_face = harmonic(centre[:, 1:], centre[:, :-1])
    y_face = jnp.concatenate([centre[:, :1], y_face, centre[:, -1:]], axis=1)
    z_face = harmonic(centre[:, :, 1:], centre[:, :, :-1])
    z_face = jnp.concatenate([centre[:, :, :1], z_face, centre[:, :, -1:]], axis=2)
    faces = [
        x_face[:-1],
        x_face[1:],
        y_face[:, :-1],
        y_face[:, 1:],
        z_face[:, :, :-1],
        z_face[:, :, 1:],
    ]
    denom = faces[0] + faces[1] + faces[2] + faces[3] + faces[4] + faces[5]
    scale = jnp.where(outside[1:-1], 0.0, 1.0 / denom)
    empty = jnp.zeros_like(denom)
    sweep = jnp.stack([face * scale for face in faces] + [empty, empty], axis=2)
    sweep = jnp.pad(sweep, ((1, 1), (0, 0), (0, 0), (0, lanes - rows_z)))
    own = slice(depth - 1, depth - 1 + planes)
    plane = jnp.arange(planes, dtype=jnp.int32)[:, None, None]
    row_y = jnp.arange(rows_y, dtype=jnp.int32)[None, :, None]
    row_z = jnp.arange(rows_z, dtype=jnp.int32)[None, None, :]
    upper_half = row_y >= rows_y // 2
    counted = [
        jnp.where(plane > 0, 1.0, jnp.where(first | ~upper_half, 0.0, 2.0)),
        jnp.where(plane < planes - 1, 1.0, jnp.where(last | upper_half, 0.0, 2.0)),
        jnp.where(row_y > 0, 1.0, 0.0),
        jnp.where(row_y < rows_y - 1, 1.0, 0.0),
        jnp.where(row_z > 0, 1.0, 0.0),
        jnp.where(row_z < rows_z - 1, 1.0, 0.0),
    ]
    rows = [face[own] * share for face, share in zip(faces, counted)]
    rows += [denom[own], kappa[depth : depth + planes] * (1.0 / 16.0)]
    stiff = jnp.pad(jnp.stack(rows, axis=2), ((0, 0), (0, 0), (0, 0), (0, lanes - rows_z)))
    return sweep, stiff


def relax_kernel(
    own,
    low,
    high,
    sweep_rows,
    stiff_rows,
    y_vals,
    z_vals,
    face_ids,
    snap,
    gram,
    state_a,
    state_b,
    pad_rows,
    both,
):
    planes, rows_y, rows_z, width = own.shape
    length = state_a.shape[0]
    lanes = state_a.shape[3]
    half = rows_y // 2
    spare_lines = low.shape[0] - planes * rows_y + half
    bf16 = jnp.bfloat16
    row = lax.broadcasted_iota(jnp.int32, (width, width), 0)
    col = lax.broadcasted_iota(jnp.int32, (width, width), 1)
    eye = jnp.where(row == col, 1.0, 0.0).astype(bf16)
    part = 16
    valid = lax.broadcasted_iota(jnp.int32, (part, lanes), 1) < rows_z

    def turn(lines):
        return lax.dot_general(
            eye, lines, (((1,), (1,)), ((), ())), preferred_element_type=jnp.float32
        )

    ids = face_ids[...]
    picks = [(ids == side).astype(jnp.float32) for side in range(4)]
    spare = lanes - rows_z
    place = lax.broadcasted_iota(jnp.int32, (spare, width), 0)
    z_all = z_vals[...].astype(jnp.float32)
    z_low = z_all * picks[2]
    z_high = z_all * picks[3]
    for y in range(rows_y):
        rows = jnp.where(place == 0, z_high[y : y + 1], 0.0)
        pad_rows[y] = jnp.where(place == spare - 1, z_low[y : y + 1], rows).astype(bf16)
    y_all = y_vals[...].astype(jnp.float32)
    blank = jnp.zeros((spare, width), bf16)
    ghost_low = turn(jnp.concatenate([(y_all * picks[0]).astype(bf16), blank], axis=0))
    ghost_high = turn(jnp.concatenate([(y_all * picks[1]).astype(bf16), blank], axis=0))

    def edges(e, carry):
        for state in (state_a, state_b):
            state[e, 0] = ghost_low
            state[e, rows_y + 1] = ghost_high
        return carry

    lax.fori_loop(0, length, edges, 0)

    def fill(get, e, y_from, y_to):
        for y in range(y_from, y_to, 2):
            lines = turn(
                jnp.concatenate([get(y), pad_rows[y], get(y + 1), pad_rows[y + 1]], axis=0)
            )
            state_a[e, y + 1] = lines[:, :lanes]
            state_a[e, y + 2] = lines[:, lanes:]

    def fill_planes(i, carry):
        fill(lambda y: own[i, y], planes + i, 0, rows_y)
        return carry

    def fill_sides(i, carry):
        fill(lambda y: low[spare_lines + half + i * rows_y + y], 1 + i, 0, rows_y)
        fill(lambda y: high[spare_lines + i * rows_y + y], 2 * planes + i, 0, rows_y)
        return carry

    lax.fori_loop(0, planes, fill_planes, 0)
    lax.fori_loop(0, planes - 1, fill_sides, 0)
    fill(lambda y: low[spare_lines + y - half], 0, half, rows_y)
    fill(lambda y: high[spare_lines + (planes - 1) * rows_y + y], length - 1, 0, half)

    def relax_line(src, dst, e, y, keep):
        rows = sweep_rows[e, y]
        weights = [jnp.broadcast_to(rows[k : k + 1], (part, lanes)) for k in range(6)]
        for start in range(0, width, part):
            some = pl.ds(start, part)
            middle = src[e, y + 1, some]
            fresh = (
                weights[0] * src[e - 1, y + 1, some]
                + weights[1] * src[e + 1, y + 1, some]
                + weights[2] * src[e, y, some]
                + weights[3] * src[e, y + 2, some]
                + weights[4] * pltpu.roll(middle, 1, 1)
                + weights[5] * pltpu.roll(middle, lanes - 1, 1)
            )
            fresh = fresh.astype(bf16).astype(jnp.float32)
            dst[e, y + 1, some] = jnp.where(valid, fresh, middle) if keep else fresh

    group = 2

    def relax_rows(src, dst, e, y_from, y_to, keep):
        def body(i, carry):
            for j in range(group):
                relax_line(src, dst, e, y_from + i * group + j, keep)
            return carry

        lax.fori_loop(0, (y_to - y_from) // group, body, 0)

    buffers = (state_a, state_b)
    for sweep in range(1, SWEEPS + 1):
        src, dst = buffers[(sweep - 1) % 2], buffers[sweep % 2]
        keep = sweep < SWEEPS

        def body(e, carry, src=src, dst=dst, keep=keep):
            relax_rows(src, dst, e, 0, rows_y, keep)
            return carry

        first = planes - SWEEPS - 1 + sweep
        lax.fori_loop(first + 1, length - 1 - first, body, 0)
        relax_rows(src, dst, first, half, rows_y, keep)
        relax_rows(src, dst, length - 1 - first, 0, half, keep)
    final = buffers[SWEEPS % 2]

    def stiffness(p, total):
        e = planes + p

        def line(y):
            rows = stiff_rows[p, y]
            weights = [jnp.broadcast_to(rows[k : k + 1], (part, lanes)) for k in range(8)]
            spot = pl.ds(y * lanes, lanes)
            for start in range(0, width, part):
                some = pl.ds(start, part)
                middle = final[e, y + 1, some]
                numer = (
                    weights[0] * final[e - 1, y + 1, some]
                    + weights[1] * final[e + 1, y + 1, some]
                    + weights[2] * final[e, y, some]
                    + weights[3] * final[e, y + 2, some]
                    + weights[4] * pltpu.roll(middle, 1, 1)
                    + weights[5] * pltpu.roll(middle, lanes - 1, 1)
                )
                snap[p, some, spot] = middle.astype(bf16)
                both[some, spot] = (weights[7] * middle).astype(bf16)
                both[pl.ds(width + start, part), spot] = (weights[6] * middle - numer).astype(bf16)

        for y in range(rows_y):
            line(y)
        return total + lax.dot_general(
            snap[p], both[...], (((1,), (1,)), ((), ())), preferred_element_type=jnp.float32
        )

    total = lax.fori_loop(0, planes, stiffness, jnp.zeros((width, 2 * width), jnp.float32))
    mass = total[:, :width]
    stiff = total[:, width:]
    stiff = stiff + stiff.T
    gram[pl.ds(0, width)] = jnp.where(row > col, stiff, mass)
    diagonal = jnp.sum(jnp.where(row == col, stiff, 0.0), axis=0, keepdims=True)
    gram[pl.ds(width, 8)] = jnp.broadcast_to(diagonal, (8, width))


def shift_planes(array, up):
    count = lax.axis_size("sub")
    pairs = [(i, i + 1) for i in range(count - 1)]
    if not up:
        pairs = [(j, i) for i, j in pairs]
    return lax.ppermute(array, "sub", pairs)


def relax(initial, classes, y_vals, z_vals, face_ids):
    planes, rows_y, rows_z, width = initial.shape
    lanes = 128
    index = lax.axis_index("sub")
    subs = lax.axis_size("sub")
    lines = initial.reshape(planes * rows_y, rows_z, width)
    count = planes * rows_y
    half = rows_y // 2
    marks = classes.astype(jnp.bfloat16).reshape(count, rows_z).T
    marks = jnp.pad(marks, ((0, 0), (0, -count % width)))
    marks = jnp.swapaxes(marks.reshape(rows_z, -1, width), 0, 1)
    low = shift_planes(jnp.concatenate([marks, lines[half:]], axis=0), True)
    high = shift_planes(jnp.concatenate([marks, lines[:-half]], axis=0), False)
    spare = marks.shape[0]

    def unmark(halo):
        flat = jnp.swapaxes(halo[:spare], 0, 1).reshape(rows_z, spare * width)
        return flat[:, :count].T.reshape(planes, rows_y, rows_z).astype(jnp.int32)

    extended = jnp.concatenate([unmark(low), classes, unmark(high)], axis=0)
    sweep_rows, stiff_rows = coefficients(extended, planes, index == 0, index == subs - 1, lanes)
    state = pltpu.VMEM((3 * planes, rows_y + 2, width, lanes), jnp.float32)
    return pl.pallas_call(
        relax_kernel,
        out_shape=[
            jax.ShapeDtypeStruct((planes, width, rows_y * lanes), jnp.bfloat16),
            jax.ShapeDtypeStruct((width + 8, width), jnp.float32),
        ],
        scratch_shapes=[
            state,
            state,
            pltpu.VMEM((rows_y, lanes - rows_z, width), jnp.bfloat16),
            pltpu.VMEM((2 * width, rows_y * lanes), jnp.bfloat16),
        ],
        compiler_params=pltpu.CompilerParams(vmem_limit_bytes=56 * 2**20),
    )(initial, low, high, sweep_rows, stiff_rows, y_vals, z_vals, face_ids[None])


def lane_copy(tile, lane):
    return jnp.broadcast_to(tile[:, lane : lane + 1], (8, 128))


def row_copy(tile, row):
    return jnp.broadcast_to(tile[row : row + 1, :], (8, tile.shape[1]))


def solve_spd(left, right):
    size = left.shape[0]
    count = size // 8
    sub = lax.broadcasted_iota(jnp.int32, (8, 128), 0)
    lhs = [left[8 * t : 8 * t + 8] for t in range(count)]
    rhs = [right[8 * t : 8 * t + 8] for t in range(count)]
    for k in range(count):
        cols = [lane_copy(lhs[k], 8 * k + j) for j in range(8)]
        panel_l, panel_r = lhs[k], rhs[k]
        for j in range(8):
            recip = 1.0 / row_copy(cols[j], j)
            here = sub == j
            mult = jnp.where(here, recip, -cols[j] * recip)
            for l in range(j + 1, 8):
                cols[l] = jnp.where(here, 0.0, cols[l]) + mult * row_copy(cols[l], j)
            panel_l = jnp.where(here, 0.0, panel_l) + mult * row_copy(panel_l, j)
            panel_r = jnp.where(here, 0.0, panel_r) + mult * row_copy(panel_r, j)
        rows_l = [row_copy(panel_l, j) for j in range(8)]
        rows_r = [row_copy(panel_r, j) for j in range(8)]
        order = list(range(k + 1, count)) + list(range(k))
        for t in order:
            tile_cols = [lane_copy(lhs[t], 8 * k + j) for j in range(8)]
            if k + 1 < count:
                lhs[t] = lhs[t] - tree([tile_cols[j] * rows_l[j] for j in range(8)])
            rhs[t] = rhs[t] - tree([tile_cols[j] * rows_r[j] for j in range(8)])
        lhs[k], rhs[k] = panel_l, panel_r
    return jnp.concatenate(rhs, axis=0)


def tree(terms):
    while len(terms) > 1:
        terms = [a + b for a, b in zip(terms[::2], terms[1::2])] + terms[len(terms) & ~1 :]
    return terms[0]


def whiten(inner, block):
    size = inner.shape[0]
    count = size // 8
    sub = lax.broadcasted_iota(jnp.int32, (8, 128), 0)
    lhs = [inner[8 * t : 8 * t + 8] for t in range(count)]
    rhs = [block[8 * t : 8 * t + 8] for t in range(count)]
    done = []
    for k in range(count):
        live = range(k, count)
        cols = {t: [lane_copy(lhs[t], 8 * k + j) for j in range(8)] for t in live}
        scale = None
        for j in range(8):
            pivot = row_copy(cols[k][j], j)
            recip = 1.0 / pivot
            root = lax.rsqrt(pivot)
            scale = root if scale is None else jnp.where(sub >= j, root, scale)
            head = {l: row_copy(cols[k][l], j) for l in range(j + 1, 8)}
            row_l, row_r = row_copy(lhs[k], j), row_copy(rhs[k], j)
            for t in live:
                mult = cols[t][j] * recip
                if t == k:
                    mult = jnp.where(sub > j, mult, 0.0)
                for l in range(j + 1, 8):
                    cols[t][l] = cols[t][l] - mult * head[l]
                lhs[t] = lhs[t] - mult[:, : row_l.shape[1]] * row_l
                rhs[t] = rhs[t] - mult * row_r
        done.append(rhs[k] * scale)
    return jnp.concatenate(done, axis=0)


def dot(a, b, dims):
    return lax.dot_general(
        a, b, (dims, ((), ())), precision=lax.Precision.HIGHEST, preferred_element_type=jnp.float32
    )


def modes_kernel(cell_count, rows_z, *refs):
    *part_refs, start_ref, snap_hbm, out_ref, snap_ref, sem = refs
    fetch = pltpu.make_async_copy(snap_hbm, snap_ref, sem)
    fetch.start()
    total = part_refs[0][...]
    for part in part_refs[1:]:
        total = total + part[...]
    width = total.shape[1]
    row = lax.broadcasted_iota(jnp.int32, (width, width), 0)
    col = lax.broadcasted_iota(jnp.int32, (width, width), 1)
    packed = total[:width]
    turned = packed.T
    mass = jnp.where(row <= col, packed, turned) * (1.0 / cell_count)
    stiff = jnp.where(row > col, packed, jnp.where(row < col, turned, total[width : width + 1]))
    stiff = stiff * (0.5 / cell_count)
    step = solve_spd(stiff, mass)
    form = dot(step, dot(mass, step, ((1,), (0,))), ((0,), (0,)))
    block = start_ref[...]
    for _ in range(ITERS):
        weighted = dot(block, form, ((1,), (0,)))
        solved = dot(block, step, ((1,), (1,)))
        inner = dot(weighted, block, ((1,), (1,)))
        block = whiten(inner, solved)
    modes = block.astype(jnp.bfloat16)
    fetch.wait()
    planes, _, columns = snap_ref.shape
    lanes = 128
    rows_y = columns // lanes
    piece_rows = planes * rows_y // out_ref.shape[0]
    for p in range(planes):
        basis = jnp.dot(modes, snap_ref[p], preferred_element_type=jnp.float32)
        for y in range(rows_y):
            piece, spot = divmod(p * rows_y + y, piece_rows)
            out_ref[piece, :, pl.ds(spot * rows_z, rows_z)] = basis[
                :, y * lanes : y * lanes + rows_z
            ].astype(jnp.bfloat16)


def on_device(snap_init, channel_map, yface_vals, zface_vals, face_of, start_block, correlation):
    subs = lax.axis_size("sub")
    owner_count = lax.axis_size("nbhd")
    planes, rows_y, rows_z, width = snap_init.shape[1:]
    snapshots, own = relax(
        snap_init[0], channel_map[0], yface_vals[0], zface_vals[0], face_of[0]
    )
    parts = [own] + [
        lax.ppermute(own, "sub", [(i, (i + shift) % subs) for i in range(subs)])
        for shift in range(1, subs)
    ]
    cells = planes * rows_y * rows_z
    modes = start_block.shape[-1]
    pieces = pl.pallas_call(
        functools.partial(modes_kernel, float(subs * cells), rows_z),
        out_shape=jax.ShapeDtypeStruct((owner_count, modes, cells // owner_count), jnp.bfloat16),
        in_specs=[pl.BlockSpec(memory_space=pltpu.VMEM)] * (subs + 1)
        + [pl.BlockSpec(memory_space=pl.ANY)],
        scratch_shapes=[
            pltpu.VMEM(snapshots.shape, snapshots.dtype),
            pltpu.SemaphoreType.DMA,
        ],
        compiler_params=pltpu.CompilerParams(vmem_limit_bytes=56 * 2**20),
    )(*parts, start_block[0].T, snapshots)
    received = lax.all_to_all(pieces, "nbhd", split_axis=0, concat_axis=0, tiled=True)
    column = lax.dynamic_slice_in_dim(correlation, lax.axis_index("nbhd"), 1, axis=1)[:, 0]
    result = received * column.astype(jnp.bfloat16)[:, None, None]
    return result[None, None]


def solution(mesh):
    return jax.shard_map(
        on_device,
        mesh=mesh,
        in_specs=(
            P("nbhd", "sub", None, None, None),
            P("nbhd", "sub", None, None),
            P("nbhd", None, None),
            P("nbhd", None, None),
            P("nbhd", None),
            P("nbhd", None, None),
            P(),
        ),
        out_specs=P("nbhd", "sub", None, None, None),
        check_vma=False,
    )
```

```python
import functools

import jax
import jax.numpy as jnp
from jax import lax
from jax.experimental import pallas as pl
from jax.experimental.pallas import tpu as pltpu
from jax.sharding import PartitionSpec as P

SWEEPS = 3
ITERS = 4


def harmonic(left_k, right_k):
    return 2.0 * left_k * right_k / (left_k + right_k)


LANES = 128


def weight_rows(kappa_ref, weights, stiff_rows, lines, first, last, rows_y, rows_z):
    total = kappa_ref.shape[0]
    depth = (total - lines) // 2
    kappa = kappa_ref[...]
    shape = kappa.shape
    line = lax.broadcasted_iota(jnp.int32, shape, 0)
    row_z = lax.broadcasted_iota(jnp.int32, shape, 1)
    row_y = lax.rem(line, rows_y)

    def face(other, edge):
        return jnp.where(edge, kappa, harmonic(kappa, other))

    top = depth + lines
    faces = [
        face(pltpu.roll(kappa, rows_y, 0), (line >= depth) & (line < depth + rows_y * first)),
        face(pltpu.roll(kappa, total - rows_y, 0), (line >= top - rows_y * last) & (line < top)),
        face(pltpu.roll(kappa, 1, 0), row_y == 0),
        face(pltpu.roll(kappa, total - 1, 0), row_y == rows_y - 1),
        face(pltpu.roll(kappa, 1, 1), row_z == 0),
        face(pltpu.roll(kappa, LANES - 1, 1), row_z == rows_z - 1),
    ]
    denom = faces[0] + faces[1] + faces[2] + faces[3] + faces[4] + faces[5]
    outside = (line < depth * first) | (line >= total - depth * last) | (row_z >= rows_z)
    scale = jnp.where(outside, 0.0, 1.0 / denom)
    for k in range(6):
        weights[k] = faces[k] * scale
    upper = row_y >= rows_y // 2
    low_edge = line < depth + rows_y
    high_edge = line >= top - rows_y
    low_cross = jnp.where(upper, 2.0 - 2.0 * first.astype(jnp.float32), 0.0)
    high_cross = jnp.where(upper, 0.0, 2.0 - 2.0 * last.astype(jnp.float32))
    shares = [
        jnp.where(low_edge, low_cross, 1.0),
        jnp.where(high_edge, high_cross, 1.0),
        jnp.where(row_y == 0, 0.0, 1.0),
        jnp.where(row_y == rows_y - 1, 0.0, 1.0),
        jnp.where(row_z == 0, 0.0, 1.0),
        jnp.where(row_z == rows_z - 1, 0.0, 1.0),
    ]
    rows = [item * share for item, share in zip(faces, shares)] + [denom, kappa * (1.0 / 16.0)]
    inside = (row_z < rows_z)[depth:top]
    for k in range(8):
        stiff_rows[k] = jnp.where(inside, rows[k][depth:top], 0.0)


def turned(lines):
    width = lines.shape[1]
    row = lax.broadcasted_iota(jnp.int32, (width, width), 0)
    col = lax.broadcasted_iota(jnp.int32, (width, width), 1)
    eye = jnp.where(row == col, 1.0, 0.0).astype(jnp.bfloat16)
    return lax.dot_general(eye, lines, (((1,), (1,)), ((), ())), preferred_element_type=jnp.float32)


def place(line, rows_y):
    return lax.div(line, rows_y), lax.rem(line, rows_y)


def fill(state, source, skip, count, first_line, pad_rows):
    rows_y = pad_rows.shape[0]
    group = 4

    def body(i, carry):
        done = []
        for j in range(0, group, 2):
            at = i * group + j
            e, y = place(first_line + at, rows_y)
            lines = [source[skip + at], pad_rows[y], source[skip + at + 1], pad_rows[y + 1]]
            done.append((e, y, turned(jnp.concatenate(lines, axis=0))))
        for e, y, both in done:
            state[e, y + 1] = both[:, :LANES]
            state[e, y + 2] = both[:, LANES:]
        return carry

    lax.fori_loop(0, count // group, body, 0)


def neighbour_sum(src, e, y, rows, some, middle):
    return (
        rows[0] * src[e - 1, y + 1, some]
        + rows[1] * src[e + 1, y + 1, some]
        + rows[2] * src[e, y, some]
        + rows[3] * src[e, y + 2, some]
        + rows[4] * pltpu.roll(middle, 1, 1)
        + rows[5] * pltpu.roll(middle, LANES - 1, 1)
    )


PART = 64


def relax_lines(src, dst, weights, first_line, count, rows_y, rows_z, keep):
    width = src.shape[2]
    group = 4
    valid = lax.broadcasted_iota(jnp.int32, (PART, LANES), 1) < rows_z

    def body(i, carry):
        waiting = []
        for j in range(group):
            line = first_line + i * group + j
            e, y = place(line, rows_y)
            rows = [weights[k, pl.ds(line, 1)] for k in range(6)]
            for start in range(0, width, PART):
                some = pl.ds(start, PART)
                middle = src[e, y + 1, some]
                fresh = neighbour_sum(src, e, y, rows, some, middle)
                fresh = fresh.astype(jnp.bfloat16).astype(jnp.float32)
                if keep:
                    fresh = jnp.where(valid, fresh, middle)
                waiting.append((e, y, some, fresh))
                if len(waiting) > 1:
                    e0, y0, some0, value = waiting.pop(0)
                    dst[e0, y0 + 1, some0] = value
        for e0, y0, some0, value in waiting:
            dst[e0, y0 + 1, some0] = value
        return carry

    lax.fori_loop(0, count // group, body, 0)


def near_kernel(
    flags,
    own,
    near_a,
    near_b,
    classes,
    y_vals,
    z_vals,
    face_ids,
    hand_a,
    hand_b,
    weights,
    stiff_rows,
    pad_rows,
    state_a,
    state_b,
    kappa,
    sems,
):
    lines, rows_z, width = own.shape
    rows_y = pad_rows.shape[0]
    planes = lines // rows_y
    near = lines // 2
    bf16 = jnp.bfloat16
    even, first, last = flags[0], flags[1], flags[2]
    one = jnp.int32(1)

    def powers(marks):
        return jnp.left_shift(one, 2 * marks).astype(jnp.float32)

    base_a = pl.multiple_of(even * (2 * lines), 8)
    base_b = pl.multiple_of((1 - even) * (2 * lines), 8)
    kappa[...] = jnp.ones(kappa.shape, jnp.float32)
    kappa[pl.ds(lines, lines), pl.ds(0, rows_z)] = powers(classes[...])
    kappa[pl.ds(base_a, lines)] = powers(near_a[0][:lines].astype(jnp.float32).astype(jnp.int32))
    kappa[pl.ds(base_b, lines)] = powers(near_b[0][:lines].astype(jnp.float32).astype(jnp.int32))
    weight_rows(kappa, weights, stiff_rows, lines, first, last, rows_y, rows_z)

    ids = face_ids[...]
    picks = [(ids == side).astype(jnp.float32) for side in range(4)]
    spare = LANES - rows_z
    spot = lax.broadcasted_iota(jnp.int32, (spare, width), 0)
    z_all = z_vals[...].astype(jnp.float32)
    z_low = z_all * picks[2]
    z_high = z_all * picks[3]
    for y in range(rows_y):
        rows = jnp.where(spot == 0, z_high[y : y + 1], 0.0)
        pad_rows[y] = jnp.where(spot == spare - 1, z_low[y : y + 1], rows).astype(bf16)
    y_all = y_vals[...].astype(jnp.float32)
    blank = jnp.zeros((spare, width), bf16)
    ghost_low = turned(jnp.concatenate([(y_all * picks[0]).astype(bf16), blank], axis=0))
    ghost_high = turned(jnp.concatenate([(y_all * picks[1]).astype(bf16), blank], axis=0))
    for e in range(planes - 2, 2 * planes + 2):
        for state in (state_a, state_b):
            state[e, 0] = ghost_low
            state[e, rows_y + 1] = ghost_high

    fill(state_a, own, 0, lines, lines, pad_rows)
    fill(state_a, near_a, 1, near, near + even * (lines + near), pad_rows)
    fill(state_a, near_b, 1, near, near + (1 - even) * (lines + near), pad_rows)

    sent = []

    def send(state, hand, e, count, offset):
        copy = pltpu.make_async_copy(
            state.at[pl.ds(e, count)], hand.at[pl.ds(e - offset, count)], sems.at[len(sent)]
        )
        copy.start()
        sent.append(copy)

    step = functools.partial(relax_lines, weights=weights, rows_y=rows_y, rows_z=rows_z)
    send(state_a, hand_a, planes - 2, 2, planes - 2)
    send(state_a, hand_a, 2 * planes, 2, planes - 2)
    step(state_a, state_b, first_line=lines - rows_y, count=lines + 2 * rows_y, keep=True)
    send(state_b, hand_b, planes - 1, 2, planes - 1)
    send(state_b, hand_b, 2 * planes - 1, 2, planes - 1)
    step(state_b, state_a, first_line=lines, count=lines, keep=True)
    send(state_a, hand_a, planes, planes, planes - 2)
    step(state_a, state_b, first_line=lines + rows_y, count=lines - 2 * rows_y, keep=False)
    send(state_b, hand_b, planes + 1, planes - 2, planes - 1)
    for copy in sent:
        copy.wait()


def far_kernel(
    flags,
    far_a,
    far_b,
    weights,
    stiff_rows,
    pad_rows,
    hand_a,
    hand_b,
    snap,
    gram,
    state_a,
    state_b,
    both,
    sems,
):
    planes, width, _ = snap.shape
    rows_y = pad_rows.shape[0]
    rows_z = far_a.shape[1]
    lines = planes * rows_y
    half = rows_y // 2
    even = flags[0]
    bf16 = jnp.bfloat16
    taken = []

    def take(dst, src):
        copy = pltpu.make_async_copy(src, dst, sems.at[len(taken)])
        copy.start()
        taken.append(copy)

    top = rows_y + 1
    a_off, b_off = planes - 2, planes - 1
    take(state_a.at[pl.ds(a_off, 2)], hand_a.at[pl.ds(0, 2)])
    take(state_a.at[pl.ds(2 * planes, 2)], hand_a.at[pl.ds(2 * planes - a_off, 2)])
    take(state_a.at[1, top], hand_a.at[0, top])
    take(state_a.at[3 * planes - 2, 0], hand_a.at[0, 0])
    take(state_b.at[pl.ds(b_off, 2)], hand_b.at[pl.ds(0, 2)])
    take(state_b.at[pl.ds(2 * planes - 1, 2)], hand_b.at[pl.ds(2 * planes - 1 - b_off, 2)])
    take(state_b.at[2, top], hand_b.at[0, top])
    take(state_b.at[3 * planes - 3, 0], hand_b.at[0, 0])
    take(state_a.at[pl.ds(planes, planes)], hand_a.at[pl.ds(planes - a_off, planes)])
    take(state_b.at[pl.ds(planes + 1, planes - 2)], hand_b.at[pl.ds(planes + 1 - b_off, planes - 2)])

    far = far_a.shape[0]
    low_line = half
    high_line = 3 * lines - half - far
    fill(state_a, far_a, 0, far, low_line + even * (high_line - low_line), pad_rows)
    fill(state_a, far_b, 0, far, high_line - even * (high_line - low_line), pad_rows)

    waits = {1: range(0, 4), 2: range(4, 8), 3: range(8, 9)}
    buffers = (state_a, state_b)
    for sweep in range(1, SWEEPS + 1):
        for k in waits[sweep]:
            taken[k].wait()
        src, dst = buffers[(sweep - 1) % 2], buffers[sweep % 2]
        for first_line in (half + sweep * rows_y, 3 * lines - half - far - sweep * rows_y):
            relax_lines(src, dst, weights, first_line, far, rows_y, rows_z, sweep < SWEEPS)
    taken[9].wait()
    final = buffers[SWEEPS % 2]

    def stiffness(p, total):
        e = planes + p
        waiting = []

        def store(y, some, below, values):
            spot = pl.ds(y * LANES, LANES)
            snap[p, some, spot] = values[0]
            both[some, spot] = values[1]
            both[below, spot] = values[2]

        for y in range(rows_y):
            rows = [stiff_rows[k, pl.ds(p * rows_y + y, 1)] for k in range(8)]
            for start in range(0, width, PART):
                some = pl.ds(start, PART)
                middle = final[e, y + 1, some]
                numer = neighbour_sum(final, e, y, rows, some, middle)
                values = [middle, rows[7] * middle, rows[6] * middle - numer]
                values = [value.astype(bf16) for value in values]
                waiting.append((y, some, pl.ds(width + start, PART), values))
                if len(waiting) > 1:
                    store(*waiting.pop(0))
        for item in waiting:
            store(*item)
        return total + lax.dot_general(
            snap[p], both[...], (((1,), (1,)), ((), ())), preferred_element_type=jnp.float32
        )

    total = lax.fori_loop(0, planes, stiffness, jnp.zeros((width, 2 * width), jnp.float32))
    mass = total[:, :width]
    stiff = total[:, width:]
    stiff = stiff + stiff.T
    row = lax.broadcasted_iota(jnp.int32, (width, width), 0)
    col = lax.broadcasted_iota(jnp.int32, (width, width), 1)
    gram[pl.ds(0, width)] = jnp.where(row > col, stiff, mass)
    diagonal = jnp.sum(jnp.where(row == col, stiff, 0.0), axis=0, keepdims=True)
    gram[pl.ds(width, 8)] = jnp.broadcast_to(diagonal, (8, width))


def swap(array, start):
    count = lax.axis_size("sub")
    pairs = [(i, i + 1) for i in range(start, count - 1, 2)]
    return lax.ppermute(array, "sub", pairs + [(j, i) for i, j in pairs])


def relax(initial, classes, y_vals, z_vals, face_ids):
    planes, rows_y, rows_z, width = initial.shape
    index = lax.axis_index("sub")
    subs = lax.axis_size("sub")
    even = (index + 1) % 2
    flags = jnp.stack([even, index == 0, index == subs - 1, 0]).astype(jnp.int32)
    lines = initial.reshape(planes * rows_y, rows_z, width)
    count = planes * rows_y
    near, far, half = 2 * rows_y, 2 * rows_y - rows_y // 2, rows_y // 2
    marks = classes.astype(jnp.bfloat16).reshape(1, count, rows_z)
    marks = jnp.pad(marks, ((0, 0), (0, rows_z - count), (0, width - rows_z)))

    def near_part(upward):
        part = lax.dynamic_slice_in_dim(lines, upward * (count - near), near, axis=0)
        return jnp.concatenate([marks, part], axis=0)

    def far_part(upward):
        start = upward * half + (1 - upward) * near
        return lax.dynamic_slice_in_dim(lines, start, far, axis=0)

    near_a = swap(near_part(even), 0)
    near_b = swap(near_part(1 - even), 1)
    far_a = swap(far_part(even), 0)
    far_b = swap(far_part(1 - even), 1)

    vmem = pl.BlockSpec(memory_space=pltpu.VMEM)
    smem = pl.BlockSpec(memory_space=pltpu.SMEM)
    hbm = pl.BlockSpec(memory_space=pltpu.HBM)
    state = pltpu.VMEM((3 * planes, rows_y + 2, width, LANES), jnp.float32)
    params = pltpu.CompilerParams(vmem_limit_bytes=48 * 2**20)
    hand_a, hand_b, weights, stiff_rows, pad_rows = pl.pallas_call(
        near_kernel,
        out_shape=[
            jax.ShapeDtypeStruct((planes + 4, rows_y + 2, width, LANES), jnp.float32),
            jax.ShapeDtypeStruct((planes + 2, rows_y + 2, width, LANES), jnp.float32),
            jax.ShapeDtypeStruct((6, 3 * count, LANES), jnp.float32),
            jax.ShapeDtypeStruct((8, count, LANES), jnp.float32),
            jax.ShapeDtypeStruct((rows_y, LANES - rows_z, width), jnp.bfloat16),
        ],
        in_specs=[smem] + [vmem] * 7,
        out_specs=[hbm, hbm, vmem, vmem, vmem],
        scratch_shapes=[
            state,
            state,
            pltpu.VMEM((3 * count, LANES), jnp.float32),
            pltpu.SemaphoreType.DMA((6,)),
        ],
        compiler_params=params,
    )(
        flags,
        lines,
        near_a,
        near_b,
        classes.reshape(count, rows_z),
        y_vals,
        z_vals,
        face_ids[None],
    )
    return pl.pallas_call(
        far_kernel,
        out_shape=[
            jax.ShapeDtypeStruct((planes, width, rows_y * LANES), jnp.bfloat16),
            jax.ShapeDtypeStruct((width + 8, width), jnp.float32),
        ],
        in_specs=[smem] + [vmem] * 5 + [hbm] * 2,
        out_specs=[vmem, vmem],
        scratch_shapes=[
            state,
            state,
            pltpu.VMEM((2 * width, rows_y * LANES), jnp.bfloat16),
            pltpu.SemaphoreType.DMA((10,)),
        ],
        compiler_params=params,
    )(flags, far_a, far_b, weights, stiff_rows, pad_rows, hand_a, hand_b)


def lane_copy(tile, lane):
    return jnp.broadcast_to(tile[:, lane : lane + 1], (8, 128))


def row_copy(tile, row):
    return jnp.broadcast_to(tile[row : row + 1, :], (8, tile.shape[1]))


def solve_spd(left, right):
    size = left.shape[0]
    count = size // 8
    sub = lax.broadcasted_iota(jnp.int32, (8, 128), 0)
    lhs = [left[8 * t : 8 * t + 8] for t in range(count)]
    rhs = [right[8 * t : 8 * t + 8] for t in range(count)]
    for k in range(count):
        cols = [lane_copy(lhs[k], 8 * k + j) for j in range(8)]
        panel_l, panel_r = lhs[k], rhs[k]
        for j in range(8):
            recip = 1.0 / row_copy(cols[j], j)
            here = sub == j
            mult = jnp.where(here, recip, -cols[j] * recip)
            for l in range(j + 1, 8):
                cols[l] = jnp.where(here, 0.0, cols[l]) + mult * row_copy(cols[l], j)
            panel_l = jnp.where(here, 0.0, panel_l) + mult * row_copy(panel_l, j)
            panel_r = jnp.where(here, 0.0, panel_r) + mult * row_copy(panel_r, j)
        rows_l = [row_copy(panel_l, j) for j in range(8)]
        rows_r = [row_copy(panel_r, j) for j in range(8)]
        order = list(range(k + 1, count)) + list(range(k))
        for t in order:
            tile_cols = [lane_copy(lhs[t], 8 * k + j) for j in range(8)]
            if k + 1 < count:
                lhs[t] = lhs[t] - tree([tile_cols[j] * rows_l[j] for j in range(8)])
            rhs[t] = rhs[t] - tree([tile_cols[j] * rows_r[j] for j in range(8)])
        lhs[k], rhs[k] = panel_l, panel_r
    return jnp.concatenate(rhs, axis=0)


def tree(terms):
    while len(terms) > 1:
        terms = [a + b for a, b in zip(terms[::2], terms[1::2])] + terms[len(terms) & ~1 :]
    return terms[0]


def whiten(inner, block):
    size = inner.shape[0]
    count = size // 8
    sub = lax.broadcasted_iota(jnp.int32, (8, 128), 0)
    lhs = [inner[8 * t : 8 * t + 8] for t in range(count)]
    rhs = [block[8 * t : 8 * t + 8] for t in range(count)]
    done = []
    for k in range(count):
        live = range(k, count)
        cols = {t: [lane_copy(lhs[t], 8 * k + j) for j in range(8)] for t in live}
        scale = None
        for j in range(8):
            pivot = row_copy(cols[k][j], j)
            recip = 1.0 / pivot
            root = lax.rsqrt(pivot)
            scale = root if scale is None else jnp.where(sub >= j, root, scale)
            head = {l: row_copy(cols[k][l], j) for l in range(j + 1, 8)}
            row_l, row_r = row_copy(lhs[k], j), row_copy(rhs[k], j)
            for t in live:
                mult = cols[t][j] * recip
                if t == k:
                    mult = jnp.where(sub > j, mult, 0.0)
                for l in range(j + 1, 8):
                    cols[t][l] = cols[t][l] - mult * head[l]
                lhs[t] = lhs[t] - mult[:, : row_l.shape[1]] * row_l
                rhs[t] = rhs[t] - mult * row_r
        done.append(rhs[k] * scale)
    return jnp.concatenate(done, axis=0)


def dot(a, b, dims):
    return lax.dot_general(
        a, b, (dims, ((), ())), precision=lax.Precision.HIGHEST, preferred_element_type=jnp.float32
    )


def modes_kernel(cell_count, rows_z, *refs):
    *part_refs, start_ref, snap_hbm, out_ref, snap_ref, sem = refs
    fetch = pltpu.make_async_copy(snap_hbm, snap_ref, sem)
    fetch.start()
    total = part_refs[0][...]
    for part in part_refs[1:]:
        total = total + part[...]
    width = total.shape[1]
    row = lax.broadcasted_iota(jnp.int32, (width, width), 0)
    col = lax.broadcasted_iota(jnp.int32, (width, width), 1)
    packed = total[:width]
    turned = packed.T
    mass = jnp.where(row <= col, packed, turned) * (1.0 / cell_count)
    stiff = jnp.where(row > col, packed, jnp.where(row < col, turned, total[width : width + 1]))
    stiff = stiff * (0.5 / cell_count)
    step = solve_spd(stiff, mass)
    form = dot(step, dot(mass, step, ((1,), (0,))), ((0,), (0,)))
    block = start_ref[...]
    for _ in range(ITERS):
        weighted = dot(block, form, ((1,), (0,)))
        solved = dot(block, step, ((1,), (1,)))
        inner = dot(weighted, block, ((1,), (1,)))
        block = whiten(inner, solved)
    modes = block.astype(jnp.bfloat16)
    fetch.wait()
    planes, _, columns = snap_ref.shape
    lanes = LANES
    rows_y = columns // lanes
    piece_rows = planes * rows_y // out_ref.shape[0]
    for p in range(planes):
        basis = jnp.dot(modes, snap_ref[p], preferred_element_type=jnp.float32)
        for y in range(rows_y):
            piece, spot = divmod(p * rows_y + y, piece_rows)
            out_ref[piece, :, pl.ds(spot * rows_z, rows_z)] = basis[
                :, y * lanes : y * lanes + rows_z
            ].astype(jnp.bfloat16)


def on_device(snap_init, channel_map, yface_vals, zface_vals, face_of, start_block, correlation):
    subs = lax.axis_size("sub")
    owner_count = lax.axis_size("nbhd")
    planes, rows_y, rows_z, width = snap_init.shape[1:]
    snapshots, own = relax(
        snap_init[0], channel_map[0], yface_vals[0], zface_vals[0], face_of[0]
    )
    parts = [own] + [
        lax.ppermute(own, "sub", [(i, (i + shift) % subs) for i in range(subs)])
        for shift in range(1, subs)
    ]
    cells = planes * rows_y * rows_z
    modes = start_block.shape[-1]
    pieces = pl.pallas_call(
        functools.partial(modes_kernel, float(subs * cells), rows_z),
        out_shape=jax.ShapeDtypeStruct((owner_count, modes, cells // owner_count), jnp.bfloat16),
        in_specs=[pl.BlockSpec(memory_space=pltpu.VMEM)] * (subs + 1)
        + [pl.BlockSpec(memory_space=pltpu.HBM)],
        scratch_shapes=[
            pltpu.VMEM(snapshots.shape, snapshots.dtype),
            pltpu.SemaphoreType.DMA,
        ],
        compiler_params=pltpu.CompilerParams(vmem_limit_bytes=24 * 2**20),
    )(*parts, start_block[0].T, snapshots)
    received = lax.all_to_all(pieces, "nbhd", split_axis=0, concat_axis=0, tiled=True)
    column = lax.dynamic_slice_in_dim(correlation, lax.axis_index("nbhd"), 1, axis=1)[:, 0]
    result = received * column.astype(jnp.bfloat16)[:, None, None]
    return result[None, None]


def solution(mesh):
    return jax.shard_map(
        on_device,
        mesh=mesh,
        in_specs=(
            P("nbhd", "sub", None, None, None),
            P("nbhd", "sub", None, None),
            P("nbhd", None, None),
            P("nbhd", None, None),
            P("nbhd", None),
            P("nbhd", None, None),
            P(),
        ),
        out_specs=P("nbhd", "sub", None, None, None),
        check_vma=False,
    )
```

```python
import functools

import jax
import jax.numpy as jnp
from jax import lax
from jax.experimental import pallas as pl
from jax.experimental.pallas import tpu as pltpu
from jax.sharding import PartitionSpec as P

SWEEPS = 3
ITERS = 4


def harmonic(left_k, right_k):
    return 2.0 * left_k * right_k / (left_k + right_k)


LANES = 128


def weight_rows(kappa_ref, weights, stiff_rows, lines, first, last, rows_y, rows_z):
    total = kappa_ref.shape[0]
    depth = (total - lines) // 2
    kappa = kappa_ref[...]
    shape = kappa.shape
    line = lax.broadcasted_iota(jnp.int32, shape, 0)
    row_z = lax.broadcasted_iota(jnp.int32, shape, 1)
    row_y = lax.rem(line, rows_y)

    def face(other, edge):
        return jnp.where(edge, kappa, harmonic(kappa, other))

    top = depth + lines
    faces = [
        face(pltpu.roll(kappa, rows_y, 0), (line >= depth) & (line < depth + rows_y * first)),
        face(pltpu.roll(kappa, total - rows_y, 0), (line >= top - rows_y * last) & (line < top)),
        face(pltpu.roll(kappa, 1, 0), row_y == 0),
        face(pltpu.roll(kappa, total - 1, 0), row_y == rows_y - 1),
        face(pltpu.roll(kappa, 1, 1), row_z == 0),
        face(pltpu.roll(kappa, LANES - 1, 1), row_z == rows_z - 1),
    ]
    denom = faces[0] + faces[1] + faces[2] + faces[3] + faces[4] + faces[5]
    outside = (line < depth * first) | (line >= total - depth * last) | (row_z >= rows_z)
    scale = jnp.where(outside, 0.0, 1.0 / denom)
    for k in range(6):
        weights[k] = faces[k] * scale
    upper = row_y >= rows_y // 2
    plane = lax.div(line - depth, rows_y)
    planes = lines // rows_y
    low_cross = jnp.where(upper, 2.0 - 2.0 * first.astype(jnp.float32), 0.0)
    high_cross = jnp.where(upper, 0.0, 2.0 - 2.0 * last.astype(jnp.float32))
    shares = [
        jnp.where(plane == 0, low_cross, jnp.where(plane == 1, 0.0, 1.0)),
        jnp.where(plane == planes - 1, high_cross, jnp.where(plane == planes - 2, 0.0, 1.0)),
        jnp.where(row_y == 0, 0.0, 1.0),
        jnp.where(row_y == rows_y - 1, 0.0, 1.0),
        jnp.where(row_z == 0, 0.0, 1.0),
        jnp.where(row_z == rows_z - 1, 0.0, 1.0),
    ]
    shares[0] = jnp.where(plane == planes - 1, 2.0, shares[0])
    shares[1] = jnp.where(plane == 0, 2.0, shares[1])
    rows = [item * share for item, share in zip(faces, shares)] + [denom, kappa * (1.0 / 16.0)]
    inside = (row_z < rows_z)[depth:top]
    for k in range(8):
        stiff_rows[k] = jnp.where(inside, rows[k][depth:top], 0.0)


def turned(lines):
    width = lines.shape[1]
    row = lax.broadcasted_iota(jnp.int32, (width, width), 0)
    col = lax.broadcasted_iota(jnp.int32, (width, width), 1)
    eye = jnp.where(row == col, 1.0, 0.0).astype(jnp.bfloat16)
    return lax.dot_general(eye, lines, (((1,), (1,)), ((), ())), preferred_element_type=jnp.float32)


def place(line, rows_y):
    return lax.div(line, rows_y), lax.rem(line, rows_y)


def fill(state, source, skip, count, first_line, pad_rows):
    rows_y = pad_rows.shape[0]
    group = 16 if count % 16 == 0 else 8

    def body(i, carry):
        waiting = []

        def store(e, y, both):
            state[e, y + 1] = both[:, :LANES]
            state[e, y + 2] = both[:, LANES:]

        for j in range(0, group, 2):
            at = i * group + j
            e, y = place(first_line + at, rows_y)
            lines = [source[skip + at], pad_rows[y], source[skip + at + 1], pad_rows[y + 1]]
            waiting.append((e, y, turned(jnp.concatenate(lines, axis=0))))
            if len(waiting) > 1:
                store(*waiting.pop(0))
        for item in waiting:
            store(*item)
        return carry

    lax.fori_loop(0, count // group, body, 0)


def neighbour_sum(src, e, y, rows, some, middle):
    return (
        rows[0] * src[e - 1, y + 1, some]
        + rows[1] * src[e + 1, y + 1, some]
        + rows[2] * src[e, y, some]
        + rows[3] * src[e, y + 2, some]
        + rows[4] * pltpu.roll(middle, 1, 1)
        + rows[5] * pltpu.roll(middle, LANES - 1, 1)
    )


PART = 64


def relax_lines(src, dst, weights, first_line, count, rows_y, rows_z, keep):
    width = src.shape[2]
    group = 8
    valid = lax.broadcasted_iota(jnp.int32, (PART, LANES), 1) < rows_z

    def body(i, carry):
        waiting = []
        for j in range(group):
            line = first_line + i * group + j
            e, y = place(line, rows_y)
            rows = [weights[k, pl.ds(line, 1)] for k in range(6)]
            for start in range(0, width, PART):
                some = pl.ds(start, PART)
                middle = src[e, y + 1, some]
                fresh = neighbour_sum(src, e, y, rows, some, middle)
                fresh = fresh.astype(jnp.bfloat16).astype(jnp.float32)
                if keep:
                    fresh = jnp.where(valid, fresh, middle)
                waiting.append((e, y, some, fresh))
                if len(waiting) > 1:
                    e0, y0, some0, value = waiting.pop(0)
                    dst[e0, y0 + 1, some0] = value
        for e0, y0, some0, value in waiting:
            dst[e0, y0 + 1, some0] = value
        return carry

    lax.fori_loop(0, count // group, body, 0)


def gram_terms(final, places, planes, stiff_rows, snap, both, total):
    _, width, columns = snap.shape
    rows_y = columns // LANES
    for item, e in enumerate(places):
        p = e - planes
        waiting = []

        def store(y, some, below, values, item=item):
            spot = pl.ds(y * LANES, LANES)
            snap[item, some, spot] = values[0]
            both[some, spot] = values[1]
            both[below, spot] = values[2]

        for y in range(rows_y):
            rows = [stiff_rows[k, pl.ds(p * rows_y + y, 1)] for k in range(8)]
            for start in range(0, width, PART):
                some = pl.ds(start, PART)
                middle = final[e, y + 1, some]
                numer = neighbour_sum(final, e, y, rows, some, middle)
                values = [middle, rows[7] * middle, rows[6] * middle - numer]
                values = [value.astype(jnp.bfloat16) for value in values]
                waiting.append((y, some, pl.ds(width + start, PART), values))
                if len(waiting) > 1:
                    store(*waiting.pop(0))
        for entry in waiting:
            store(*entry)
        total = total + lax.dot_general(
            snap[item], both[...], (((1,), (1,)), ((), ())), preferred_element_type=jnp.float32
        )
    return total


def powers(marks):
    return jnp.left_shift(jnp.int32(1), 2 * marks).astype(jnp.float32)


def own_kernel(
    flags,
    own,
    classes,
    y_vals,
    z_vals,
    face_ids,
    hand,
    inner,
    pad_rows,
    state_a,
    state_b,
    kappa,
    weights,
    stiff_rows,
    sems,
):
    lines, rows_z, width = own.shape
    rows_y = pad_rows.shape[0]
    planes = lines // rows_y
    bf16 = jnp.bfloat16
    ids = face_ids[...]
    picks = [(ids == side).astype(jnp.float32) for side in range(4)]
    spare = LANES - rows_z
    spot = lax.broadcasted_iota(jnp.int32, (spare, width), 0)
    z_all = z_vals[...].astype(jnp.float32)
    z_low = z_all * picks[2]
    z_high = z_all * picks[3]
    for y in range(rows_y):
        rows = jnp.where(spot == 0, z_high[y : y + 1], 0.0)
        pad_rows[y] = jnp.where(spot == spare - 1, z_low[y : y + 1], rows).astype(bf16)
    y_all = y_vals[...].astype(jnp.float32)
    blank = jnp.zeros((spare, width), bf16)
    ghost_low = turned(jnp.concatenate([(y_all * picks[0]).astype(bf16), blank], axis=0))
    ghost_high = turned(jnp.concatenate([(y_all * picks[1]).astype(bf16), blank], axis=0))
    for e in range(planes, 2 * planes):
        for state in (state_a, state_b):
            state[e, 0] = ghost_low
            state[e, rows_y + 1] = ghost_high
    fill(state_a, own, 0, lines, lines, pad_rows)
    sends = [
        pltpu.make_async_copy(state_a.at[pl.ds(planes, planes)], hand, sems.at[0]),
        pltpu.make_async_copy(state_b.at[pl.ds(planes + 1, planes - 2)], inner, sems.at[1]),
    ]
    sends[0].start()
    kappa[...] = jnp.ones(kappa.shape, jnp.float32)
    kappa[pl.ds(lines, lines), pl.ds(0, rows_z)] = powers(classes[...])
    weight_rows(kappa, weights, stiff_rows, lines, flags[1], flags[2], rows_y, rows_z)
    middle = (lines + rows_y, lines - 2 * rows_y)
    relax_lines(state_a, state_b, weights, *middle, rows_y, rows_z, True)
    sends[1].start()
    for copy in sends:
        copy.wait()


def near_kernel(
    flags,
    near_a,
    near_b,
    classes,
    pad_rows,
    hand,
    inner,
    hand_a,
    hand_b,
    weights,
    stiff_rows,
    snap,
    gram,
    state_a,
    state_b,
    kappa,
    both,
    sems,
):
    lines = classes.shape[0]
    rows_z = near_a.shape[1]
    rows_y = pad_rows.shape[0]
    planes = lines // rows_y
    near = lines // 2
    even, first, last = flags[0], flags[1], flags[2]
    taken = [
        pltpu.make_async_copy(hand, state_a.at[pl.ds(planes, planes)], sems.at[0]),
        pltpu.make_async_copy(inner, state_b.at[pl.ds(planes + 1, planes - 2)], sems.at[1]),
    ]
    for copy in taken:
        copy.start()

    base_a = pl.multiple_of(even * (2 * lines), 8)
    base_b = pl.multiple_of((1 - even) * (2 * lines), 8)
    kappa[...] = jnp.ones(kappa.shape, jnp.float32)
    kappa[pl.ds(lines, lines), pl.ds(0, rows_z)] = powers(classes[...])
    kappa[pl.ds(base_a, lines)] = powers(near_a[0][:lines].astype(jnp.float32).astype(jnp.int32))
    kappa[pl.ds(base_b, lines)] = powers(near_b[0][:lines].astype(jnp.float32).astype(jnp.int32))
    weight_rows(kappa, weights, stiff_rows, lines, first, last, rows_y, rows_z)
    fill(state_a, near_a, 1, near, near + even * (lines + near), pad_rows)
    fill(state_a, near_b, 1, near, near + (1 - even) * (lines + near), pad_rows)
    for copy in taken:
        copy.wait()
    ghost_low = state_a[planes, 0]
    ghost_high = state_a[planes, rows_y + 1]
    for e in (planes - 2, planes - 1, 2 * planes, 2 * planes + 1):
        state_a[e, 0] = ghost_low
        state_a[e, rows_y + 1] = ghost_high
    for e in (planes - 1, planes, 2 * planes - 1, 2 * planes):
        state_b[e, 0] = ghost_low
        state_b[e, rows_y + 1] = ghost_high

    sent = []

    def send(state, to, e, count, offset):
        copy = pltpu.make_async_copy(
            state.at[pl.ds(e, count)], to.at[pl.ds(e - offset, count)], sems.at[2 + len(sent)]
        )
        copy.start()
        sent.append(copy)

    step = functools.partial(relax_lines, weights=weights, rows_y=rows_y, rows_z=rows_z)
    send(state_a, hand_a, planes - 2, 2, planes - 2)
    send(state_a, hand_a, 2 * planes, 2, planes - 2)
    step(state_a, state_b, first_line=lines - rows_y, count=2 * rows_y, keep=True)
    step(state_a, state_b, first_line=2 * lines - rows_y, count=2 * rows_y, keep=True)
    send(state_b, hand_b, planes - 1, 2, planes - 1)
    send(state_b, hand_b, 2 * planes - 1, 2, planes - 1)
    step(state_b, state_a, first_line=lines, count=lines, keep=True)
    send(state_a, hand_a, planes, planes, planes - 2)
    step(state_a, state_b, first_line=lines + rows_y, count=lines - 2 * rows_y, keep=False)
    send(state_b, hand_b, planes + 1, planes - 2, planes - 1)
    inside = range(planes + 1, 2 * planes - 1)
    blank = jnp.zeros(gram.shape, jnp.float32)
    gram[...] = gram_terms(state_b, inside, planes, stiff_rows, snap, both, blank)
    for copy in sent:
        copy.wait()


def far_kernel(
    flags,
    far_a,
    far_b,
    weights,
    stiff_rows,
    pad_rows,
    near_gram,
    hand_a,
    hand_b,
    snap,
    gram,
    state_a,
    state_b,
    both,
    sems,
):
    width = snap.shape[1]
    rows_y = pad_rows.shape[0]
    rows_z = far_a.shape[1]
    lines = stiff_rows.shape[1]
    planes = lines // rows_y
    half = rows_y // 2
    even = flags[0]
    taken = []

    def take(dst, src):
        copy = pltpu.make_async_copy(src, dst, sems.at[len(taken)])
        copy.start()
        taken.append(copy)

    top = rows_y + 1
    a_off, b_off = planes - 2, planes - 1
    take(state_a.at[pl.ds(a_off, 2)], hand_a.at[pl.ds(0, 2)])
    take(state_a.at[pl.ds(2 * planes, 2)], hand_a.at[pl.ds(2 * planes - a_off, 2)])
    take(state_a.at[1, top], hand_a.at[0, top])
    take(state_a.at[3 * planes - 2, 0], hand_a.at[0, 0])
    take(state_b.at[pl.ds(b_off, 2)], hand_b.at[pl.ds(0, 2)])
    take(state_b.at[pl.ds(2 * planes - 1, 2)], hand_b.at[pl.ds(2 * planes - 1 - b_off, 2)])
    take(state_b.at[2, top], hand_b.at[0, top])
    take(state_b.at[3 * planes - 3, 0], hand_b.at[0, 0])
    take(state_a.at[pl.ds(planes, planes)], hand_a.at[pl.ds(planes - a_off, planes)])
    take(state_b.at[pl.ds(planes + 1, planes - 2)], hand_b.at[pl.ds(planes + 1 - b_off, planes - 2)])

    far = far_a.shape[0]
    low_line = half
    high_line = 3 * lines - half - far
    fill(state_a, far_a, 0, far, low_line + even * (high_line - low_line), pad_rows)
    fill(state_a, far_b, 0, far, high_line - even * (high_line - low_line), pad_rows)

    waits = {1: range(0, 4), 2: range(4, 8), 3: range(8, 9)}
    buffers = (state_a, state_b)
    for sweep in range(1, SWEEPS + 1):
        for k in waits[sweep]:
            taken[k].wait()
        src, dst = buffers[(sweep - 1) % 2], buffers[sweep % 2]
        for first_line in (half + sweep * rows_y, 3 * lines - half - far - sweep * rows_y):
            relax_lines(src, dst, weights, first_line, far, rows_y, rows_z, sweep < SWEEPS)
    taken[9].wait()
    final = buffers[SWEEPS % 2]

    outer = (planes, 2 * planes - 1)
    total = gram_terms(final, outer, planes, stiff_rows, snap, both, near_gram[...])
    mass = total[:, :width]
    stiff = total[:, width:]
    stiff = stiff + stiff.T
    row = lax.broadcasted_iota(jnp.int32, (width, width), 0)
    col = lax.broadcasted_iota(jnp.int32, (width, width), 1)
    gram[pl.ds(0, width)] = jnp.where(row > col, stiff, mass)
    diagonal = jnp.sum(jnp.where(row == col, stiff, 0.0), axis=0, keepdims=True)
    gram[pl.ds(width, 8)] = jnp.broadcast_to(diagonal, (8, width))


def swap(array, start):
    count = lax.axis_size("sub")
    pairs = [(i, i + 1) for i in range(start, count - 1, 2)]
    return lax.ppermute(array, "sub", pairs + [(j, i) for i, j in pairs])


def relax(initial, classes, y_vals, z_vals, face_ids):
    planes, rows_y, rows_z, width = initial.shape
    index = lax.axis_index("sub")
    subs = lax.axis_size("sub")
    even = (index + 1) % 2
    flags = jnp.stack([even, index == 0, index == subs - 1, 0]).astype(jnp.int32)
    lines = initial.reshape(planes * rows_y, rows_z, width)
    count = planes * rows_y
    near, far, half = 2 * rows_y, 2 * rows_y - rows_y // 2, rows_y // 2
    marks = classes.astype(jnp.bfloat16).reshape(1, count, rows_z)
    marks = jnp.pad(marks, ((0, 0), (0, rows_z - count), (0, width - rows_z)))

    def near_part(upward):
        part = lax.dynamic_slice_in_dim(lines, upward * (count - near), near, axis=0)
        return jnp.concatenate([marks, part], axis=0)

    def far_part(upward):
        start = upward * half + (1 - upward) * near
        return lax.dynamic_slice_in_dim(lines, start, far, axis=0)

    near_a = swap(near_part(even), 0)
    near_b = swap(near_part(1 - even), 1)
    far_a = swap(far_part(even), 0)
    far_b = swap(far_part(1 - even), 1)

    vmem = pl.BlockSpec(memory_space=pltpu.VMEM)
    smem = pl.BlockSpec(memory_space=pltpu.SMEM)
    hbm = pl.BlockSpec(memory_space=pltpu.HBM)
    state = pltpu.VMEM((3 * planes, rows_y + 2, width, LANES), jnp.float32)
    params = pltpu.CompilerParams(vmem_limit_bytes=48 * 2**20)
    kappa = pltpu.VMEM((3 * count, LANES), jnp.float32)
    both = pltpu.VMEM((2 * width, rows_y * LANES), jnp.bfloat16)

    def slab(depth):
        return jax.ShapeDtypeStruct((depth, rows_y + 2, width, LANES), jnp.float32)

    def sems(number):
        return pltpu.SemaphoreType.DMA((number,))

    def kept(depth):
        return jax.ShapeDtypeStruct((depth, width, rows_y * LANES), jnp.bfloat16)

    rows = [
        jax.ShapeDtypeStruct((6, 3 * count, LANES), jnp.float32),
        jax.ShapeDtypeStruct((8, count, LANES), jnp.float32),
    ]
    flat_classes = classes.reshape(count, rows_z)
    hand, inner, pad_rows = pl.pallas_call(
        own_kernel,
        out_shape=[
            slab(planes),
            slab(planes - 2),
            jax.ShapeDtypeStruct((rows_y, LANES - rows_z, width), jnp.bfloat16),
        ],
        in_specs=[smem] + [vmem] * 5,
        out_specs=[hbm, hbm, vmem],
        scratch_shapes=[state, state, kappa]
        + [pltpu.VMEM(item.shape, item.dtype) for item in rows]
        + [sems(2)],
        compiler_params=params,
    )(flags, lines, flat_classes, y_vals, z_vals, face_ids[None])
    hand_a, hand_b, weights, stiff_rows, snap_near, gram_near = pl.pallas_call(
        near_kernel,
        out_shape=[
            slab(planes + 4),
            slab(planes + 2),
            *rows,
            kept(planes - 2),
            jax.ShapeDtypeStruct((width, 2 * width), jnp.float32),
        ],
        in_specs=[smem] + [vmem] * 4 + [hbm] * 2,
        out_specs=[hbm, hbm] + [vmem] * 4,
        scratch_shapes=[state, state, kappa, both, sems(8)],
        compiler_params=params,
    )(flags, near_a, near_b, flat_classes, pad_rows, hand, inner)
    snap_far, gram = pl.pallas_call(
        far_kernel,
        out_shape=[kept(2), jax.ShapeDtypeStruct((width + 8, width), jnp.float32)],
        in_specs=[smem] + [vmem] * 6 + [hbm] * 2,
        out_specs=[vmem, vmem],
        scratch_shapes=[state, state, both, sems(10)],
        compiler_params=params,
    )(flags, far_a, far_b, weights, stiff_rows, pad_rows, gram_near, hand_a, hand_b)
    return snap_near, snap_far, gram


def lane_copy(tile, lane):
    return jnp.broadcast_to(tile[:, lane : lane + 1], (8, 128))


def row_copy(tile, row):
    return jnp.broadcast_to(tile[row : row + 1, :], (8, tile.shape[1]))


def solve_spd(left, right):
    size = left.shape[0]
    count = size // 8
    sub = lax.broadcasted_iota(jnp.int32, (8, 128), 0)
    lhs = [left[8 * t : 8 * t + 8] for t in range(count)]
    rhs = [right[8 * t : 8 * t + 8] for t in range(count)]
    for k in range(count):
        cols = [lane_copy(lhs[k], 8 * k + j) for j in range(8)]
        panel_l, panel_r = lhs[k], rhs[k]
        for j in range(8):
            recip = pl.reciprocal(row_copy(cols[j], j), approx=True)
            here = sub == j
            mult = jnp.where(here, recip, -cols[j] * recip)
            for l in range(j + 1, 8):
                cols[l] = jnp.where(here, 0.0, cols[l]) + mult * row_copy(cols[l], j)
            panel_l = jnp.where(here, 0.0, panel_l) + mult * row_copy(panel_l, j)
            panel_r = jnp.where(here, 0.0, panel_r) + mult * row_copy(panel_r, j)
        rows_l = [row_copy(panel_l, j) for j in range(8)]
        rows_r = [row_copy(panel_r, j) for j in range(8)]
        order = list(range(k + 1, count)) + list(range(k))
        for t in order:
            tile_cols = [lane_copy(lhs[t], 8 * k + j) for j in range(8)]
            if k + 1 < count:
                lhs[t] = lhs[t] - tree([tile_cols[j] * rows_l[j] for j in range(8)])
            rhs[t] = rhs[t] - tree([tile_cols[j] * rows_r[j] for j in range(8)])
        lhs[k], rhs[k] = panel_l, panel_r
    return jnp.concatenate(rhs, axis=0)


def tree(terms):
    while len(terms) > 1:
        terms = [a + b for a, b in zip(terms[::2], terms[1::2])] + terms[len(terms) & ~1 :]
    return terms[0]


def whiten(inner, block):
    size = inner.shape[0]
    count = size // 8
    sub = lax.broadcasted_iota(jnp.int32, (8, 128), 0)
    lhs = [inner[8 * t : 8 * t + 8] for t in range(count)]
    rhs = [block[8 * t : 8 * t + 8] for t in range(count)]
    done = []
    for k in range(count):
        live = range(k, count)
        cols = {t: [lane_copy(lhs[t], 8 * k + j) for j in range(8)] for t in live}
        scale = None
        for j in range(8):
            pivot = row_copy(cols[k][j], j)
            recip = pl.reciprocal(pivot, approx=True)
            root = lax.rsqrt(pivot)
            scale = root if scale is None else jnp.where(sub >= j, root, scale)
            head = {l: row_copy(cols[k][l], j) for l in range(j + 1, 8)}
            row_l, row_r = row_copy(lhs[k], j), row_copy(rhs[k], j)
            for t in live:
                mult = cols[t][j] * recip
                if t == k:
                    mult = jnp.where(sub > j, mult, 0.0)
                for l in range(j + 1, 8):
                    cols[t][l] = cols[t][l] - mult * head[l]
                lhs[t] = lhs[t] - mult[:, : row_l.shape[1]] * row_l
                rhs[t] = rhs[t] - mult * row_r
        done.append(rhs[k] * scale)
    return jnp.concatenate(done, axis=0)


def dot(a, b, dims):
    return lax.dot_general(
        a, b, (dims, ((), ())), precision=lax.Precision.HIGHEST, preferred_element_type=jnp.float32
    )


def modes_kernel(cell_count, rows_z, *refs):
    mask_ref, *part_refs, start_ref, near_hbm, far_hbm, out_ref, snap_ref, sems = refs
    planes, _, columns = snap_ref.shape
    places = [(far_hbm, 0, 0, 1), (near_hbm, 0, 1, planes - 2), (far_hbm, 1, planes - 1, 1)]
    fetches = [
        pltpu.make_async_copy(src.at[pl.ds(at, n)], snap_ref.at[pl.ds(to, n)], sems.at[k])
        for k, (src, at, to, n) in enumerate(places)
    ]
    for fetch in fetches:
        fetch.start()
    total = part_refs[0][...]
    for part in part_refs[1:]:
        total = total + part[...]
    width = total.shape[1]
    row = lax.broadcasted_iota(jnp.int32, (width, width), 0)
    col = lax.broadcasted_iota(jnp.int32, (width, width), 1)
    packed = total[:width]
    turned = packed.T
    mass = jnp.where(row <= col, packed, turned) * (1.0 / cell_count)
    stiff = jnp.where(row > col, packed, jnp.where(row < col, turned, total[width : width + 1]))
    stiff = stiff * (0.5 / cell_count)
    step = solve_spd(stiff, mass)
    form = dot(step, dot(mass, step, ((1,), (0,))), ((0,), (0,)))
    block = start_ref[...]
    for _ in range(ITERS):
        weighted = dot(block, form, ((1,), (0,)))
        solved = dot(block, step, ((1,), (1,)))
        inner = dot(weighted, block, ((1,), (1,)))
        block = whiten(inner, solved)
    modes = block.astype(jnp.bfloat16)
    for fetch in fetches:
        fetch.wait()
    lanes = LANES
    rows_y = columns // lanes
    piece_rows = planes * rows_y // out_ref.shape[0]
    for p in range(planes):
        basis = jnp.dot(modes, snap_ref[p], preferred_element_type=jnp.float32)
        for y in range(rows_y):
            piece, spot = divmod(p * rows_y + y, piece_rows)
            values = basis[:, y * lanes : y * lanes + rows_z].astype(jnp.bfloat16)
            wanted = mask_ref[piece] != 0
            out_ref[piece, :, pl.ds(spot * rows_z, rows_z)] = jnp.where(wanted, values, 0.0)


def on_device(snap_init, channel_map, yface_vals, zface_vals, face_of, start_block, correlation):
    subs = lax.axis_size("sub")
    owner_count = lax.axis_size("nbhd")
    planes, rows_y, rows_z, width = snap_init.shape[1:]
    snap_near, snap_far, own = relax(
        snap_init[0], channel_map[0], yface_vals[0], zface_vals[0], face_of[0]
    )
    parts = [own] + [
        lax.ppermute(own, "sub", [(i, (i + shift) % subs) for i in range(subs)])
        for shift in range(1, subs)
    ]
    cells = planes * rows_y * rows_z
    modes = start_block.shape[-1]
    mask = lax.dynamic_slice_in_dim(correlation, lax.axis_index("nbhd"), 1, axis=0)[0]
    pieces = pl.pallas_call(
        functools.partial(modes_kernel, float(subs * cells), rows_z),
        out_shape=jax.ShapeDtypeStruct((owner_count, modes, cells // owner_count), jnp.bfloat16),
        in_specs=[pl.BlockSpec(memory_space=pltpu.SMEM)]
        + [pl.BlockSpec(memory_space=pltpu.VMEM)] * (subs + 1)
        + [pl.BlockSpec(memory_space=pltpu.HBM)] * 2,
        scratch_shapes=[
            pltpu.VMEM((planes, width, rows_y * LANES), jnp.bfloat16),
            pltpu.SemaphoreType.DMA((3,)),
        ],
        compiler_params=pltpu.CompilerParams(vmem_limit_bytes=24 * 2**20),
    )(mask, *parts, start_block[0].T, snap_near, snap_far)
    received = lax.all_to_all(pieces, "nbhd", split_axis=0, concat_axis=0, tiled=True)
    return received[None, None]


def solution(mesh):
    return jax.shard_map(
        on_device,
        mesh=mesh,
        in_specs=(
            P("nbhd", "sub", None, None, None),
            P("nbhd", "sub", None, None),
            P("nbhd", None, None),
            P("nbhd", None, None),
            P("nbhd", None),
            P("nbhd", None, None),
            P(),
        ),
        out_specs=P("nbhd", "sub", None, None, None),
        check_vma=False,
    )
```

```python
import functools

import jax
import jax.numpy as jnp
from jax import lax
from jax.experimental import pallas as pl
from jax.experimental.pallas import tpu as pltpu
from jax.sharding import PartitionSpec as P

SWEEPS = 3
ITERS = 4


def harmonic(left_k, right_k):
    return 2.0 * left_k * right_k / (left_k + right_k)


LANES = 128


def weight_rows(kappa_ref, weights, stiff_rows, lines, first, last, rows_y, rows_z):
    total = kappa_ref.shape[0]
    depth = (total - lines) // 2
    kappa = kappa_ref[...]
    shape = kappa.shape
    line = lax.broadcasted_iota(jnp.int32, shape, 0)
    row_z = lax.broadcasted_iota(jnp.int32, shape, 1)
    row_y = lax.rem(line, rows_y)

    def face(other, edge):
        return jnp.where(edge, kappa, harmonic(kappa, other))

    top = depth + lines
    faces = [
        face(pltpu.roll(kappa, rows_y, 0), (line >= depth) & (line < depth + rows_y * first)),
        face(pltpu.roll(kappa, total - rows_y, 0), (line >= top - rows_y * last) & (line < top)),
        face(pltpu.roll(kappa, 1, 0), row_y == 0),
        face(pltpu.roll(kappa, total - 1, 0), row_y == rows_y - 1),
        face(pltpu.roll(kappa, 1, 1), row_z == 0),
        face(pltpu.roll(kappa, LANES - 1, 1), row_z == rows_z - 1),
    ]
    denom = faces[0] + faces[1] + faces[2] + faces[3] + faces[4] + faces[5]
    outside = (line < depth * first) | (line >= total - depth * last) | (row_z >= rows_z)
    scale = jnp.where(outside, 0.0, 1.0 / denom)
    for k in range(6):
        weights[k] = faces[k] * scale
    upper = row_y >= rows_y // 2
    plane = lax.div(line - depth, rows_y)
    planes = lines // rows_y
    low_cross = jnp.where(upper, 2.0 - 2.0 * first.astype(jnp.float32), 0.0)
    high_cross = jnp.where(upper, 0.0, 2.0 - 2.0 * last.astype(jnp.float32))
    shares = [
        jnp.where(plane == 0, low_cross, jnp.where(plane == 1, 0.0, 1.0)),
        jnp.where(plane == planes - 1, high_cross, jnp.where(plane == planes - 2, 0.0, 1.0)),
        jnp.where(row_y == 0, 0.0, 1.0),
        jnp.where(row_y == rows_y - 1, 0.0, 1.0),
        jnp.where(row_z == 0, 0.0, 1.0),
        jnp.where(row_z == rows_z - 1, 0.0, 1.0),
    ]
    shares[0] = jnp.where(plane == planes - 1, 2.0, shares[0])
    shares[1] = jnp.where(plane == 0, 2.0, shares[1])
    rows = [item * share for item, share in zip(faces, shares)] + [denom, kappa * (1.0 / 16.0)]
    inside = (row_z < rows_z)[depth:top]
    for k in range(8):
        stiff_rows[k] = jnp.where(inside, rows[k][depth:top], 0.0)


def turned(lines):
    width = lines.shape[1]
    row = lax.broadcasted_iota(jnp.int32, (width, width), 0)
    col = lax.broadcasted_iota(jnp.int32, (width, width), 1)
    eye = jnp.where(row == col, 1.0, 0.0).astype(jnp.bfloat16)
    return lax.dot_general(eye, lines, (((1,), (1,)), ((), ())), preferred_element_type=jnp.float32)


def place(line, rows_y):
    return lax.div(line, rows_y), lax.rem(line, rows_y)


def fill(state, source, skip, count, first_line, pad_rows):
    rows_y = pad_rows.shape[0]
    group = 16 if count % 16 == 0 else 8

    def body(i, carry):
        waiting = []

        def store(e, y, both):
            state[e, y + 1] = both[:, :LANES]
            state[e, y + 2] = both[:, LANES:]

        for j in range(0, group, 2):
            at = i * group + j
            e, y = place(first_line + at, rows_y)
            lines = [source[skip + at], pad_rows[y], source[skip + at + 1], pad_rows[y + 1]]
            waiting.append((e, y, turned(jnp.concatenate(lines, axis=0))))
            if len(waiting) > 1:
                store(*waiting.pop(0))
        for item in waiting:
            store(*item)
        return carry

    lax.fori_loop(0, count // group, body, 0)


def neighbour_sum(src, e, y, rows, some, middle):
    return (
        rows[0] * src[e - 1, y + 1, some]
        + rows[1] * src[e + 1, y + 1, some]
        + rows[2] * src[e, y, some]
        + rows[3] * src[e, y + 2, some]
        + rows[4] * pltpu.roll(middle, 1, 1)
        + rows[5] * pltpu.roll(middle, LANES - 1, 1)
    )


PART = 64


def relax_lines(src, dst, weights, first_line, count, rows_y, rows_z, keep):
    width = src.shape[2]
    group = 8
    valid = lax.broadcasted_iota(jnp.int32, (PART, LANES), 1) < rows_z

    def body(i, carry):
        waiting = []
        for j in range(group):
            line = first_line + i * group + j
            e, y = place(line, rows_y)
            rows = [weights[k, pl.ds(line, 1)] for k in range(6)]
            for start in range(0, width, PART):
                some = pl.ds(start, PART)
                middle = src[e, y + 1, some]
                fresh = neighbour_sum(src, e, y, rows, some, middle)
                fresh = fresh.astype(jnp.bfloat16).astype(jnp.float32)
                if keep:
                    fresh = jnp.where(valid, fresh, middle)
                waiting.append((e, y, some, fresh))
                if len(waiting) > 1:
                    e0, y0, some0, value = waiting.pop(0)
                    dst[e0, y0 + 1, some0] = value
        for e0, y0, some0, value in waiting:
            dst[e0, y0 + 1, some0] = value
        return carry

    lax.fori_loop(0, count // group, body, 0)


def gram_terms(final, places, planes, stiff_rows, snap, both, total):
    _, width, columns = snap.shape
    rows_y = columns // LANES
    for item, e in enumerate(places):
        p = e - planes
        waiting = []

        def store(y, some, below, values, item=item):
            spot = pl.ds(y * LANES, LANES)
            snap[item, some, spot] = values[0]
            both[some, spot] = values[1]
            both[below, spot] = values[2]

        for y in range(rows_y):
            rows = [stiff_rows[k, pl.ds(p * rows_y + y, 1)] for k in range(8)]
            for start in range(0, width, PART):
                some = pl.ds(start, PART)
                middle = final[e, y + 1, some]
                numer = neighbour_sum(final, e, y, rows, some, middle)
                values = [middle, rows[7] * middle, rows[6] * middle - numer]
                values = [value.astype(jnp.bfloat16) for value in values]
                waiting.append((y, some, pl.ds(width + start, PART), values))
                if len(waiting) > 1:
                    store(*waiting.pop(0))
        for entry in waiting:
            store(*entry)
        total = total + lax.dot_general(
            snap[item], both[...], (((1,), (1,)), ((), ())), preferred_element_type=jnp.float32
        )
    return total


def powers(marks):
    return jnp.left_shift(jnp.int32(1), 2 * marks).astype(jnp.float32)


def own_kernel(
    flags,
    own,
    classes,
    y_vals,
    z_vals,
    face_ids,
    state_a,
    state_b,
    pad_rows,
    kappa,
    weights,
    stiff_rows,
):
    lines, rows_z, width = own.shape
    rows_y = pad_rows.shape[0]
    planes = lines // rows_y
    bf16 = jnp.bfloat16
    ids = face_ids[...]
    picks = [(ids == side).astype(jnp.float32) for side in range(4)]
    spare = LANES - rows_z
    spot = lax.broadcasted_iota(jnp.int32, (spare, width), 0)
    z_all = z_vals[...].astype(jnp.float32)
    z_low = z_all * picks[2]
    z_high = z_all * picks[3]
    for y in range(rows_y):
        rows = jnp.where(spot == 0, z_high[y : y + 1], 0.0)
        pad_rows[y] = jnp.where(spot == spare - 1, z_low[y : y + 1], rows).astype(bf16)
    y_all = y_vals[...].astype(jnp.float32)
    blank = jnp.zeros((spare, width), bf16)
    ghost_low = turned(jnp.concatenate([(y_all * picks[0]).astype(bf16), blank], axis=0))
    ghost_high = turned(jnp.concatenate([(y_all * picks[1]).astype(bf16), blank], axis=0))

    def edges(e, carry):
        for state in (state_a, state_b):
            state[e, 0] = ghost_low
            state[e, rows_y + 1] = ghost_high
        return carry

    lax.fori_loop(1, state_a.shape[0] - 1, edges, 0)
    fill(state_a, own, 0, lines, lines, pad_rows)
    kappa[...] = jnp.ones(kappa.shape, jnp.float32)
    kappa[pl.ds(lines, lines), pl.ds(0, rows_z)] = powers(classes[...])
    weight_rows(kappa, weights, stiff_rows, lines, flags[1], flags[2], rows_y, rows_z)
    middle = (lines + rows_y, lines - 2 * rows_y)
    relax_lines(state_a, state_b, weights, *middle, rows_y, rows_z, True)


def near_kernel(
    flags,
    near_a,
    near_b,
    class_a,
    class_b,
    classes,
    pad_rows,
    old_a,
    old_b,
    state_a,
    state_b,
    weights,
    stiff_rows,
    snap,
    gram,
    kappa,
    both,
):
    del old_a, old_b
    lines, rows_z = classes.shape
    rows_y = pad_rows.shape[0]
    near = lines // 2
    even, first, last = flags[0], flags[1], flags[2]
    base_a = pl.multiple_of(even * (2 * lines), 8)
    base_b = pl.multiple_of((1 - even) * (2 * lines), 8)
    kappa[...] = jnp.ones(kappa.shape, jnp.float32)
    for base, marks in ((lines, classes), (base_a, class_a), (base_b, class_b)):
        kappa[pl.ds(base, lines), pl.ds(0, rows_z)] = powers(marks[...])
    weight_rows(kappa, weights, stiff_rows, lines, first, last, rows_y, rows_z)
    fill(state_a, near_a, 0, near, near + even * (lines + near), pad_rows)
    fill(state_a, near_b, 0, near, near + (1 - even) * (lines + near), pad_rows)
    step = functools.partial(relax_lines, weights=weights, rows_y=rows_y, rows_z=rows_z)
    step(state_a, state_b, first_line=lines - rows_y, count=2 * rows_y, keep=True)
    step(state_a, state_b, first_line=2 * lines - rows_y, count=2 * rows_y, keep=True)
    step(state_b, state_a, first_line=lines, count=lines, keep=True)
    step(state_a, state_b, first_line=lines + rows_y, count=lines - 2 * rows_y, keep=False)
    planes = lines // rows_y
    inside = range(planes + 1, 2 * planes - 1)
    blank = jnp.zeros(gram.shape, jnp.float32)
    gram[...] = gram_terms(state_b, inside, planes, stiff_rows, snap, both, blank)


def far_kernel(
    flags,
    far_a,
    far_b,
    weights,
    stiff_rows,
    pad_rows,
    near_gram,
    old_a,
    old_b,
    state_a,
    state_b,
    snap,
    gram,
    both,
):
    del old_a, old_b
    width = snap.shape[1]
    rows_y = pad_rows.shape[0]
    far, rows_z = far_a.shape[:2]
    lines = stiff_rows.shape[1]
    planes = lines // rows_y
    half = rows_y // 2
    even = flags[0]
    low_line = half
    high_line = 3 * lines - half - far
    fill(state_a, far_a, 0, far, low_line + even * (high_line - low_line), pad_rows)
    fill(state_a, far_b, 0, far, high_line - even * (high_line - low_line), pad_rows)
    buffers = (state_a, state_b)
    for sweep in range(1, SWEEPS + 1):
        src, dst = buffers[(sweep - 1) % 2], buffers[sweep % 2]
        for first_line in (half + sweep * rows_y, 3 * lines - half - far - sweep * rows_y):
            relax_lines(src, dst, weights, first_line, far, rows_y, rows_z, sweep < SWEEPS)
    final = buffers[SWEEPS % 2]
    outer = (planes, 2 * planes - 1)
    total = gram_terms(final, outer, planes, stiff_rows, snap, both, near_gram[...])
    mass = total[:, :width]
    stiff = total[:, width:]
    stiff = stiff + stiff.T
    row = lax.broadcasted_iota(jnp.int32, (width, width), 0)
    col = lax.broadcasted_iota(jnp.int32, (width, width), 1)
    gram[pl.ds(0, width)] = jnp.where(row > col, stiff, mass)
    diagonal = jnp.sum(jnp.where(row == col, stiff, 0.0), axis=0, keepdims=True)
    gram[pl.ds(width, 8)] = jnp.broadcast_to(diagonal, (8, width))


def swap(array, start):
    count = lax.axis_size("sub")
    pairs = [(i, i + 1) for i in range(start, count - 1, 2)]
    return lax.ppermute(array, "sub", pairs + [(j, i) for i, j in pairs])


def relax(initial, classes, y_vals, z_vals, face_ids):
    planes, rows_y, rows_z, width = initial.shape
    index = lax.axis_index("sub")
    subs = lax.axis_size("sub")
    even = (index + 1) % 2
    flags = jnp.stack([even, index == 0, index == subs - 1, 0]).astype(jnp.int32)
    lines = initial.reshape(planes * rows_y, rows_z, width)
    count = planes * rows_y
    near, far, half = 2 * rows_y, 2 * rows_y - rows_y // 2, rows_y // 2
    def near_part(upward):
        return lax.dynamic_slice_in_dim(lines, upward * (count - near), near, axis=0)

    def far_part(upward):
        start = upward * half + (1 - upward) * near
        return lax.dynamic_slice_in_dim(lines, start, far, axis=0)

    near_a = swap(near_part(even), 0)
    near_b = swap(near_part(1 - even), 1)
    flat_classes = classes.reshape(count, rows_z)
    class_a = swap(flat_classes, 0)
    class_b = swap(flat_classes, 1)
    far_a = swap(far_part(even), 0)
    far_b = swap(far_part(1 - even), 1)

    vmem = pl.BlockSpec(memory_space=pltpu.VMEM)
    smem = pl.BlockSpec(memory_space=pltpu.SMEM)
    state = pltpu.VMEM((3 * planes, rows_y + 2, width, LANES), jnp.float32)
    kappa = pltpu.VMEM((3 * count, LANES), jnp.float32)
    both = pltpu.VMEM((2 * width, rows_y * LANES), jnp.bfloat16)
    params = pltpu.CompilerParams(vmem_limit_bytes=14 * 2**20)

    def kept(depth):
        return jax.ShapeDtypeStruct((depth, width, rows_y * LANES), jnp.bfloat16)

    def held(item):
        return pltpu.with_memory_space_constraint(item, pltpu.VMEM)

    rows = [
        jax.ShapeDtypeStruct((6, 3 * count, LANES), jnp.float32),
        jax.ShapeDtypeStruct((8, count, LANES), jnp.float32),
    ]
    state_a, state_b, pad_rows = pl.pallas_call(
        own_kernel,
        out_shape=[
            state,
            state,
            jax.ShapeDtypeStruct((rows_y, LANES - rows_z, width), jnp.bfloat16),
        ],
        in_specs=[smem] + [vmem] * 5,
        out_specs=[vmem] * 3,
        scratch_shapes=[kappa] + [pltpu.VMEM(item.shape, item.dtype) for item in rows],
        compiler_params=params,
    )(flags, lines, flat_classes, y_vals, z_vals, face_ids[None])
    state_a, state_b, weights, stiff_rows, snap_near, gram_near = pl.pallas_call(
        near_kernel,
        out_shape=[
            state,
            state,
            *rows,
            kept(planes - 2),
            jax.ShapeDtypeStruct((width, 2 * width), jnp.float32),
        ],
        in_specs=[smem] + [vmem] * 8,
        out_specs=[vmem] * 6,
        scratch_shapes=[kappa, both],
        input_output_aliases={7: 0, 8: 1},
        compiler_params=params,
    )(
        flags,
        near_a,
        near_b,
        class_a,
        class_b,
        flat_classes,
        pad_rows,
        held(state_a),
        held(state_b),
    )
    _, _, snap_far, gram = pl.pallas_call(
        far_kernel,
        out_shape=[state, state, kept(2), jax.ShapeDtypeStruct((width + 8, width), jnp.float32)],
        in_specs=[smem] + [vmem] * 8,
        out_specs=[vmem] * 4,
        scratch_shapes=[both],
        input_output_aliases={7: 0, 8: 1},
        compiler_params=params,
    )(
        flags,
        far_a,
        far_b,
        weights,
        stiff_rows,
        pad_rows,
        gram_near,
        held(state_a),
        held(state_b),
    )
    return snap_near, snap_far, gram


def lane_copy(tile, lane):
    return jnp.broadcast_to(tile[:, lane : lane + 1], (8, 128))


def row_copy(tile, row):
    return jnp.broadcast_to(tile[row : row + 1, :], (8, tile.shape[1]))


def eliminate(cols, panels):
    grid = {(i, j): row_copy(cols[j], i) for j in range(8) for i in range(j, 8)}
    rows = [[row_copy(panel, i) for panel in panels] for i in range(8)]
    factor, pivots, recips = {}, [], []
    for j in range(8):
        pivot = grid[j, j]
        recip = pl.reciprocal(pivot, approx=True)
        pivots.append(pivot)
        recips.append(recip)
        for i in range(j + 1, 8):
            factor[i, j] = grid[i, j] * recip
            for k in range(j + 1, i + 1):
                grid[i, k] = grid[i, k] - factor[i, j] * grid[k, j]
            rows[i] = [a - factor[i, j][:, : a.shape[1]] * b for a, b in zip(rows[i], rows[j])]
    solved = [[a * recips[i][:, : a.shape[1]] for a in rows[i]] for i in range(8)]
    for i in range(7, 0, -1):
        for j in range(i):
            solved[j] = [
                a - factor[i, j][:, : a.shape[1]] * b for a, b in zip(solved[j], solved[i])
            ]
    return rows, pivots, solved


def gather_rows(rows):
    sub = lax.broadcasted_iota(jnp.int32, rows[0].shape, 0)
    out = rows[0]
    for i in range(1, 8):
        out = jnp.where(sub == i, rows[i], out)
    return out


def solve_spd(left, right):
    size = left.shape[0]
    count = size // 8
    lhs = [left[8 * t : 8 * t + 8] for t in range(count)]
    rhs = [right[8 * t : 8 * t + 8] for t in range(count)]
    for k in range(count):
        cols = [lane_copy(lhs[k], 8 * k + j) for j in range(8)]
        _, _, solved = eliminate(cols, [lhs[k], rhs[k]])
        for t in list(range(k + 1, count)) + list(range(k)):
            tile_cols = [lane_copy(lhs[t], 8 * k + j) for j in range(8)]
            if k + 1 < count:
                lhs[t] = lhs[t] - tree([tile_cols[j] * solved[j][0] for j in range(8)])
            rhs[t] = rhs[t] - tree([tile_cols[j] * solved[j][1] for j in range(8)])
        lhs[k] = gather_rows([solved[j][0] for j in range(8)])
        rhs[k] = gather_rows([solved[j][1] for j in range(8)])
    return jnp.concatenate(rhs, axis=0)


def tree(terms):
    while len(terms) > 1:
        terms = [a + b for a, b in zip(terms[::2], terms[1::2])] + terms[len(terms) & ~1 :]
    return terms[0]


def whiten(inner, block):
    size = inner.shape[0]
    count = size // 8
    lhs = [inner[8 * t : 8 * t + 8] for t in range(count)]
    rhs = [block[8 * t : 8 * t + 8] for t in range(count)]
    done = []
    for k in range(count):
        cols = [lane_copy(lhs[k], 8 * k + j) for j in range(8)]
        rows, pivots, solved = eliminate(cols, [lhs[k], rhs[k]])
        done.append(gather_rows([rows[j][1] * lax.rsqrt(pivots[j]) for j in range(8)]))
        for t in range(k + 1, count):
            tile_cols = [lane_copy(lhs[t], 8 * k + j) for j in range(8)]
            lhs[t] = lhs[t] - tree([tile_cols[j][:, :size] * solved[j][0] for j in range(8)])
            rhs[t] = rhs[t] - tree([tile_cols[j] * solved[j][1] for j in range(8)])
    return jnp.concatenate(done, axis=0)


def dot(a, b, dims):
    return lax.dot_general(
        a, b, (dims, ((), ())), precision=lax.Precision.HIGHEST, preferred_element_type=jnp.float32
    )


def modes_kernel(cell_count, rows_z, *refs):
    mask_ref, *part_refs, start_ref, near_hbm, far_hbm, out_ref, snap_ref, sems = refs
    planes, _, columns = snap_ref.shape
    places = [(far_hbm, 0, 0, 1), (near_hbm, 0, 1, planes - 2), (far_hbm, 1, planes - 1, 1)]
    fetches = [
        pltpu.make_async_copy(src.at[pl.ds(at, n)], snap_ref.at[pl.ds(to, n)], sems.at[k])
        for k, (src, at, to, n) in enumerate(places)
    ]
    for fetch in fetches:
        fetch.start()
    total = part_refs[0][...]
    for part in part_refs[1:]:
        total = total + part[...]
    width = total.shape[1]
    row = lax.broadcasted_iota(jnp.int32, (width, width), 0)
    col = lax.broadcasted_iota(jnp.int32, (width, width), 1)
    packed = total[:width]
    turned = packed.T
    mass = jnp.where(row <= col, packed, turned) * (1.0 / cell_count)
    stiff = jnp.where(row > col, packed, jnp.where(row < col, turned, total[width : width + 1]))
    stiff = stiff * (0.5 / cell_count)
    step = solve_spd(stiff, mass)
    form = dot(step, dot(mass, step, ((1,), (0,))), ((0,), (0,)))
    block = start_ref[...]
    for _ in range(ITERS):
        weighted = dot(block, form, ((1,), (0,)))
        solved = dot(block, step, ((1,), (1,)))
        inner = dot(weighted, block, ((1,), (1,)))
        block = whiten(inner, solved)
    modes = block.astype(jnp.bfloat16)
    for fetch in fetches:
        fetch.wait()
    lanes = LANES
    rows_y = columns // lanes
    piece_rows = planes * rows_y // out_ref.shape[0]
    for p in range(planes):
        basis = jnp.dot(modes, snap_ref[p], preferred_element_type=jnp.float32)
        for y in range(rows_y):
            piece, spot = divmod(p * rows_y + y, piece_rows)
            values = basis[:, y * lanes : y * lanes + rows_z].astype(jnp.bfloat16)
            wanted = mask_ref[piece] != 0
            out_ref[piece, :, pl.ds(spot * rows_z, rows_z)] = jnp.where(wanted, values, 0.0)


def on_device(snap_init, channel_map, yface_vals, zface_vals, face_of, start_block, correlation):
    subs = lax.axis_size("sub")
    owner_count = lax.axis_size("nbhd")
    planes, rows_y, rows_z, width = snap_init.shape[1:]
    snap_near, snap_far, own = relax(
        snap_init[0], channel_map[0], yface_vals[0], zface_vals[0], face_of[0]
    )
    parts = [own] + [
        lax.ppermute(own, "sub", [(i, (i + shift) % subs) for i in range(subs)])
        for shift in range(1, subs)
    ]
    cells = planes * rows_y * rows_z
    modes = start_block.shape[-1]
    mask = lax.dynamic_slice_in_dim(correlation, lax.axis_index("nbhd"), 1, axis=0)[0]
    pieces = pl.pallas_call(
        functools.partial(modes_kernel, float(subs * cells), rows_z),
        out_shape=jax.ShapeDtypeStruct((owner_count, modes, cells // owner_count), jnp.bfloat16),
        in_specs=[pl.BlockSpec(memory_space=pltpu.SMEM)]
        + [pl.BlockSpec(memory_space=pltpu.VMEM)] * (subs + 1)
        + [pl.BlockSpec(memory_space=pltpu.HBM)] * 2,
        scratch_shapes=[
            pltpu.VMEM((planes, width, rows_y * LANES), jnp.bfloat16),
            pltpu.SemaphoreType.DMA((3,)),
        ],
        compiler_params=pltpu.CompilerParams(vmem_limit_bytes=24 * 2**20),
    )(mask, *parts, start_block[0].T, snap_near, snap_far)
    received = lax.all_to_all(pieces, "nbhd", split_axis=0, concat_axis=0, tiled=True)
    return received[None, None]


def solution(mesh):
    return jax.shard_map(
        on_device,
        mesh=mesh,
        in_specs=(
            P("nbhd", "sub", None, None, None),
            P("nbhd", "sub", None, None),
            P("nbhd", None, None),
            P("nbhd", None, None),
            P("nbhd", None),
            P("nbhd", None, None),
            P(),
        ),
        out_specs=P("nbhd", "sub", None, None, None),
        check_vma=False,
    )
```

```python
import functools

import jax
import jax.numpy as jnp
from jax import lax
from jax.experimental import pallas as pl
from jax.experimental.pallas import tpu as pltpu
from jax.sharding import PartitionSpec as P

SWEEPS = 3
ITERS = 4


def harmonic(left_k, right_k):
    return 2.0 * left_k * right_k / (left_k + right_k)


LANES = 128


def weight_rows(kappa_ref, weights, stiff_rows, lines, first, last, rows_y, rows_z):
    total = kappa_ref.shape[0]
    depth = (total - lines) // 2
    kappa = kappa_ref[...]
    shape = kappa.shape
    line = lax.broadcasted_iota(jnp.int32, shape, 0)
    row_z = lax.broadcasted_iota(jnp.int32, shape, 1)
    row_y = lax.rem(line, rows_y)

    def face(other, edge):
        return jnp.where(edge, kappa, harmonic(kappa, other))

    top = depth + lines
    faces = [
        face(pltpu.roll(kappa, rows_y, 0), (line >= depth) & (line < depth + rows_y * first)),
        face(pltpu.roll(kappa, total - rows_y, 0), (line >= top - rows_y * last) & (line < top)),
        face(pltpu.roll(kappa, 1, 0), row_y == 0),
        face(pltpu.roll(kappa, total - 1, 0), row_y == rows_y - 1),
        face(pltpu.roll(kappa, 1, 1), row_z == 0),
        face(pltpu.roll(kappa, LANES - 1, 1), row_z == rows_z - 1),
    ]
    denom = faces[0] + faces[1] + faces[2] + faces[3] + faces[4] + faces[5]
    outside = (line < depth * first) | (line >= total - depth * last) | (row_z >= rows_z)
    scale = jnp.where(outside, 0.0, 1.0 / denom)
    for k in range(6):
        weights[k] = faces[k] * scale
    upper = row_y >= rows_y // 2
    plane = lax.div(line - depth, rows_y)
    planes = lines // rows_y
    low_cross = jnp.where(upper, 2.0 - 2.0 * first.astype(jnp.float32), 0.0)
    high_cross = jnp.where(upper, 0.0, 2.0 - 2.0 * last.astype(jnp.float32))
    shares = [
        jnp.where(plane == 0, low_cross, jnp.where(plane == 1, 0.0, 1.0)),
        jnp.where(plane == planes - 1, high_cross, jnp.where(plane == planes - 2, 0.0, 1.0)),
        jnp.where(row_y == 0, 0.0, 1.0),
        jnp.where(row_y == rows_y - 1, 0.0, 1.0),
        jnp.where(row_z == 0, 0.0, 1.0),
        jnp.where(row_z == rows_z - 1, 0.0, 1.0),
    ]
    shares[0] = jnp.where(plane == planes - 1, 2.0, shares[0])
    shares[1] = jnp.where(plane == 0, 2.0, shares[1])
    rows = [item * share for item, share in zip(faces, shares)] + [denom, kappa * (1.0 / 16.0)]
    inside = (row_z < rows_z)[depth:top]
    for k in range(8):
        stiff_rows[k] = jnp.where(inside, rows[k][depth:top], 0.0)


def turned(lines):
    width = lines.shape[1]
    row = lax.broadcasted_iota(jnp.int32, (width, width), 0)
    col = lax.broadcasted_iota(jnp.int32, (width, width), 1)
    eye = jnp.where(row == col, 1.0, 0.0).astype(jnp.bfloat16)
    return lax.dot_general(eye, lines, (((1,), (1,)), ((), ())), preferred_element_type=jnp.float32)


def place(line, rows_y):
    return lax.div(line, rows_y), lax.rem(line, rows_y)


def fill(state, source, skip, count, first_line, pad_rows):
    rows_y = pad_rows.shape[0]
    group = 16 if count % 16 == 0 else 8

    def body(i, carry):
        waiting = []

        def store(e, y, both):
            state[e, y + 1] = both[:, :LANES]
            state[e, y + 2] = both[:, LANES:]

        for j in range(0, group, 2):
            at = i * group + j
            e, y = place(first_line + at, rows_y)
            lines = [source[skip + at], pad_rows[y], source[skip + at + 1], pad_rows[y + 1]]
            waiting.append((e, y, turned(jnp.concatenate(lines, axis=0))))
            if len(waiting) > 1:
                store(*waiting.pop(0))
        for item in waiting:
            store(*item)
        return carry

    lax.fori_loop(0, count // group, body, 0)


def neighbour_sum(src, e, y, rows, some, middle):
    return (
        rows[0] * src[e - 1, y + 1, some]
        + rows[1] * src[e + 1, y + 1, some]
        + rows[2] * src[e, y, some]
        + rows[3] * src[e, y + 2, some]
        + rows[4] * pltpu.roll(middle, 1, 1)
        + rows[5] * pltpu.roll(middle, LANES - 1, 1)
    )


PART = 64


def relax_lines(src, dst, weights, first_lines, count, rows_y, rows_z, keep):
    width = src.shape[2]
    group = 8
    total = weights.shape[1] // rows_y
    src_skip = (total - src.shape[0]) // 2
    dst_skip = (total - dst.shape[0]) // 2
    valid = lax.broadcasted_iota(jnp.int32, (PART, LANES), 1) < rows_z

    def body(i, carry):
        waiting = []
        for j in range(group * len(first_lines)):
            line = first_lines[j // group] + i * group + j % group
            e, y = place(line, rows_y)
            rows = [weights[k, pl.ds(line, 1)] for k in range(6)]
            for start in range(0, width, PART):
                some = pl.ds(start, PART)
                middle = src[e - src_skip, y + 1, some]
                fresh = neighbour_sum(src, e - src_skip, y, rows, some, middle)
                fresh = fresh.astype(jnp.bfloat16).astype(jnp.float32)
                if keep:
                    fresh = jnp.where(valid, fresh, middle)
                waiting.append((e - dst_skip, y, some, fresh))
                if len(waiting) > 1:
                    e0, y0, some0, value = waiting.pop(0)
                    dst[e0, y0 + 1, some0] = value
        for e0, y0, some0, value in waiting:
            dst[e0, y0 + 1, some0] = value
        return carry

    lax.fori_loop(0, count // group, body, 0)


def gram_terms(final, places, planes, stiff_rows, snap, both, total):
    _, width, columns = snap.shape
    rows_y = columns // LANES
    for item, e in enumerate(places):
        p = e - planes
        e = e - (3 * planes - final.shape[0]) // 2
        waiting = []

        def store(y, some, below, values, item=item):
            spot = pl.ds(y * LANES, LANES)
            snap[item, some, spot] = values[0]
            both[some, spot] = values[1]
            both[below, spot] = values[2]

        for y in range(rows_y):
            rows = [stiff_rows[k, pl.ds(p * rows_y + y, 1)] for k in range(8)]
            for start in range(0, width, PART):
                some = pl.ds(start, PART)
                middle = final[e, y + 1, some]
                numer = neighbour_sum(final, e, y, rows, some, middle)
                values = [middle, rows[7] * middle, rows[6] * middle - numer]
                values = [value.astype(jnp.bfloat16) for value in values]
                waiting.append((y, some, pl.ds(width + start, PART), values))
                if len(waiting) > 1:
                    store(*waiting.pop(0))
        for entry in waiting:
            store(*entry)
        total = total + lax.dot_general(
            snap[item], both[...], (((1,), (1,)), ((), ())), preferred_element_type=jnp.float32
        )
    return total


def powers(marks):
    return jnp.left_shift(jnp.int32(1), 2 * marks).astype(jnp.float32)


def pack_kernel(flags, class_map, lines, near_a, near_b, far_a, far_b, classes, sems):
    count, rows_z = classes.shape
    far = far_a.shape[0]
    near = near_a.shape[0] - 1
    upward = flags[0]
    fetch = pltpu.make_async_copy(class_map, classes, sems.at[4])
    fetch.start()
    copies = []
    for out, skip, size, start in (
        (near_a, 1, near, upward * (count - near)),
        (near_b, 1, near, (1 - upward) * (count - near)),
        (far_a, 0, far, near - upward * far),
        (far_b, 0, far, near - (1 - upward) * far),
    ):
        copies.append(
            pltpu.make_async_copy(
                lines.at[pl.ds(start, size)], out.at[pl.ds(skip, size)], sems.at[len(copies)]
            )
        )
        copies[-1].start()
    fetch.wait()
    marks = classes[...].astype(jnp.float32).astype(jnp.bfloat16)
    width = near_a.shape[2]
    marks = jnp.concatenate([marks, jnp.zeros((count, width - rows_z), jnp.bfloat16)], axis=1)
    for out in (near_a, near_b):
        out[0, pl.ds(0, count)] = marks
        out[0, pl.ds(count, rows_z - count)] = jnp.zeros((rows_z - count, width), jnp.bfloat16)
    for copy in copies:
        copy.wait()


def own_kernel(
    flags,
    own,
    classes,
    y_vals,
    z_vals,
    face_ids,
    state_a,
    state_b,
    pad_rows,
    last_a,
    last_b,
    own_kappa,
    kappa,
    weights,
    stiff_rows,
):
    lines, rows_z, width = own.shape
    rows_y = pad_rows.shape[0]
    planes = lines // rows_y
    bf16 = jnp.bfloat16
    ids = face_ids[...]
    picks = [(ids == side).astype(jnp.float32) for side in range(4)]
    spare = LANES - rows_z
    spot = lax.broadcasted_iota(jnp.int32, (spare, width), 0)
    z_all = z_vals[...].astype(jnp.float32)
    z_low = z_all * picks[2]
    z_high = z_all * picks[3]
    for y in range(rows_y):
        rows = jnp.where(spot == 0, z_high[y : y + 1], 0.0)
        pad_rows[y] = jnp.where(spot == spare - 1, z_low[y : y + 1], rows).astype(bf16)
    y_all = y_vals[...].astype(jnp.float32)
    blank = jnp.zeros((spare, width), bf16)
    ghost_low = turned(jnp.concatenate([(y_all * picks[0]).astype(bf16), blank], axis=0))
    ghost_high = turned(jnp.concatenate([(y_all * picks[1]).astype(bf16), blank], axis=0))

    def edges(e, carry):
        for state, at in ((state_a, e + 1), (state_b, e)):
            state[at, 0] = ghost_low
            state[at, rows_y + 1] = ghost_high
        return carry

    lax.fori_loop(0, state_b.shape[0], edges, 0)
    fill(state_a, own, 0, lines, lines, pad_rows)
    kappa[...] = jnp.ones(kappa.shape, jnp.float32)
    kappa[pl.ds(lines, lines), pl.ds(0, rows_z)] = powers(classes[...])
    own_kappa[...] = kappa[pl.ds(lines, lines)]
    weight_rows(kappa, weights, stiff_rows, lines, flags[1], flags[2], rows_y, rows_z)
    inside = lines - 2 * rows_y
    relax_lines(state_a, state_b, weights, (lines + rows_y,), inside, rows_y, rows_z, True)
    half = rows_y // 2
    for out, upward in ((last_a, flags[0]), (last_b, 1 - flags[0])):
        out[...] = own[pl.ds(upward * half + (1 - upward) * (lines - rows_y), half)]


def near_kernel(
    flags,
    near_a,
    near_b,
    own_kappa,
    pad_rows,
    old_a,
    old_b,
    state_a,
    state_b,
    weights,
    stiff_rows,
    snap,
    gram,
    kappa,
    both,
):
    del old_a, old_b
    lines = own_kappa.shape[0]
    rows_z = near_a.shape[1]
    rows_y = pad_rows.shape[0]
    near = lines // 2
    even, first, last = flags[0], flags[1], flags[2]
    base_a = pl.multiple_of(even * (2 * lines), 8)
    base_b = pl.multiple_of((1 - even) * (2 * lines), 8)
    kappa[...] = jnp.ones(kappa.shape, jnp.float32)
    kappa[pl.ds(lines, lines)] = own_kappa[...]
    for base, part in ((base_a, near_a), (base_b, near_b)):
        marks = part[0][:lines].astype(jnp.float32).astype(jnp.int32)
        kappa[pl.ds(base, lines)] = powers(marks)
    weight_rows(kappa, weights, stiff_rows, lines, first, last, rows_y, rows_z)
    fill(state_a, near_a, 1, near, near + even * (lines + near), pad_rows)
    fill(state_a, near_b, 1, near, near + (1 - even) * (lines + near), pad_rows)
    step = functools.partial(relax_lines, weights=weights, rows_y=rows_y, rows_z=rows_z)
    ends = (lines - rows_y, 2 * lines - rows_y)
    step(state_a, state_b, first_lines=ends, count=2 * rows_y, keep=True)
    step(state_b, state_a, first_lines=(lines,), count=lines, keep=True)
    inner = (lines + rows_y,)
    step(state_a, state_b, first_lines=inner, count=lines - 2 * rows_y, keep=False)
    planes = lines // rows_y
    inside = range(planes + 1, 2 * planes - 1)
    blank = jnp.zeros(gram.shape, jnp.float32)
    gram[...] = gram_terms(state_b, inside, planes, stiff_rows, snap, both, blank)


def advance(buffers, weights, low_line, count, total, rows_y, rows_z):
    for sweep in range(1, SWEEPS + 1):
        src, dst = buffers[(sweep - 1) % 2], buffers[sweep % 2]
        low = low_line + sweep * rows_y
        ends = (low, total - low - count)
        relax_lines(src, dst, weights, ends, count, rows_y, rows_z, sweep < SWEEPS)


def far_kernel(flags, far_a, far_b, weights, pad_rows, old_a, old_b, state_a, state_b):
    del old_a, old_b
    rows_y = pad_rows.shape[0]
    count, rows_z = far_a.shape[:2]
    total = weights.shape[1]
    even = flags[0]
    shift = even * (total - 2 * rows_y - count)
    fill(state_a, far_a, 0, count, rows_y + shift, pad_rows)
    fill(state_a, far_b, 0, count, total - rows_y - count - shift, pad_rows)
    advance((state_a, state_b), weights, rows_y, count, total, rows_y, rows_z)


def last_kernel(
    flags,
    last_a,
    last_b,
    weights,
    stiff_rows,
    pad_rows,
    near_gram,
    old_a,
    old_b,
    state_a,
    state_b,
    snap,
    gram,
    both,
):
    del old_a, old_b
    width = snap.shape[1]
    rows_y = pad_rows.shape[0]
    count, rows_z = last_a.shape[:2]
    planes = stiff_rows.shape[1] // rows_y
    lines = weights.shape[1]
    shift = flags[0] * (lines - 3 * count)
    fill(state_a, last_a, 0, count, count + shift, pad_rows)
    fill(state_a, last_b, 0, count, lines - 2 * count - shift, pad_rows)
    buffers = (state_a, state_b)
    advance(buffers, weights, count, count, lines, rows_y, rows_z)
    final = buffers[SWEEPS % 2]
    outer = (planes, 2 * planes - 1)
    total = gram_terms(final, outer, planes, stiff_rows, snap, both, near_gram[...])
    mass = total[:, :width]
    stiff = total[:, width:]
    stiff = stiff + stiff.T
    row = lax.broadcasted_iota(jnp.int32, (width, width), 0)
    col = lax.broadcasted_iota(jnp.int32, (width, width), 1)
    gram[pl.ds(0, width)] = jnp.where(row > col, stiff, mass)
    diagonal = jnp.sum(jnp.where(row == col, stiff, 0.0), axis=0, keepdims=True)
    gram[pl.ds(width, 8)] = jnp.broadcast_to(diagonal, (8, width))


def swap(array, start):
    count = lax.axis_size("sub")
    pairs = [(i, i + 1) for i in range(start, count - 1, 2)]
    return lax.ppermute(array, "sub", pairs + [(j, i) for i, j in pairs])


def relax(initial, classes, y_vals, z_vals, face_ids):
    planes, rows_y, rows_z, width = initial.shape
    index = lax.axis_index("sub")
    subs = lax.axis_size("sub")
    even = (index + 1) % 2
    flags = jnp.stack([even, index == 0, index == subs - 1, 0]).astype(jnp.int32)
    lines = initial.reshape(planes * rows_y, rows_z, width)
    count = planes * rows_y
    near, half = 2 * rows_y, rows_y // 2
    flat_classes = classes.reshape(count, rows_z)
    part = functools.partial(jax.ShapeDtypeStruct, dtype=initial.dtype)
    vmem = pl.BlockSpec(memory_space=pltpu.VMEM)
    smem = pl.BlockSpec(memory_space=pltpu.SMEM)
    first_state = pltpu.VMEM((3 * planes, rows_y + 2, width, LANES), jnp.float32)
    second_state = pltpu.VMEM((3 * planes - 2, rows_y + 2, width, LANES), jnp.float32)
    kappa = pltpu.VMEM((3 * count, LANES), jnp.float32)
    both = pltpu.VMEM((2 * width, rows_y * LANES), jnp.bfloat16)
    params = pltpu.CompilerParams(vmem_limit_bytes=8 * 2**20)

    def kept(depth):
        return jax.ShapeDtypeStruct((depth, width, rows_y * LANES), jnp.bfloat16)

    def in_hbm(item):
        return pltpu.with_memory_space_constraint(item, pltpu.HBM)

    def held(item):
        return pltpu.with_memory_space_constraint(item, pltpu.VMEM)

    rows = [
        jax.ShapeDtypeStruct((6, 3 * count, LANES), jnp.float32),
        jax.ShapeDtypeStruct((8, count, LANES), jnp.float32),
    ]
    near_a, near_b, far_a, far_b = pl.pallas_call(
        pack_kernel,
        out_shape=[part((near + 1, rows_z, width))] * 2 + [part((rows_y, rows_z, width))] * 2,
        in_specs=[smem] + [pl.BlockSpec(memory_space=pltpu.HBM)] * 2,
        out_specs=[vmem] * 4,
        scratch_shapes=[
            pltpu.VMEM((count, rows_z), jnp.int32),
            pltpu.SemaphoreType.DMA((5,)),
        ],
        compiler_params=params,
    )(flags, in_hbm(flat_classes), in_hbm(lines))
    near_a = swap(near_a, 0)
    near_b = swap(near_b, 1)
    far_a = swap(far_a, 0)
    far_b = swap(far_b, 1)
    state_a, state_b, pad_rows, last_a, last_b, own_kappa = pl.pallas_call(
        own_kernel,
        out_shape=[
            first_state,
            second_state,
            part((rows_y, LANES - rows_z, width)),
            part((half, rows_z, width)),
            part((half, rows_z, width)),
            jax.ShapeDtypeStruct((count, LANES), jnp.float32),
        ],
        in_specs=[smem] + [vmem] * 5,
        out_specs=[vmem] * 6,
        scratch_shapes=[kappa] + [pltpu.VMEM(item.shape, item.dtype) for item in rows],
        compiler_params=params,
    )(flags, lines, flat_classes, y_vals, z_vals, face_ids[None])
    last_a = swap(last_a, 0)
    last_b = swap(last_b, 1)
    state_a, state_b, weights, stiff_rows, snap_near, gram_near = pl.pallas_call(
        near_kernel,
        out_shape=[
            first_state,
            second_state,
            *rows,
            kept(planes - 2),
            jax.ShapeDtypeStruct((width, 2 * width), jnp.float32),
        ],
        in_specs=[smem] + [vmem] * 6,
        out_specs=[vmem] * 6,
        scratch_shapes=[kappa, both],
        input_output_aliases={5: 0, 6: 1},
        compiler_params=params,
    )(flags, near_a, near_b, own_kappa, pad_rows, held(state_a), held(state_b))
    state_a, state_b = pl.pallas_call(
        far_kernel,
        out_shape=[first_state, second_state],
        in_specs=[smem] + [vmem] * 6,
        out_specs=[vmem] * 2,
        input_output_aliases={5: 0, 6: 1},
        compiler_params=params,
    )(flags, far_a, far_b, weights, pad_rows, held(state_a), held(state_b))
    _, _, snap_far, gram = pl.pallas_call(
        last_kernel,
        out_shape=[
            first_state,
            second_state,
            kept(2),
            jax.ShapeDtypeStruct((width + 8, width), jnp.float32),
        ],
        in_specs=[smem] + [vmem] * 8,
        out_specs=[vmem] * 4,
        scratch_shapes=[both],
        input_output_aliases={7: 0, 8: 1},
        compiler_params=params,
    )(
        flags,
        last_a,
        last_b,
        weights,
        stiff_rows,
        pad_rows,
        gram_near,
        held(state_a),
        held(state_b),
    )
    return snap_near, snap_far, gram


def lane_copy(tile, lane):
    return jnp.broadcast_to(tile[:, lane : lane + 1], (8, 128))


def row_copy(tile, row):
    return jnp.broadcast_to(tile[row : row + 1, :], (8, tile.shape[1]))


def solve_spd(left, right):
    size = left.shape[0]
    count = size // 8
    sub = lax.broadcasted_iota(jnp.int32, (8, 128), 0)
    lhs = [left[8 * t : 8 * t + 8] for t in range(count)]
    rhs = [right[8 * t : 8 * t + 8] for t in range(count)]
    for k in range(count):
        cols = [lane_copy(lhs[k], 8 * k + j) for j in range(8)]
        panel_l, panel_r = lhs[k], rhs[k]
        for j in range(8):
            recip = pl.reciprocal(row_copy(cols[j], j), approx=True)
            here = sub == j
            mult = jnp.where(here, recip, -cols[j] * recip)
            for l in range(j + 1, 8):
                cols[l] = jnp.where(here, 0.0, cols[l]) + mult * row_copy(cols[l], j)
            panel_l = jnp.where(here, 0.0, panel_l) + mult * row_copy(panel_l, j)
            panel_r = jnp.where(here, 0.0, panel_r) + mult * row_copy(panel_r, j)
        rows_l = [row_copy(panel_l, j) for j in range(8)]
        rows_r = [row_copy(panel_r, j) for j in range(8)]
        order = list(range(k + 1, count)) + list(range(k))
        for t in order:
            tile_cols = [lane_copy(lhs[t], 8 * k + j) for j in range(8)]
            if k + 1 < count:
                lhs[t] = lhs[t] - tree([tile_cols[j] * rows_l[j] for j in range(8)])
            rhs[t] = rhs[t] - tree([tile_cols[j] * rows_r[j] for j in range(8)])
        lhs[k], rhs[k] = panel_l, panel_r
    return jnp.concatenate(rhs, axis=0)


def tree(terms):
    while len(terms) > 1:
        terms = [a + b for a, b in zip(terms[::2], terms[1::2])] + terms[len(terms) & ~1 :]
    return terms[0]


def whiten(inner, block):
    size = inner.shape[0]
    count = size // 8
    sub = lax.broadcasted_iota(jnp.int32, (8, 128), 0)
    lhs = [inner[8 * t : 8 * t + 8] for t in range(count)]
    rhs = [block[8 * t : 8 * t + 8] for t in range(count)]
    done = []
    for k in range(count):
        live = range(k, count)
        cols = {t: [lane_copy(lhs[t], 8 * k + j) for j in range(8)] for t in live}
        scale = None
        for j in range(8):
            pivot = row_copy(cols[k][j], j)
            recip = pl.reciprocal(pivot, approx=True)
            root = lax.rsqrt(pivot)
            scale = root if scale is None else jnp.where(sub >= j, root, scale)
            head = {l: row_copy(cols[k][l], j) for l in range(j + 1, 8)}
            row_l, row_r = row_copy(lhs[k], j), row_copy(rhs[k], j)
            for t in live:
                mult = cols[t][j] * recip
                if t == k:
                    mult = jnp.where(sub > j, mult, 0.0)
                for l in range(j + 1, 8):
                    cols[t][l] = cols[t][l] - mult * head[l]
                lhs[t] = lhs[t] - mult[:, : row_l.shape[1]] * row_l
                rhs[t] = rhs[t] - mult * row_r
        done.append(rhs[k] * scale)
    return jnp.concatenate(done, axis=0)


def pieces_of(value):
    high = value.astype(jnp.bfloat16)
    return high, (value - high.astype(jnp.float32)).astype(jnp.bfloat16)


def dot_rows(left, right):
    left_high, left_low = pieces_of(left)
    right_high, right_low = pieces_of(right)
    return lax.dot_general(
        jnp.concatenate([left_high, left_high, left_low], axis=1),
        jnp.concatenate([right_high, right_low, right_high], axis=1),
        (((1,), (1,)), ((), ())),
        preferred_element_type=jnp.float32,
    )


def modes_kernel(cell_count, rows_z, *refs):
    mask_ref, *part_refs, start_ref, near_hbm, far_hbm, out_ref, snap_ref, sems = refs
    planes, _, columns = snap_ref.shape
    places = [(far_hbm, 0, 0, 1), (near_hbm, 0, 1, planes - 2), (far_hbm, 1, planes - 1, 1)]
    fetches = [
        pltpu.make_async_copy(src.at[pl.ds(at, n)], snap_ref.at[pl.ds(to, n)], sems.at[k])
        for k, (src, at, to, n) in enumerate(places)
    ]
    for fetch in fetches:
        fetch.start()
    total = part_refs[0][...]
    for part in part_refs[1:]:
        total = total + part[...]
    width = total.shape[1]
    row = lax.broadcasted_iota(jnp.int32, (width, width), 0)
    col = lax.broadcasted_iota(jnp.int32, (width, width), 1)
    packed = total[:width]
    turned = packed.T
    mass = jnp.where(row <= col, packed, turned) * (1.0 / cell_count)
    stiff = jnp.where(row > col, packed, jnp.where(row < col, turned, total[width : width + 1]))
    stiff = stiff * (0.5 / cell_count)
    step = solve_spd(stiff, mass)
    turned_step = step.T
    form = dot_rows(turned_step, dot_rows(turned_step, mass))
    both = jnp.concatenate([form, step], axis=0)
    block = start_ref[...]
    for _ in range(ITERS):
        products = dot_rows(block, both)
        inner = dot_rows(products[:, :width], block)
        block = whiten(inner, products[:, width:])
    modes = block.astype(jnp.bfloat16)
    for fetch in fetches:
        fetch.wait()
    lanes = LANES
    rows_y = columns // lanes
    piece_rows = planes * rows_y // out_ref.shape[0]
    for p in range(planes):
        basis = jnp.dot(modes, snap_ref[p], preferred_element_type=jnp.float32)
        for y in range(rows_y):
            piece, spot = divmod(p * rows_y + y, piece_rows)
            values = basis[:, y * lanes : y * lanes + rows_z].astype(jnp.bfloat16)
            wanted = mask_ref[piece] != 0
            out_ref[piece, :, pl.ds(spot * rows_z, rows_z)] = jnp.where(wanted, values, 0.0)


def on_device(snap_init, channel_map, yface_vals, zface_vals, face_of, start_block, correlation):
    subs = lax.axis_size("sub")
    owner_count = lax.axis_size("nbhd")
    planes, rows_y, rows_z, width = snap_init.shape[1:]
    snap_near, snap_far, own = relax(
        snap_init[0], channel_map[0], yface_vals[0], zface_vals[0], face_of[0]
    )
    parts = [own] + [
        lax.ppermute(own, "sub", [(i, (i + shift) % subs) for i in range(subs)])
        for shift in range(1, subs)
    ]
    cells = planes * rows_y * rows_z
    modes = start_block.shape[-1]
    mask = lax.dynamic_slice_in_dim(correlation, lax.axis_index("nbhd"), 1, axis=0)[0]
    pieces = pl.pallas_call(
        functools.partial(modes_kernel, float(subs * cells), rows_z),
        out_shape=jax.ShapeDtypeStruct((owner_count, modes, cells // owner_count), jnp.bfloat16),
        in_specs=[pl.BlockSpec(memory_space=pltpu.SMEM)]
        + [pl.BlockSpec(memory_space=pltpu.VMEM)] * (subs + 1)
        + [pl.BlockSpec(memory_space=pltpu.HBM)] * 2,
        scratch_shapes=[
            pltpu.VMEM((planes, width, rows_y * LANES), jnp.bfloat16),
            pltpu.SemaphoreType.DMA((3,)),
        ],
        compiler_params=pltpu.CompilerParams(vmem_limit_bytes=24 * 2**20),
    )(mask, *parts, start_block[0].T, snap_near, snap_far)
    received = lax.all_to_all(pieces, "nbhd", split_axis=0, concat_axis=0, tiled=True)
    return received[None, None]


def solution(mesh):
    return jax.shard_map(
        on_device,
        mesh=mesh,
        in_specs=(
            P("nbhd", "sub", None, None, None),
            P("nbhd", "sub", None, None),
            P("nbhd", None, None),
            P("nbhd", None, None),
            P("nbhd", None),
            P("nbhd", None, None),
            P(),
        ),
        out_specs=P("nbhd", "sub", None, None, None),
        check_vma=False,
    )
```

```python
import functools

import jax
import jax.numpy as jnp
from jax import lax
from jax.experimental import pallas as pl
from jax.experimental.pallas import tpu as pltpu
from jax.sharding import PartitionSpec as P

SWEEPS = 3
ITERS = 4


def harmonic(left_k, right_k):
    return 2.0 * left_k * right_k / (left_k + right_k)


LANES = 128


def weight_rows(kappa_ref, weights, stiff_rows, lines, first, last, rows_y, rows_z):
    total = kappa_ref.shape[0]
    depth = (total - lines) // 2
    kappa = kappa_ref[...]
    shape = kappa.shape
    line = lax.broadcasted_iota(jnp.int32, shape, 0)
    row_z = lax.broadcasted_iota(jnp.int32, shape, 1)
    row_y = lax.rem(line, rows_y)

    def face(other, edge):
        return jnp.where(edge, kappa, harmonic(kappa, other))

    top = depth + lines
    faces = [
        face(pltpu.roll(kappa, rows_y, 0), (line >= depth) & (line < depth + rows_y * first)),
        face(pltpu.roll(kappa, total - rows_y, 0), (line >= top - rows_y * last) & (line < top)),
        face(pltpu.roll(kappa, 1, 0), row_y == 0),
        face(pltpu.roll(kappa, total - 1, 0), row_y == rows_y - 1),
        face(pltpu.roll(kappa, 1, 1), row_z == 0),
        face(pltpu.roll(kappa, LANES - 1, 1), row_z == rows_z - 1),
    ]
    denom = faces[0] + faces[1] + faces[2] + faces[3] + faces[4] + faces[5]
    outside = (line < depth * first) | (line >= total - depth * last) | (row_z >= rows_z)
    scale = jnp.where(outside, 0.0, 1.0 / denom)
    for k in range(6):
        weights[k] = faces[k] * scale
    upper = row_y >= rows_y // 2
    plane = lax.div(line - depth, rows_y)
    planes = lines // rows_y
    low_cross = jnp.where(upper, 2.0 - 2.0 * first.astype(jnp.float32), 0.0)
    high_cross = jnp.where(upper, 0.0, 2.0 - 2.0 * last.astype(jnp.float32))
    shares = [
        jnp.where(plane == 0, low_cross, jnp.where(plane == 1, 0.0, 1.0)),
        jnp.where(plane == planes - 1, high_cross, jnp.where(plane == planes - 2, 0.0, 1.0)),
        jnp.where(row_y == 0, 0.0, 1.0),
        jnp.where(row_y == rows_y - 1, 0.0, 1.0),
        jnp.where(row_z == 0, 0.0, 1.0),
        jnp.where(row_z == rows_z - 1, 0.0, 1.0),
    ]
    shares[0] = jnp.where(plane == planes - 1, 2.0, shares[0])
    shares[1] = jnp.where(plane == 0, 2.0, shares[1])
    rows = [item * share for item, share in zip(faces, shares)] + [denom, kappa * (1.0 / 16.0)]
    inside = (row_z < rows_z)[depth:top]
    for k in range(8):
        stiff_rows[k] = jnp.where(inside, rows[k][depth:top], 0.0)


def turned(lines):
    width = lines.shape[1]
    row = lax.broadcasted_iota(jnp.int32, (width, width), 0)
    col = lax.broadcasted_iota(jnp.int32, (width, width), 1)
    eye = jnp.where(row == col, 1.0, 0.0).astype(jnp.bfloat16)
    return lax.dot_general(eye, lines, (((1,), (1,)), ((), ())), preferred_element_type=jnp.float32)


def place(line, rows_y):
    return lax.div(line, rows_y), lax.rem(line, rows_y)


def fill(state, source, skip, count, first_line, pad_rows):
    rows_y = pad_rows.shape[0]
    group = 16 if count % 16 == 0 else 8

    def body(i, carry):
        waiting = []

        def store(e, y, both):
            state[e, y + 1] = both[:, :LANES]
            state[e, y + 2] = both[:, LANES:]

        for j in range(0, group, 2):
            at = i * group + j
            e, y = place(first_line + at, rows_y)
            lines = [source[skip + at], pad_rows[y], source[skip + at + 1], pad_rows[y + 1]]
            waiting.append((e, y, turned(jnp.concatenate(lines, axis=0))))
            if len(waiting) > 1:
                store(*waiting.pop(0))
        for item in waiting:
            store(*item)
        return carry

    lax.fori_loop(0, count // group, body, 0)


def neighbour_sum(src, e, y, rows, some, middle):
    return (
        rows[0] * src[e - 1, y + 1, some]
        + rows[1] * src[e + 1, y + 1, some]
        + rows[2] * src[e, y, some]
        + rows[3] * src[e, y + 2, some]
        + rows[4] * pltpu.roll(middle, 1, 1)
        + rows[5] * pltpu.roll(middle, LANES - 1, 1)
    )


PART = 64


def relax_lines(src, dst, weights, first_lines, count, rows_y, rows_z, keep):
    width = src.shape[2]
    group = 8
    total = weights.shape[1] // rows_y
    src_skip = (total - src.shape[0]) // 2
    dst_skip = (total - dst.shape[0]) // 2
    valid = lax.broadcasted_iota(jnp.int32, (PART, LANES), 1) < rows_z

    def body(i, carry):
        waiting = []
        for j in range(group * len(first_lines)):
            line = first_lines[j // group] + i * group + j % group
            e, y = place(line, rows_y)
            rows = [weights[k, pl.ds(line, 1)] for k in range(6)]
            for start in range(0, width, PART):
                some = pl.ds(start, PART)
                middle = src[e - src_skip, y + 1, some]
                fresh = neighbour_sum(src, e - src_skip, y, rows, some, middle)
                fresh = fresh.astype(jnp.bfloat16).astype(jnp.float32)
                if keep:
                    fresh = jnp.where(valid, fresh, middle)
                waiting.append((e - dst_skip, y, some, fresh))
                if len(waiting) > 1:
                    e0, y0, some0, value = waiting.pop(0)
                    dst[e0, y0 + 1, some0] = value
        for e0, y0, some0, value in waiting:
            dst[e0, y0 + 1, some0] = value
        return carry

    lax.fori_loop(0, count // group, body, 0)


def gram_terms(final, places, planes, stiff_rows, snap, both, total):
    _, width, columns = snap.shape
    rows_y = columns // LANES
    for item, e in enumerate(places):
        p = e - planes
        e = e - (3 * planes - final.shape[0]) // 2
        waiting = []

        def store(y, some, below, values, item=item):
            spot = pl.ds(y * LANES, LANES)
            snap[item, some, spot] = values[0]
            both[some, spot] = values[1]
            both[below, spot] = values[2]

        for y in range(rows_y):
            rows = [stiff_rows[k, pl.ds(p * rows_y + y, 1)] for k in range(8)]
            for start in range(0, width, PART):
                some = pl.ds(start, PART)
                middle = final[e, y + 1, some]
                numer = neighbour_sum(final, e, y, rows, some, middle)
                values = [middle, rows[7] * middle, rows[6] * middle - numer]
                values = [value.astype(jnp.bfloat16) for value in values]
                waiting.append((y, some, pl.ds(width + start, PART), values))
                if len(waiting) > 1:
                    store(*waiting.pop(0))
        for entry in waiting:
            store(*entry)
        total = total + lax.dot_general(
            snap[item], both[...], (((1,), (1,)), ((), ())), preferred_element_type=jnp.float32
        )
    return total


def powers(marks):
    return jnp.left_shift(jnp.int32(1), 2 * marks).astype(jnp.float32)


def pack_kernel(flags, class_map, lines, near_a, near_b, far_a, far_b, classes, sems):
    count, rows_z = classes.shape
    far = far_a.shape[0]
    near = near_a.shape[0] - 1
    upward = flags[0]
    fetch = pltpu.make_async_copy(class_map, classes, sems.at[4])
    fetch.start()
    copies = []
    for out, skip, size, start in (
        (near_a, 1, near, upward * (count - near)),
        (near_b, 1, near, (1 - upward) * (count - near)),
        (far_a, 0, far, near - upward * far),
        (far_b, 0, far, near - (1 - upward) * far),
    ):
        copies.append(
            pltpu.make_async_copy(
                lines.at[pl.ds(start, size)], out.at[pl.ds(skip, size)], sems.at[len(copies)]
            )
        )
        copies[-1].start()
    fetch.wait()
    marks = classes[...].astype(jnp.float32).astype(jnp.bfloat16)
    width = near_a.shape[2]
    marks = jnp.concatenate([marks, jnp.zeros((count, width - rows_z), jnp.bfloat16)], axis=1)
    for out in (near_a, near_b):
        out[0, pl.ds(0, count)] = marks
        out[0, pl.ds(count, rows_z - count)] = jnp.zeros((rows_z - count, width), jnp.bfloat16)
    for copy in copies:
        copy.wait()


def own_kernel(
    flags,
    own,
    classes,
    y_vals,
    z_vals,
    face_ids,
    hand,
    inner,
    pad_rows,
    last_a,
    last_b,
    own_kappa,
    state_a,
    state_b,
    kappa,
    weights,
    stiff_rows,
    sems,
):
    lines, rows_z, width = own.shape
    rows_y = pad_rows.shape[0]
    planes = lines // rows_y
    bf16 = jnp.bfloat16
    ids = face_ids[...]
    picks = [(ids == side).astype(jnp.float32) for side in range(4)]
    spare = LANES - rows_z
    spot = lax.broadcasted_iota(jnp.int32, (spare, width), 0)
    z_all = z_vals[...].astype(jnp.float32)
    z_low = z_all * picks[2]
    z_high = z_all * picks[3]
    for y in range(rows_y):
        rows = jnp.where(spot == 0, z_high[y : y + 1], 0.0)
        pad_rows[y] = jnp.where(spot == spare - 1, z_low[y : y + 1], rows).astype(bf16)
    y_all = y_vals[...].astype(jnp.float32)
    blank = jnp.zeros((spare, width), bf16)
    ghost_low = turned(jnp.concatenate([(y_all * picks[0]).astype(bf16), blank], axis=0))
    ghost_high = turned(jnp.concatenate([(y_all * picks[1]).astype(bf16), blank], axis=0))

    def edges(e, carry):
        for state, at in ((state_a, e), (state_b, e - 1)):
            state[at, 0] = ghost_low
            state[at, rows_y + 1] = ghost_high
        return carry

    lax.fori_loop(planes, 2 * planes, edges, 0)
    fill(state_a, own, 0, lines, lines, pad_rows)
    sends = [
        pltpu.make_async_copy(state_a.at[pl.ds(planes, planes)], hand, sems.at[0]),
        pltpu.make_async_copy(state_b.at[pl.ds(planes, planes - 2)], inner, sems.at[1]),
    ]
    sends[0].start()
    kappa[...] = jnp.ones(kappa.shape, jnp.float32)
    kappa[pl.ds(lines, lines), pl.ds(0, rows_z)] = powers(classes[...])
    own_kappa[...] = kappa[pl.ds(lines, lines)]
    weight_rows(kappa, weights, stiff_rows, lines, flags[1], flags[2], rows_y, rows_z)
    inside = lines - 2 * rows_y
    relax_lines(state_a, state_b, weights, (lines + rows_y,), inside, rows_y, rows_z, True)
    sends[1].start()
    half = rows_y // 2
    for out, upward in ((last_a, flags[0]), (last_b, 1 - flags[0])):
        out[...] = own[pl.ds(upward * half + (1 - upward) * (lines - rows_y), half)]
    for copy in sends:
        copy.wait()


def near_kernel(
    flags,
    near_a,
    near_b,
    own_kappa,
    pad_rows,
    hand,
    inner,
    state_a,
    state_b,
    weights,
    stiff_rows,
    snap,
    gram,
    kappa,
    both,
    sems,
):
    lines = own_kappa.shape[0]
    rows_z = near_a.shape[1]
    rows_y = pad_rows.shape[0]
    near = lines // 2
    planes = lines // rows_y
    taken = [
        pltpu.make_async_copy(hand, state_a.at[pl.ds(planes, planes)], sems.at[0]),
        pltpu.make_async_copy(inner, state_b.at[pl.ds(planes, planes - 2)], sems.at[1]),
    ]
    for copy in taken:
        copy.start()
    even, first, last = flags[0], flags[1], flags[2]
    base_a = pl.multiple_of(even * (2 * lines), 8)
    base_b = pl.multiple_of((1 - even) * (2 * lines), 8)
    kappa[...] = jnp.ones(kappa.shape, jnp.float32)
    kappa[pl.ds(lines, lines)] = own_kappa[...]
    for base, part in ((base_a, near_a), (base_b, near_b)):
        marks = part[0][:lines].astype(jnp.float32).astype(jnp.int32)
        kappa[pl.ds(base, lines)] = powers(marks)
    weight_rows(kappa, weights, stiff_rows, lines, first, last, rows_y, rows_z)
    fill(state_a, near_a, 1, near, near + even * (lines + near), pad_rows)
    fill(state_a, near_b, 1, near, near + (1 - even) * (lines + near), pad_rows)
    for copy in taken:
        copy.wait()
    ghost_low = state_a[planes, 0]
    ghost_high = state_a[planes, rows_y + 1]
    for e in range(1, 3 * planes - 1):
        if e not in range(planes, 2 * planes):
            state_a[e, 0] = ghost_low
            state_a[e, rows_y + 1] = ghost_high
        if e not in range(planes + 1, 2 * planes - 1):
            state_b[e - 1, 0] = ghost_low
            state_b[e - 1, rows_y + 1] = ghost_high
    step = functools.partial(relax_lines, weights=weights, rows_y=rows_y, rows_z=rows_z)
    ends = (lines - rows_y, 2 * lines - rows_y)
    step(state_a, state_b, first_lines=ends, count=2 * rows_y, keep=True)
    step(state_b, state_a, first_lines=(lines,), count=lines, keep=True)
    inner = (lines + rows_y,)
    step(state_a, state_b, first_lines=inner, count=lines - 2 * rows_y, keep=False)
    inside = range(planes + 1, 2 * planes - 1)
    blank = jnp.zeros(gram.shape, jnp.float32)
    gram[...] = gram_terms(state_b, inside, planes, stiff_rows, snap, both, blank)


def advance(buffers, weights, low_line, count, total, rows_y, rows_z):
    for sweep in range(1, SWEEPS + 1):
        src, dst = buffers[(sweep - 1) % 2], buffers[sweep % 2]
        low = low_line + sweep * rows_y
        ends = (low, total - low - count)
        relax_lines(src, dst, weights, ends, count, rows_y, rows_z, sweep < SWEEPS)


def far_kernel(flags, far_a, far_b, weights, pad_rows, old_a, old_b, state_a, state_b):
    del old_a, old_b
    rows_y = pad_rows.shape[0]
    count, rows_z = far_a.shape[:2]
    total = weights.shape[1]
    even = flags[0]
    shift = even * (total - 2 * rows_y - count)
    fill(state_a, far_a, 0, count, rows_y + shift, pad_rows)
    fill(state_a, far_b, 0, count, total - rows_y - count - shift, pad_rows)
    advance((state_a, state_b), weights, rows_y, count, total, rows_y, rows_z)


def last_kernel(
    flags,
    last_a,
    last_b,
    weights,
    stiff_rows,
    pad_rows,
    near_gram,
    old_a,
    old_b,
    state_a,
    state_b,
    snap,
    gram,
    both,
):
    del old_a, old_b
    width = snap.shape[1]
    rows_y = pad_rows.shape[0]
    count, rows_z = last_a.shape[:2]
    planes = stiff_rows.shape[1] // rows_y
    lines = weights.shape[1]
    shift = flags[0] * (lines - 3 * count)
    fill(state_a, last_a, 0, count, count + shift, pad_rows)
    fill(state_a, last_b, 0, count, lines - 2 * count - shift, pad_rows)
    buffers = (state_a, state_b)
    advance(buffers, weights, count, count, lines, rows_y, rows_z)
    final = buffers[SWEEPS % 2]
    outer = (planes, 2 * planes - 1)
    total = gram_terms(final, outer, planes, stiff_rows, snap, both, near_gram[...])
    mass = total[:, :width]
    stiff = total[:, width:]
    stiff = stiff + stiff.T
    row = lax.broadcasted_iota(jnp.int32, (width, width), 0)
    col = lax.broadcasted_iota(jnp.int32, (width, width), 1)
    gram[pl.ds(0, width)] = jnp.where(row > col, stiff, mass)
    diagonal = jnp.sum(jnp.where(row == col, stiff, 0.0), axis=0, keepdims=True)
    gram[pl.ds(width, 8)] = jnp.broadcast_to(diagonal, (8, width))


def swap(array, start):
    count = lax.axis_size("sub")
    pairs = [(i, i + 1) for i in range(start, count - 1, 2)]
    return lax.ppermute(array, "sub", pairs + [(j, i) for i, j in pairs])


def relax(initial, classes, y_vals, z_vals, face_ids):
    planes, rows_y, rows_z, width = initial.shape
    index = lax.axis_index("sub")
    subs = lax.axis_size("sub")
    even = (index + 1) % 2
    flags = jnp.stack([even, index == 0, index == subs - 1, 0]).astype(jnp.int32)
    lines = initial.reshape(planes * rows_y, rows_z, width)
    count = planes * rows_y
    near, half = 2 * rows_y, rows_y // 2
    flat_classes = classes.reshape(count, rows_z)
    part = functools.partial(jax.ShapeDtypeStruct, dtype=initial.dtype)
    vmem = pl.BlockSpec(memory_space=pltpu.VMEM)
    smem = pl.BlockSpec(memory_space=pltpu.SMEM)
    hbm = pl.BlockSpec(memory_space=pltpu.HBM)
    first_state = pltpu.VMEM((3 * planes, rows_y + 2, width, LANES), jnp.float32)
    second_state = pltpu.VMEM((3 * planes - 2, rows_y + 2, width, LANES), jnp.float32)
    kappa = pltpu.VMEM((3 * count, LANES), jnp.float32)
    both = pltpu.VMEM((2 * width, rows_y * LANES), jnp.bfloat16)
    params = pltpu.CompilerParams(vmem_limit_bytes=8 * 2**20)

    def kept(depth):
        return jax.ShapeDtypeStruct((depth, width, rows_y * LANES), jnp.bfloat16)

    def in_hbm(item):
        return pltpu.with_memory_space_constraint(item, pltpu.HBM)

    def held(item):
        return pltpu.with_memory_space_constraint(item, pltpu.VMEM)

    rows = [
        jax.ShapeDtypeStruct((6, 3 * count, LANES), jnp.float32),
        jax.ShapeDtypeStruct((8, count, LANES), jnp.float32),
    ]
    near_a, near_b, far_a, far_b = pl.pallas_call(
        pack_kernel,
        out_shape=[part((near + 1, rows_z, width))] * 2 + [part((rows_y, rows_z, width))] * 2,
        in_specs=[smem] + [hbm] * 2,
        out_specs=[vmem] * 4,
        scratch_shapes=[
            pltpu.VMEM((count, rows_z), jnp.int32),
            pltpu.SemaphoreType.DMA((5,)),
        ],
        compiler_params=params,
    )(flags, in_hbm(flat_classes), in_hbm(lines))
    near_a = swap(near_a, 0)
    near_b = swap(near_b, 1)
    far_a = swap(far_a, 0)
    far_b = swap(far_b, 1)
    hand, inner, pad_rows, last_a, last_b, own_kappa = pl.pallas_call(
        own_kernel,
        out_shape=[
            pltpu.HBM((planes,) + first_state.shape[1:], jnp.float32),
            pltpu.HBM((planes - 2,) + first_state.shape[1:], jnp.float32),
            part((rows_y, LANES - rows_z, width)),
            part((half, rows_z, width)),
            part((half, rows_z, width)),
            jax.ShapeDtypeStruct((count, LANES), jnp.float32),
        ],
        in_specs=[smem] + [vmem] * 5,
        out_specs=[hbm] * 2 + [vmem] * 4,
        scratch_shapes=[first_state, second_state, kappa]
        + [pltpu.VMEM(item.shape, item.dtype) for item in rows]
        + [pltpu.SemaphoreType.DMA((2,))],
        compiler_params=pltpu.CompilerParams(vmem_limit_bytes=40 * 2**20),
    )(flags, lines, flat_classes, y_vals, z_vals, face_ids[None])
    last_a = swap(last_a, 0)
    last_b = swap(last_b, 1)
    state_a, state_b, weights, stiff_rows, snap_near, gram_near = pl.pallas_call(
        near_kernel,
        out_shape=[
            first_state,
            second_state,
            *rows,
            kept(planes - 2),
            jax.ShapeDtypeStruct((width, 2 * width), jnp.float32),
        ],
        in_specs=[smem] + [vmem] * 4 + [hbm] * 2,
        out_specs=[vmem] * 6,
        scratch_shapes=[kappa, both, pltpu.SemaphoreType.DMA((2,))],
        compiler_params=params,
    )(flags, near_a, near_b, own_kappa, pad_rows, in_hbm(hand), in_hbm(inner))
    state_a, state_b = pl.pallas_call(
        far_kernel,
        out_shape=[first_state, second_state],
        in_specs=[smem] + [vmem] * 6,
        out_specs=[vmem] * 2,
        input_output_aliases={5: 0, 6: 1},
        compiler_params=params,
    )(flags, far_a, far_b, weights, pad_rows, held(state_a), held(state_b))
    _, _, snap_far, gram = pl.pallas_call(
        last_kernel,
        out_shape=[
            first_state,
            second_state,
            kept(2),
            jax.ShapeDtypeStruct((width + 8, width), jnp.float32),
        ],
        in_specs=[smem] + [vmem] * 8,
        out_specs=[vmem] * 4,
        scratch_shapes=[both],
        input_output_aliases={7: 0, 8: 1},
        compiler_params=params,
    )(
        flags,
        last_a,
        last_b,
        weights,
        stiff_rows,
        pad_rows,
        gram_near,
        held(state_a),
        held(state_b),
    )
    return snap_near, snap_far, gram


def lane_copy(tile, lane):
    return jnp.broadcast_to(tile[:, lane : lane + 1], (8, 128))


def row_copy(tile, row):
    return jnp.broadcast_to(tile[row : row + 1, :], (8, tile.shape[1]))


def solve_spd(left, right):
    size = left.shape[0]
    count = size // 8
    sub = lax.broadcasted_iota(jnp.int32, (8, 128), 0)
    lhs = [left[8 * t : 8 * t + 8] for t in range(count)]
    rhs = [right[8 * t : 8 * t + 8] for t in range(count)]
    for k in range(count):
        cols = [lane_copy(lhs[k], 8 * k + j) for j in range(8)]
        panel_l, panel_r = lhs[k], rhs[k]
        for j in range(8):
            recip = pl.reciprocal(row_copy(cols[j], j), approx=True)
            here = sub == j
            mult = jnp.where(here, recip, -cols[j] * recip)
            for l in range(j + 1, 8):
                cols[l] = jnp.where(here, 0.0, cols[l]) + mult * row_copy(cols[l], j)
            panel_l = jnp.where(here, 0.0, panel_l) + mult * row_copy(panel_l, j)
            panel_r = jnp.where(here, 0.0, panel_r) + mult * row_copy(panel_r, j)
        rows_l = [row_copy(panel_l, j) for j in range(8)]
        rows_r = [row_copy(panel_r, j) for j in range(8)]
        order = list(range(k + 1, count)) + list(range(k))
        for t in order:
            tile_cols = [lane_copy(lhs[t], 8 * k + j) for j in range(8)]
            if k + 1 < count:
                lhs[t] = lhs[t] - tree([tile_cols[j] * rows_l[j] for j in range(8)])
            rhs[t] = rhs[t] - tree([tile_cols[j] * rows_r[j] for j in range(8)])
        lhs[k], rhs[k] = panel_l, panel_r
    return jnp.concatenate(rhs, axis=0)


def tree(terms):
    while len(terms) > 1:
        terms = [a + b for a, b in zip(terms[::2], terms[1::2])] + terms[len(terms) & ~1 :]
    return terms[0]


def whiten(inner, block):
    size = inner.shape[0]
    count = size // 8
    sub = lax.broadcasted_iota(jnp.int32, (8, 128), 0)
    lhs = [inner[8 * t : 8 * t + 8] for t in range(count)]
    rhs = [block[8 * t : 8 * t + 8] for t in range(count)]
    done = []
    for k in range(count):
        live = range(k, count)
        cols = {t: [lane_copy(lhs[t], 8 * k + j) for j in range(8)] for t in live}
        scale = None
        for j in range(8):
            pivot = row_copy(cols[k][j], j)
            recip = pl.reciprocal(pivot, approx=True)
            root = lax.rsqrt(pivot)
            scale = root if scale is None else jnp.where(sub >= j, root, scale)
            head = {l: row_copy(cols[k][l], j) for l in range(j + 1, 8)}
            row_l, row_r = row_copy(lhs[k], j), row_copy(rhs[k], j)
            for t in live:
                mult = cols[t][j] * recip
                if t == k:
                    mult = jnp.where(sub > j, mult, 0.0)
                for l in range(j + 1, 8):
                    cols[t][l] = cols[t][l] - mult * head[l]
                lhs[t] = lhs[t] - mult[:, : row_l.shape[1]] * row_l
                rhs[t] = rhs[t] - mult * row_r
        done.append(rhs[k] * scale)
    return jnp.concatenate(done, axis=0)


def pieces_of(value):
    high = value.astype(jnp.bfloat16)
    return high, (value - high.astype(jnp.float32)).astype(jnp.bfloat16)


def dot_rows(left, right):
    left_high, left_low = pieces_of(left)
    right_high, right_low = pieces_of(right)
    return lax.dot_general(
        jnp.concatenate([left_high, left_high, left_low], axis=1),
        jnp.concatenate([right_high, right_low, right_high], axis=1),
        (((1,), (1,)), ((), ())),
        preferred_element_type=jnp.float32,
    )


def modes_kernel(cell_count, rows_z, *refs):
    mask_ref, *part_refs, start_ref, near_hbm, far_hbm, out_ref, snap_ref, sems = refs
    planes, _, columns = snap_ref.shape
    places = [(far_hbm, 0, 0, 1), (near_hbm, 0, 1, planes - 2), (far_hbm, 1, planes - 1, 1)]
    fetches = [
        pltpu.make_async_copy(src.at[pl.ds(at, n)], snap_ref.at[pl.ds(to, n)], sems.at[k])
        for k, (src, at, to, n) in enumerate(places)
    ]
    for fetch in fetches:
        fetch.start()
    total = part_refs[0][...]
    for part in part_refs[1:]:
        total = total + part[...]
    width = total.shape[1]
    row = lax.broadcasted_iota(jnp.int32, (width, width), 0)
    col = lax.broadcasted_iota(jnp.int32, (width, width), 1)
    packed = total[:width]
    turned = packed.T
    mass = jnp.where(row <= col, packed, turned) * (1.0 / cell_count)
    stiff = jnp.where(row > col, packed, jnp.where(row < col, turned, total[width : width + 1]))
    stiff = stiff * (0.5 / cell_count)
    step = solve_spd(stiff, mass)
    turned_step = step.T
    form = dot_rows(turned_step, dot_rows(turned_step, mass))
    both = jnp.concatenate([form, step], axis=0)
    block = start_ref[...]
    for _ in range(ITERS):
        products = dot_rows(block, both)
        inner = dot_rows(products[:, :width], block)
        block = whiten(inner, products[:, width:])
    modes = block.astype(jnp.bfloat16)
    for fetch in fetches:
        fetch.wait()
    lanes = LANES
    rows_y = columns // lanes
    piece_rows = planes * rows_y // out_ref.shape[0]
    for p in range(planes):
        basis = jnp.dot(modes, snap_ref[p], preferred_element_type=jnp.float32)
        for y in range(rows_y):
            piece, spot = divmod(p * rows_y + y, piece_rows)
            values = basis[:, y * lanes : y * lanes + rows_z].astype(jnp.bfloat16)
            wanted = mask_ref[piece] != 0
            out_ref[piece, :, pl.ds(spot * rows_z, rows_z)] = jnp.where(wanted, values, 0.0)


def on_device(snap_init, channel_map, yface_vals, zface_vals, face_of, start_block, correlation):
    subs = lax.axis_size("sub")
    owner_count = lax.axis_size("nbhd")
    planes, rows_y, rows_z, width = snap_init.shape[1:]
    snap_near, snap_far, own = relax(
        snap_init[0], channel_map[0], yface_vals[0], zface_vals[0], face_of[0]
    )
    parts = [own] + [
        lax.ppermute(own, "sub", [(i, (i + shift) % subs) for i in range(subs)])
        for shift in range(1, subs)
    ]
    cells = planes * rows_y * rows_z
    modes = start_block.shape[-1]
    mask = lax.dynamic_slice_in_dim(correlation, lax.axis_index("nbhd"), 1, axis=0)[0]
    pieces = pl.pallas_call(
        functools.partial(modes_kernel, float(subs * cells), rows_z),
        out_shape=jax.ShapeDtypeStruct((owner_count, modes, cells // owner_count), jnp.bfloat16),
        in_specs=[pl.BlockSpec(memory_space=pltpu.SMEM)]
        + [pl.BlockSpec(memory_space=pltpu.VMEM)] * (subs + 1)
        + [pl.BlockSpec(memory_space=pltpu.HBM)] * 2,
        scratch_shapes=[
            pltpu.VMEM((planes, width, rows_y * LANES), jnp.bfloat16),
            pltpu.SemaphoreType.DMA((3,)),
        ],
        compiler_params=pltpu.CompilerParams(vmem_limit_bytes=24 * 2**20),
    )(mask, *parts, start_block[0].T, snap_near, snap_far)
    received = lax.all_to_all(pieces, "nbhd", split_axis=0, concat_axis=0, tiled=True)
    return received[None, None]


def solution(mesh):
    return jax.shard_map(
        on_device,
        mesh=mesh,
        in_specs=(
            P("nbhd", "sub", None, None, None),
            P("nbhd", "sub", None, None),
            P("nbhd", None, None),
            P("nbhd", None, None),
            P("nbhd", None),
            P("nbhd", None, None),
            P(),
        ),
        out_specs=P("nbhd", "sub", None, None, None),
        check_vma=False,
    )
```

```python
import functools

import jax
import jax.numpy as jnp
from jax import lax
from jax.experimental import pallas as pl
from jax.experimental.pallas import tpu as pltpu
from jax.sharding import PartitionSpec as P

SWEEPS = 3
ITERS = 4


def harmonic(left_k, right_k):
    return 2.0 * left_k * right_k / (left_k + right_k)


LANES = 128


def weight_rows(kappa_ref, weights, stiff_rows, lines, first, last, rows_y, rows_z):
    total = kappa_ref.shape[0]
    depth = (total - lines) // 2
    kappa = kappa_ref[...]
    shape = kappa.shape
    line = lax.broadcasted_iota(jnp.int32, shape, 0)
    row_z = lax.broadcasted_iota(jnp.int32, shape, 1)
    row_y = lax.rem(line, rows_y)

    def face(other, edge):
        return jnp.where(edge, kappa, harmonic(kappa, other))

    top = depth + lines
    faces = [
        face(pltpu.roll(kappa, rows_y, 0), (line >= depth) & (line < depth + rows_y * first)),
        face(pltpu.roll(kappa, total - rows_y, 0), (line >= top - rows_y * last) & (line < top)),
        face(pltpu.roll(kappa, 1, 0), row_y == 0),
        face(pltpu.roll(kappa, total - 1, 0), row_y == rows_y - 1),
        face(pltpu.roll(kappa, 1, 1), row_z == 0),
        face(pltpu.roll(kappa, LANES - 1, 1), row_z == rows_z - 1),
    ]
    denom = faces[0] + faces[1] + faces[2] + faces[3] + faces[4] + faces[5]
    outside = (line < depth * first) | (line >= total - depth * last) | (row_z >= rows_z)
    scale = jnp.where(outside, 0.0, 1.0 / denom)
    for k in range(6):
        weights[k] = faces[k] * scale
    upper = row_y >= rows_y // 2
    plane = lax.div(line - depth, rows_y)
    planes = lines // rows_y
    low_cross = jnp.where(upper, 2.0 - 2.0 * first.astype(jnp.float32), 0.0)
    high_cross = jnp.where(upper, 0.0, 2.0 - 2.0 * last.astype(jnp.float32))
    shares = [
        jnp.where(plane == 0, low_cross, jnp.where(plane == 1, 0.0, 1.0)),
        jnp.where(plane == planes - 1, high_cross, jnp.where(plane == planes - 2, 0.0, 1.0)),
        jnp.where(row_y == 0, 0.0, 1.0),
        jnp.where(row_y == rows_y - 1, 0.0, 1.0),
        jnp.where(row_z == 0, 0.0, 1.0),
        jnp.where(row_z == rows_z - 1, 0.0, 1.0),
    ]
    shares[0] = jnp.where(plane == planes - 1, 2.0, shares[0])
    shares[1] = jnp.where(plane == 0, 2.0, shares[1])
    rows = [item * share for item, share in zip(faces, shares)] + [denom, kappa * (1.0 / 16.0)]
    inside = (row_z < rows_z)[depth:top]
    for k in range(8):
        stiff_rows[k] = jnp.where(inside, rows[k][depth:top], 0.0)


def turned(lines):
    width = lines.shape[1]
    row = lax.broadcasted_iota(jnp.int32, (width, width), 0)
    col = lax.broadcasted_iota(jnp.int32, (width, width), 1)
    eye = jnp.where(row == col, 1.0, 0.0).astype(jnp.bfloat16)
    return lax.dot_general(eye, lines, (((1,), (1,)), ((), ())), preferred_element_type=jnp.float32)


def place(line, rows_y):
    return lax.div(line, rows_y), lax.rem(line, rows_y)


def fill(state, source, skip, count, first_line, pad_rows):
    rows_y = pad_rows.shape[0]
    group = 16 if count % 16 == 0 else 8

    def body(i, carry):
        waiting = []

        def store(e, y, both):
            state[e, y + 1] = both[:, :LANES]
            state[e, y + 2] = both[:, LANES:]

        for j in range(0, group, 2):
            at = i * group + j
            e, y = place(first_line + at, rows_y)
            lines = [source[skip + at], pad_rows[y], source[skip + at + 1], pad_rows[y + 1]]
            waiting.append((e, y, turned(jnp.concatenate(lines, axis=0))))
            if len(waiting) > 1:
                store(*waiting.pop(0))
        for item in waiting:
            store(*item)
        return carry

    lax.fori_loop(0, count // group, body, 0)


def neighbour_sum(src, e, y, rows, some, middle):
    return (
        rows[0] * src[e - 1, y + 1, some]
        + rows[1] * src[e + 1, y + 1, some]
        + rows[2] * src[e, y, some]
        + rows[3] * src[e, y + 2, some]
        + rows[4] * pltpu.roll(middle, 1, 1)
        + rows[5] * pltpu.roll(middle, LANES - 1, 1)
    )


PART = 64


def relax_lines(src, dst, weights, first_lines, count, rows_y, rows_z, keep):
    width = src.shape[2]
    group = 8
    total = weights.shape[1] // rows_y
    src_skip = (total - src.shape[0]) // 2
    dst_skip = (total - dst.shape[0]) // 2
    valid = lax.broadcasted_iota(jnp.int32, (PART, LANES), 1) < rows_z

    def body(i, carry):
        waiting = []
        for j in range(group * len(first_lines)):
            line = first_lines[j // group] + i * group + j % group
            e, y = place(line, rows_y)
            rows = [weights[k, pl.ds(line, 1)] for k in range(6)]
            for start in range(0, width, PART):
                some = pl.ds(start, PART)
                middle = src[e - src_skip, y + 1, some]
                fresh = neighbour_sum(src, e - src_skip, y, rows, some, middle)
                fresh = fresh.astype(jnp.bfloat16).astype(jnp.float32)
                if keep:
                    fresh = jnp.where(valid, fresh, middle)
                waiting.append((e - dst_skip, y, some, fresh))
                if len(waiting) > 1:
                    e0, y0, some0, value = waiting.pop(0)
                    dst[e0, y0 + 1, some0] = value
        for e0, y0, some0, value in waiting:
            dst[e0, y0 + 1, some0] = value
        return carry

    lax.fori_loop(0, count // group, body, 0)


def gram_terms(final, places, planes, stiff_rows, snap, both, total):
    _, width, columns = snap.shape
    rows_y = columns // LANES
    for item, e in enumerate(places):
        p = e - planes
        e = e - (3 * planes - final.shape[0]) // 2
        waiting = []

        def store(y, some, below, values, item=item):
            spot = pl.ds(y * LANES, LANES)
            snap[item, some, spot] = values[0]
            both[some, spot] = values[1]
            both[below, spot] = values[2]

        for y in range(rows_y):
            rows = [stiff_rows[k, pl.ds(p * rows_y + y, 1)] for k in range(8)]
            for start in range(0, width, PART):
                some = pl.ds(start, PART)
                middle = final[e, y + 1, some]
                numer = neighbour_sum(final, e, y, rows, some, middle)
                values = [middle, rows[7] * middle, rows[6] * middle - numer]
                values = [value.astype(jnp.bfloat16) for value in values]
                waiting.append((y, some, pl.ds(width + start, PART), values))
                if len(waiting) > 1:
                    store(*waiting.pop(0))
        for entry in waiting:
            store(*entry)
        total = total + lax.dot_general(
            snap[item], both[...], (((1,), (1,)), ((), ())), preferred_element_type=jnp.float32
        )
    return total


def powers(marks):
    return jnp.left_shift(jnp.int32(1), 2 * marks).astype(jnp.float32)


def pack_kernel(flags, class_map, lines, near_a, near_b, classes, sems):
    count, rows_z = classes.shape
    near = near_a.shape[0] - 1
    upward = flags[0]
    fetch = pltpu.make_async_copy(class_map, classes, sems.at[2])
    fetch.start()
    copies = []
    for out, start in (
        (near_a, upward * (count - near)),
        (near_b, (1 - upward) * (count - near)),
    ):
        copies.append(
            pltpu.make_async_copy(
                lines.at[pl.ds(start, near)], out.at[pl.ds(1, near)], sems.at[len(copies)]
            )
        )
        copies[-1].start()
    fetch.wait()
    marks = classes[...].astype(jnp.float32).astype(jnp.bfloat16)
    width = near_a.shape[2]
    marks = jnp.concatenate([marks, jnp.zeros((count, width - rows_z), jnp.bfloat16)], axis=1)
    for out in (near_a, near_b):
        out[0, pl.ds(0, count)] = marks
        out[0, pl.ds(count, rows_z - count)] = jnp.zeros((rows_z - count, width), jnp.bfloat16)
    for copy in copies:
        copy.wait()


def own_kernel(
    flags,
    own,
    classes,
    y_vals,
    z_vals,
    face_ids,
    hand,
    inner,
    pad_rows,
    far_a,
    far_b,
    own_kappa,
    state_a,
    state_b,
    kappa,
    weights,
    stiff_rows,
    sems,
):
    lines, rows_z, width = own.shape
    rows_y = pad_rows.shape[0]
    planes = lines // rows_y
    bf16 = jnp.bfloat16
    ids = face_ids[...]
    picks = [(ids == side).astype(jnp.float32) for side in range(4)]
    spare = LANES - rows_z
    spot = lax.broadcasted_iota(jnp.int32, (spare, width), 0)
    z_all = z_vals[...].astype(jnp.float32)
    z_low = z_all * picks[2]
    z_high = z_all * picks[3]
    for y in range(rows_y):
        rows = jnp.where(spot == 0, z_high[y : y + 1], 0.0)
        pad_rows[y] = jnp.where(spot == spare - 1, z_low[y : y + 1], rows).astype(bf16)
    y_all = y_vals[...].astype(jnp.float32)
    blank = jnp.zeros((spare, width), bf16)
    ghost_low = turned(jnp.concatenate([(y_all * picks[0]).astype(bf16), blank], axis=0))
    ghost_high = turned(jnp.concatenate([(y_all * picks[1]).astype(bf16), blank], axis=0))

    def edges(e, carry):
        for state, at in ((state_a, e), (state_b, e - 1)):
            state[at, 0] = ghost_low
            state[at, rows_y + 1] = ghost_high
        return carry

    lax.fori_loop(planes, 2 * planes, edges, 0)
    fill(state_a, own, 0, lines, lines, pad_rows)
    sends = [
        pltpu.make_async_copy(state_a.at[pl.ds(planes, planes)], hand, sems.at[0]),
        pltpu.make_async_copy(state_b.at[pl.ds(planes, planes - 2)], inner, sems.at[1]),
    ]
    sends[0].start()
    kappa[...] = jnp.ones(kappa.shape, jnp.float32)
    kappa[pl.ds(lines, lines), pl.ds(0, rows_z)] = powers(classes[...])
    own_kappa[...] = kappa[pl.ds(lines, lines)]
    weight_rows(kappa, weights, stiff_rows, lines, flags[1], flags[2], rows_y, rows_z)
    inside = lines - 2 * rows_y
    relax_lines(state_a, state_b, weights, (lines + rows_y,), inside, rows_y, rows_z, True)
    sends[1].start()
    half = rows_y // 2
    far = far_a.shape[0]
    for out, upward in ((far_a, flags[0]), (far_b, 1 - flags[0])):
        out[...] = own[pl.ds(upward * half + (1 - upward) * (lines - half - far), far)]
    for copy in sends:
        copy.wait()


def near_kernel(
    flags,
    near_a,
    near_b,
    own_kappa,
    pad_rows,
    hand,
    inner,
    state_a,
    state_b,
    weights,
    stiff_rows,
    snap,
    gram,
    kappa,
    both,
    sems,
):
    lines = own_kappa.shape[0]
    rows_z = near_a.shape[1]
    rows_y = pad_rows.shape[0]
    near = lines // 2
    planes = lines // rows_y
    taken = [
        pltpu.make_async_copy(hand, state_a.at[pl.ds(planes, planes)], sems.at[0]),
        pltpu.make_async_copy(inner, state_b.at[pl.ds(planes, planes - 2)], sems.at[1]),
    ]
    for copy in taken:
        copy.start()
    even, first, last = flags[0], flags[1], flags[2]
    base_a = pl.multiple_of(even * (2 * lines), 8)
    base_b = pl.multiple_of((1 - even) * (2 * lines), 8)
    kappa[...] = jnp.ones(kappa.shape, jnp.float32)
    kappa[pl.ds(lines, lines)] = own_kappa[...]
    for base, part in ((base_a, near_a), (base_b, near_b)):
        marks = part[0][:lines].astype(jnp.float32).astype(jnp.int32)
        kappa[pl.ds(base, lines)] = powers(marks)
    weight_rows(kappa, weights, stiff_rows, lines, first, last, rows_y, rows_z)
    fill(state_a, near_a, 1, near, near + even * (lines + near), pad_rows)
    fill(state_a, near_b, 1, near, near + (1 - even) * (lines + near), pad_rows)
    for copy in taken:
        copy.wait()
    ghost_low = state_a[planes, 0]
    ghost_high = state_a[planes, rows_y + 1]
    for e in range(1, 3 * planes - 1):
        if e not in range(planes, 2 * planes):
            state_a[e, 0] = ghost_low
            state_a[e, rows_y + 1] = ghost_high
        if e not in range(planes + 1, 2 * planes - 1):
            state_b[e - 1, 0] = ghost_low
            state_b[e - 1, rows_y + 1] = ghost_high
    step = functools.partial(relax_lines, weights=weights, rows_y=rows_y, rows_z=rows_z)
    ends = (lines - rows_y, 2 * lines - rows_y)
    step(state_a, state_b, first_lines=ends, count=2 * rows_y, keep=True)
    step(state_b, state_a, first_lines=(lines,), count=lines, keep=True)
    inner = (lines + rows_y,)
    step(state_a, state_b, first_lines=inner, count=lines - 2 * rows_y, keep=False)
    inside = range(planes + 1, 2 * planes - 1)
    blank = jnp.zeros(gram.shape, jnp.float32)
    gram[...] = gram_terms(state_b, inside, planes, stiff_rows, snap, both, blank)


def advance(buffers, weights, low_line, count, total, rows_y, rows_z):
    for sweep in range(1, SWEEPS + 1):
        src, dst = buffers[(sweep - 1) % 2], buffers[sweep % 2]
        low = low_line + sweep * rows_y
        ends = (low, total - low - count)
        relax_lines(src, dst, weights, ends, count, rows_y, rows_z, sweep < SWEEPS)


def far_kernel(
    flags,
    far_a,
    far_b,
    weights,
    stiff_rows,
    pad_rows,
    near_gram,
    old_a,
    old_b,
    state_a,
    state_b,
    snap,
    gram,
    both,
):
    del old_a, old_b
    width = snap.shape[1]
    rows_y = pad_rows.shape[0]
    count, rows_z = far_a.shape[:2]
    planes = stiff_rows.shape[1] // rows_y
    lines = weights.shape[1]
    half = rows_y // 2
    shift = flags[0] * (lines - 2 * half - count)
    fill(state_a, far_a, 0, count, half + shift, pad_rows)
    fill(state_a, far_b, 0, count, lines - half - count - shift, pad_rows)
    buffers = (state_a, state_b)
    advance(buffers, weights, half, count, lines, rows_y, rows_z)
    final = buffers[SWEEPS % 2]
    outer = (planes, 2 * planes - 1)
    total = gram_terms(final, outer, planes, stiff_rows, snap, both, near_gram[...])
    mass = total[:, :width]
    stiff = total[:, width:]
    stiff = stiff + stiff.T
    row = lax.broadcasted_iota(jnp.int32, (width, width), 0)
    col = lax.broadcasted_iota(jnp.int32, (width, width), 1)
    gram[pl.ds(0, width)] = jnp.where(row > col, stiff, mass)
    diagonal = jnp.sum(jnp.where(row == col, stiff, 0.0), axis=0, keepdims=True)
    gram[pl.ds(width, 8)] = jnp.broadcast_to(diagonal, (8, width))


def swap(array, start):
    count = lax.axis_size("sub")
    pairs = [(i, i + 1) for i in range(start, count - 1, 2)]
    return lax.ppermute(array, "sub", pairs + [(j, i) for i, j in pairs])


def relax(initial, classes, y_vals, z_vals, face_ids):
    planes, rows_y, rows_z, width = initial.shape
    index = lax.axis_index("sub")
    subs = lax.axis_size("sub")
    even = (index + 1) % 2
    flags = jnp.stack([even, index == 0, index == subs - 1, 0]).astype(jnp.int32)
    lines = initial.reshape(planes * rows_y, rows_z, width)
    count = planes * rows_y
    near, half = 2 * rows_y, rows_y // 2
    flat_classes = classes.reshape(count, rows_z)
    part = functools.partial(jax.ShapeDtypeStruct, dtype=initial.dtype)
    vmem = pl.BlockSpec(memory_space=pltpu.VMEM)
    smem = pl.BlockSpec(memory_space=pltpu.SMEM)
    hbm = pl.BlockSpec(memory_space=pltpu.HBM)
    first_state = pltpu.VMEM((3 * planes, rows_y + 2, width, LANES), jnp.float32)
    second_state = pltpu.VMEM((3 * planes - 2, rows_y + 2, width, LANES), jnp.float32)
    kappa = pltpu.VMEM((3 * count, LANES), jnp.float32)
    both = pltpu.VMEM((2 * width, rows_y * LANES), jnp.bfloat16)
    params = pltpu.CompilerParams(vmem_limit_bytes=8 * 2**20)

    def kept(depth):
        return jax.ShapeDtypeStruct((depth, width, rows_y * LANES), jnp.bfloat16)

    def in_hbm(item):
        return pltpu.with_memory_space_constraint(item, pltpu.HBM)

    def held(item):
        return pltpu.with_memory_space_constraint(item, pltpu.VMEM)

    rows = [
        jax.ShapeDtypeStruct((6, 3 * count, LANES), jnp.float32),
        jax.ShapeDtypeStruct((8, count, LANES), jnp.float32),
    ]
    near_a, near_b = pl.pallas_call(
        pack_kernel,
        out_shape=[part((near + 1, rows_z, width))] * 2,
        in_specs=[smem] + [hbm] * 2,
        out_specs=[vmem] * 2,
        scratch_shapes=[
            pltpu.VMEM((count, rows_z), jnp.int32),
            pltpu.SemaphoreType.DMA((3,)),
        ],
        compiler_params=params,
    )(flags, in_hbm(flat_classes), in_hbm(lines))
    near_a = swap(near_a, 0)
    near_b = swap(near_b, 1)
    hand, inner, pad_rows, far_a, far_b, own_kappa = pl.pallas_call(
        own_kernel,
        out_shape=[
            pltpu.HBM((planes,) + first_state.shape[1:], jnp.float32),
            pltpu.HBM((planes - 2,) + first_state.shape[1:], jnp.float32),
            part((rows_y, LANES - rows_z, width)),
            part((rows_y + half, rows_z, width)),
            part((rows_y + half, rows_z, width)),
            jax.ShapeDtypeStruct((count, LANES), jnp.float32),
        ],
        in_specs=[smem] + [vmem] * 5,
        out_specs=[hbm] * 2 + [vmem] * 4,
        scratch_shapes=[first_state, second_state, kappa]
        + [pltpu.VMEM(item.shape, item.dtype) for item in rows]
        + [pltpu.SemaphoreType.DMA((2,))],
        compiler_params=pltpu.CompilerParams(vmem_limit_bytes=40 * 2**20),
    )(flags, lines, flat_classes, y_vals, z_vals, face_ids[None])
    far_a = swap(far_a, 0)
    far_b = swap(far_b, 1)
    state_a, state_b, weights, stiff_rows, snap_near, gram_near = pl.pallas_call(
        near_kernel,
        out_shape=[
            first_state,
            second_state,
            *rows,
            kept(planes - 2),
            jax.ShapeDtypeStruct((width, 2 * width), jnp.float32),
        ],
        in_specs=[smem] + [vmem] * 4 + [hbm] * 2,
        out_specs=[vmem] * 6,
        scratch_shapes=[kappa, both, pltpu.SemaphoreType.DMA((2,))],
        compiler_params=params,
    )(flags, near_a, near_b, own_kappa, pad_rows, in_hbm(hand), in_hbm(inner))
    _, _, snap_far, gram = pl.pallas_call(
        far_kernel,
        out_shape=[
            first_state,
            second_state,
            kept(2),
            jax.ShapeDtypeStruct((width + 8, width), jnp.float32),
        ],
        in_specs=[smem] + [vmem] * 8,
        out_specs=[vmem] * 4,
        scratch_shapes=[both],
        input_output_aliases={7: 0, 8: 1},
        compiler_params=params,
    )(
        flags,
        far_a,
        far_b,
        weights,
        stiff_rows,
        pad_rows,
        gram_near,
        held(state_a),
        held(state_b),
    )
    return snap_near, snap_far, gram


def lane_copy(tile, lane):
    return jnp.broadcast_to(tile[:, lane : lane + 1], (8, 128))


def row_copy(tile, row):
    return jnp.broadcast_to(tile[row : row + 1, :], (8, tile.shape[1]))


def pivot_block(left, right, first_lane):
    sub = lax.broadcasted_iota(jnp.int32, (8, 128), 0)
    cols = [lane_copy(left, first_lane + j) for j in range(8)]
    for j in range(8):
        recip = pl.reciprocal(row_copy(cols[j], j), approx=True)
        here = sub == j
        mult = jnp.where(here, recip, -cols[j] * recip)
        for l in range(j + 1, 8):
            cols[l] = jnp.where(here, 0.0, cols[l]) + mult * row_copy(cols[l], j)
        left = jnp.where(here, 0.0, left) + mult * row_copy(left, j)
        right = jnp.where(here, 0.0, right) + mult * row_copy(right, j)
        yield left, right


def solve_spd(left, right):
    size = left.shape[0]
    count = size // 8
    lhs = [left[8 * t : 8 * t + 8] for t in range(count)]
    rhs = [right[8 * t : 8 * t + 8] for t in range(count)]
    for panel in pivot_block(lhs[0], rhs[0], 0):
        lhs[0], rhs[0] = panel
    for k in range(count):
        rows_l = [row_copy(lhs[k], j) for j in range(8)]
        rows_r = [row_copy(rhs[k], j) for j in range(8)]

        def update(t, k=k, rows_l=rows_l, rows_r=rows_r):
            tile_cols = [lane_copy(lhs[t], 8 * k + j) for j in range(8)]
            if k + 1 < count:
                lhs[t] = lhs[t] - tree([tile_cols[j] * rows_l[j] for j in range(8)])
            rhs[t] = rhs[t] - tree([tile_cols[j] * rows_r[j] for j in range(8)])

        others = [t for t in range(count) if t not in (k, k + 1)]
        if k + 1 < count:
            update(k + 1)
            panel = None
            for panel in pivot_block(lhs[k + 1], rhs[k + 1], 8 * (k + 1)):
                for t in others[:2]:
                    update(t)
                others = others[2:]
            lhs[k + 1], rhs[k + 1] = panel
        for t in others:
            update(t)
    return jnp.concatenate(rhs, axis=0)


def tree(terms):
    while len(terms) > 1:
        terms = [a + b for a, b in zip(terms[::2], terms[1::2])] + terms[len(terms) & ~1 :]
    return terms[0]


def whiten(inner, block):
    size = inner.shape[0]
    count = size // 8
    sub = lax.broadcasted_iota(jnp.int32, (8, 128), 0)
    lhs = [inner[8 * t : 8 * t + 8] for t in range(count)]
    rhs = [block[8 * t : 8 * t + 8] for t in range(count)]
    done = []
    for k in range(count):
        live = range(k, count)
        cols = {t: [lane_copy(lhs[t], 8 * k + j) for j in range(8)] for t in live}
        scale = None
        for j in range(8):
            pivot = row_copy(cols[k][j], j)
            recip = pl.reciprocal(pivot, approx=True)
            root = lax.rsqrt(pivot)
            scale = root if scale is None else jnp.where(sub >= j, root, scale)
            head = {l: row_copy(cols[k][l], j) for l in range(j + 1, 8)}
            row_l, row_r = row_copy(lhs[k], j), row_copy(rhs[k], j)
            for t in live:
                mult = cols[t][j] * recip
                if t == k:
                    mult = jnp.where(sub > j, mult, 0.0)
                for l in range(j + 1, 8):
                    cols[t][l] = cols[t][l] - mult * head[l]
                lhs[t] = lhs[t] - mult[:, : row_l.shape[1]] * row_l
                rhs[t] = rhs[t] - mult * row_r
        done.append(rhs[k] * scale)
    return jnp.concatenate(done, axis=0)


def pieces_of(value):
    high = value.astype(jnp.bfloat16)
    return high, (value - high.astype(jnp.float32)).astype(jnp.bfloat16)


def dot_rows(left, right):
    left_high, left_low = pieces_of(left)
    right_high, right_low = pieces_of(right)
    return lax.dot_general(
        jnp.concatenate([left_high, left_high, left_low], axis=1),
        jnp.concatenate([right_high, right_low, right_high], axis=1),
        (((1,), (1,)), ((), ())),
        preferred_element_type=jnp.float32,
    )


def modes_kernel(cell_count, rows_z, *refs):
    mask_ref, *part_refs, start_ref, near_hbm, far_hbm, out_ref, snap_ref, sems = refs
    planes, _, columns = snap_ref.shape
    places = [(far_hbm, 0, 0, 1), (near_hbm, 0, 1, planes - 2), (far_hbm, 1, planes - 1, 1)]
    fetches = [
        pltpu.make_async_copy(src.at[pl.ds(at, n)], snap_ref.at[pl.ds(to, n)], sems.at[k])
        for k, (src, at, to, n) in enumerate(places)
    ]
    for fetch in fetches:
        fetch.start()
    total = part_refs[0][...]
    for part in part_refs[1:]:
        total = total + part[...]
    width = total.shape[1]
    row = lax.broadcasted_iota(jnp.int32, (width, width), 0)
    col = lax.broadcasted_iota(jnp.int32, (width, width), 1)
    packed = total[:width]
    turned = packed.T
    mass = jnp.where(row <= col, packed, turned) * (1.0 / cell_count)
    stiff = jnp.where(row > col, packed, jnp.where(row < col, turned, total[width : width + 1]))
    stiff = stiff * (0.5 / cell_count)
    step = solve_spd(stiff, mass)
    turned_step = step.T
    form = dot_rows(turned_step, dot_rows(turned_step, mass))
    both = jnp.concatenate([form, step], axis=0)
    block = start_ref[...]
    for _ in range(ITERS):
        products = dot_rows(block, both)
        inner = dot_rows(products[:, :width], block)
        block = whiten(inner, products[:, width:])
    modes = block.astype(jnp.bfloat16)
    for fetch in fetches:
        fetch.wait()
    lanes = LANES
    rows_y = columns // lanes
    piece_rows = planes * rows_y // out_ref.shape[0]
    for p in range(planes):
        basis = jnp.dot(modes, snap_ref[p], preferred_element_type=jnp.float32)
        for y in range(rows_y):
            piece, spot = divmod(p * rows_y + y, piece_rows)
            values = basis[:, y * lanes : y * lanes + rows_z].astype(jnp.bfloat16)
            wanted = mask_ref[piece] != 0
            out_ref[piece, :, pl.ds(spot * rows_z, rows_z)] = jnp.where(wanted, values, 0.0)


def on_device(snap_init, channel_map, yface_vals, zface_vals, face_of, start_block, correlation):
    subs = lax.axis_size("sub")
    owner_count = lax.axis_size("nbhd")
    planes, rows_y, rows_z, width = snap_init.shape[1:]
    snap_near, snap_far, own = relax(
        snap_init[0], channel_map[0], yface_vals[0], zface_vals[0], face_of[0]
    )
    parts = [own] + [
        lax.ppermute(own, "sub", [(i, (i + shift) % subs) for i in range(subs)])
        for shift in range(1, subs)
    ]
    cells = planes * rows_y * rows_z
    modes = start_block.shape[-1]
    mask = lax.dynamic_slice_in_dim(correlation, lax.axis_index("nbhd"), 1, axis=0)[0]
    pieces = pl.pallas_call(
        functools.partial(modes_kernel, float(subs * cells), rows_z),
        out_shape=jax.ShapeDtypeStruct((owner_count, modes, cells // owner_count), jnp.bfloat16),
        in_specs=[pl.BlockSpec(memory_space=pltpu.SMEM)]
        + [pl.BlockSpec(memory_space=pltpu.VMEM)] * (subs + 1)
        + [pl.BlockSpec(memory_space=pltpu.HBM)] * 2,
        scratch_shapes=[
            pltpu.VMEM((planes, width, rows_y * LANES), jnp.bfloat16),
            pltpu.SemaphoreType.DMA((3,)),
        ],
        compiler_params=pltpu.CompilerParams(vmem_limit_bytes=24 * 2**20),
    )(mask, *parts, start_block[0].T, snap_near, snap_far)
    received = lax.all_to_all(pieces, "nbhd", split_axis=0, concat_axis=0, tiled=True)
    return received[None, None]


def solution(mesh):
    return jax.shard_map(
        on_device,
        mesh=mesh,
        in_specs=(
            P("nbhd", "sub", None, None, None),
            P("nbhd", "sub", None, None),
            P("nbhd", None, None),
            P("nbhd", None, None),
            P("nbhd", None),
            P("nbhd", None, None),
            P(),
        ),
        out_specs=P("nbhd", "sub", None, None, None),
        check_vma=False,
    )
```

```python
import functools

import jax
import jax.numpy as jnp
from jax import lax
from jax.experimental import pallas as pl
from jax.experimental.pallas import tpu as pltpu
from jax.sharding import PartitionSpec as P

SWEEPS = 3
ITERS = 4


def harmonic(left_k, right_k):
    return 2.0 * left_k * right_k / (left_k + right_k)


LANES = 128


def weight_rows(kappa_ref, weights, stiff_rows, lines, first, last, rows_y, rows_z):
    total = kappa_ref.shape[0]
    depth = (total - lines) // 2
    kappa = kappa_ref[...]
    shape = kappa.shape
    line = lax.broadcasted_iota(jnp.int32, shape, 0)
    row_z = lax.broadcasted_iota(jnp.int32, shape, 1)
    row_y = lax.rem(line, rows_y)

    def face(other, edge):
        return jnp.where(edge, kappa, harmonic(kappa, other))

    top = depth + lines
    faces = [
        face(pltpu.roll(kappa, rows_y, 0), (line >= depth) & (line < depth + rows_y * first)),
        face(pltpu.roll(kappa, total - rows_y, 0), (line >= top - rows_y * last) & (line < top)),
        face(pltpu.roll(kappa, 1, 0), row_y == 0),
        face(pltpu.roll(kappa, total - 1, 0), row_y == rows_y - 1),
        face(pltpu.roll(kappa, 1, 1), row_z == 0),
        face(pltpu.roll(kappa, LANES - 1, 1), row_z == rows_z - 1),
    ]
    denom = faces[0] + faces[1] + faces[2] + faces[3] + faces[4] + faces[5]
    outside = (line < depth * first) | (line >= total - depth * last) | (row_z >= rows_z)
    scale = jnp.where(outside, 0.0, 1.0 / denom)
    for k in range(6):
        weights[k] = faces[k] * scale
    upper = row_y >= rows_y // 2
    plane = lax.div(line - depth, rows_y)
    planes = lines // rows_y
    low_cross = jnp.where(upper, 2.0 - 2.0 * first.astype(jnp.float32), 0.0)
    high_cross = jnp.where(upper, 0.0, 2.0 - 2.0 * last.astype(jnp.float32))
    shares = [
        jnp.where(plane == 0, low_cross, jnp.where(plane == 1, 0.0, 1.0)),
        jnp.where(plane == planes - 1, high_cross, jnp.where(plane == planes - 2, 0.0, 1.0)),
        jnp.where(row_y == 0, 0.0, 1.0),
        jnp.where(row_y == rows_y - 1, 0.0, 1.0),
        jnp.where(row_z == 0, 0.0, 1.0),
        jnp.where(row_z == rows_z - 1, 0.0, 1.0),
    ]
    shares[0] = jnp.where(plane == planes - 1, 2.0, shares[0])
    shares[1] = jnp.where(plane == 0, 2.0, shares[1])
    rows = [item * share for item, share in zip(faces, shares)] + [denom, kappa * (1.0 / 16.0)]
    inside = (row_z < rows_z)[depth:top]
    for k in range(8):
        stiff_rows[k] = jnp.where(inside, rows[k][depth:top], 0.0)


def turned(lines):
    width = lines.shape[1]
    row = lax.broadcasted_iota(jnp.int32, (width, width), 0)
    col = lax.broadcasted_iota(jnp.int32, (width, width), 1)
    eye = jnp.where(row == col, 1.0, 0.0).astype(jnp.bfloat16)
    return lax.dot_general(eye, lines, (((1,), (1,)), ((), ())), preferred_element_type=jnp.float32)


def place(line, rows_y):
    return lax.div(line, rows_y), lax.rem(line, rows_y)


def fill(state, source, skip, count, first_line, pad_rows):
    rows_y = pad_rows.shape[0]
    group = 16 if count % 16 == 0 else 8

    def body(i, carry):
        waiting = []

        def store(e, y, both):
            state[e, y + 1] = both[:, :LANES]
            state[e, y + 2] = both[:, LANES:]

        for j in range(0, group, 2):
            at = i * group + j
            e, y = place(first_line + at, rows_y)
            lines = [source[skip + at], pad_rows[y], source[skip + at + 1], pad_rows[y + 1]]
            waiting.append((e, y, turned(jnp.concatenate(lines, axis=0))))
            if len(waiting) > 1:
                store(*waiting.pop(0))
        for item in waiting:
            store(*item)
        return carry

    lax.fori_loop(0, count // group, body, 0)


def neighbour_sum(src, e, y, rows, some, middle):
    return (
        rows[0] * src[e - 1, y + 1, some]
        + rows[1] * src[e + 1, y + 1, some]
        + rows[2] * src[e, y, some]
        + rows[3] * src[e, y + 2, some]
        + rows[4] * pltpu.roll(middle, 1, 1)
        + rows[5] * pltpu.roll(middle, LANES - 1, 1)
    )


PART = 64


def relax_lines(src, dst, weights, first_lines, count, rows_y, rows_z, keep):
    width = src.shape[2]
    group = 8
    total = weights.shape[1] // rows_y
    src_skip = (total - src.shape[0]) // 2
    dst_skip = (total - dst.shape[0]) // 2
    valid = lax.broadcasted_iota(jnp.int32, (PART, LANES), 1) < rows_z

    def body(i, carry):
        waiting = []
        for j in range(group * len(first_lines)):
            line = first_lines[j // group] + i * group + j % group
            e, y = place(line, rows_y)
            rows = [weights[k, pl.ds(line, 1)] for k in range(6)]
            for start in range(0, width, PART):
                some = pl.ds(start, PART)
                middle = src[e - src_skip, y + 1, some]
                fresh = neighbour_sum(src, e - src_skip, y, rows, some, middle)
                fresh = fresh.astype(jnp.bfloat16).astype(jnp.float32)
                if keep:
                    fresh = jnp.where(valid, fresh, middle)
                waiting.append((e - dst_skip, y, some, fresh))
                if len(waiting) > 1:
                    e0, y0, some0, value = waiting.pop(0)
                    dst[e0, y0 + 1, some0] = value
        for e0, y0, some0, value in waiting:
            dst[e0, y0 + 1, some0] = value
        return carry

    lax.fori_loop(0, count // group, body, 0)


def gram_terms(final, places, planes, stiff_rows, snap, both, total):
    _, width, columns = snap.shape
    rows_y = columns // LANES
    for item, e in enumerate(places):
        p = e - planes
        e = e - (3 * planes - final.shape[0]) // 2
        waiting = []

        def store(y, some, below, values, item=item):
            spot = pl.ds(y * LANES, LANES)
            snap[item, some, spot] = values[0]
            both[some, spot] = values[1]
            both[below, spot] = values[2]

        for y in range(rows_y):
            rows = [stiff_rows[k, pl.ds(p * rows_y + y, 1)] for k in range(8)]
            for start in range(0, width, PART):
                some = pl.ds(start, PART)
                middle = final[e, y + 1, some]
                numer = neighbour_sum(final, e, y, rows, some, middle)
                values = [middle, rows[7] * middle, rows[6] * middle - numer]
                values = [value.astype(jnp.bfloat16) for value in values]
                waiting.append((y, some, pl.ds(width + start, PART), values))
                if len(waiting) > 1:
                    store(*waiting.pop(0))
        for entry in waiting:
            store(*entry)
        total = total + lax.dot_general(
            snap[item], both[...], (((1,), (1,)), ((), ())), preferred_element_type=jnp.float32
        )
    return total


def powers(marks):
    return jnp.left_shift(jnp.int32(1), 2 * marks).astype(jnp.float32)


def pack_kernel(flags, class_map, lines, near_a, near_b, classes, sems):
    count, rows_z = classes.shape
    near = near_a.shape[0] - 1
    upward = flags[0]
    fetch = pltpu.make_async_copy(class_map, classes, sems.at[16])
    fetch.start()
    copies = []
    chunk = near // 8
    for out, start in (
        (near_a, upward * (count - near)),
        (near_b, (1 - upward) * (count - near)),
    ):
        for at in range(0, near, chunk):
            copies.append(
                pltpu.make_async_copy(
                    lines.at[pl.ds(start + at, chunk)],
                    out.at[pl.ds(1 + at, chunk)],
                    sems.at[len(copies)],
                )
            )
            copies[-1].start()
    fetch.wait()
    marks = classes[...].astype(jnp.float32).astype(jnp.bfloat16)
    width = near_a.shape[2]
    marks = jnp.concatenate([marks, jnp.zeros((count, width - rows_z), jnp.bfloat16)], axis=1)
    for out in (near_a, near_b):
        out[0, pl.ds(0, count)] = marks
        out[0, pl.ds(count, rows_z - count)] = jnp.zeros((rows_z - count, width), jnp.bfloat16)
    for copy in copies:
        copy.wait()


def own_kernel(
    flags,
    own,
    classes,
    y_vals,
    z_vals,
    face_ids,
    hand,
    inner,
    pad_rows,
    far_a,
    far_b,
    own_kappa,
    state_a,
    state_b,
    kappa,
    weights,
    stiff_rows,
    sems,
):
    lines, rows_z, width = own.shape
    rows_y = pad_rows.shape[0]
    planes = lines // rows_y
    bf16 = jnp.bfloat16
    ids = face_ids[...]
    picks = [(ids == side).astype(jnp.float32) for side in range(4)]
    spare = LANES - rows_z
    spot = lax.broadcasted_iota(jnp.int32, (spare, width), 0)
    z_all = z_vals[...].astype(jnp.float32)
    z_low = z_all * picks[2]
    z_high = z_all * picks[3]
    for y in range(rows_y):
        rows = jnp.where(spot == 0, z_high[y : y + 1], 0.0)
        pad_rows[y] = jnp.where(spot == spare - 1, z_low[y : y + 1], rows).astype(bf16)
    y_all = y_vals[...].astype(jnp.float32)
    blank = jnp.zeros((spare, width), bf16)
    ghost_low = turned(jnp.concatenate([(y_all * picks[0]).astype(bf16), blank], axis=0))
    ghost_high = turned(jnp.concatenate([(y_all * picks[1]).astype(bf16), blank], axis=0))

    def edges(e, carry):
        for state, at in ((state_a, e), (state_b, e - 1)):
            state[at, 0] = ghost_low
            state[at, rows_y + 1] = ghost_high
        return carry

    lax.fori_loop(planes, 2 * planes, edges, 0)
    fill(state_a, own, 0, lines, lines, pad_rows)
    sends = [
        pltpu.make_async_copy(state_a.at[planes + p], hand.at[p], sems.at[p])
        for p in range(planes)
    ]
    for copy in sends:
        copy.start()
    kappa[...] = jnp.ones(kappa.shape, jnp.float32)
    kappa[pl.ds(lines, lines), pl.ds(0, rows_z)] = powers(classes[...])
    own_kappa[...] = kappa[pl.ds(lines, lines)]
    weight_rows(kappa, weights, stiff_rows, lines, flags[1], flags[2], rows_y, rows_z)
    inside = lines - 2 * rows_y
    relax_lines(state_a, state_b, weights, (lines + rows_y,), inside, rows_y, rows_z, True)
    for p in range(planes - 2):
        sends.append(
            pltpu.make_async_copy(state_b.at[planes + p], inner.at[p], sems.at[planes + p])
        )
        sends[-1].start()
    half = rows_y // 2
    far = far_a.shape[0]
    for out, upward in ((far_a, flags[0]), (far_b, 1 - flags[0])):
        out[...] = own[pl.ds(upward * half + (1 - upward) * (lines - half - far), far)]
    for copy in sends:
        copy.wait()


def near_kernel(
    flags,
    near_a,
    near_b,
    own_kappa,
    pad_rows,
    hand,
    inner,
    state_a,
    state_b,
    weights,
    stiff_rows,
    snap,
    gram,
    kappa,
    both,
    sems,
):
    lines = own_kappa.shape[0]
    rows_z = near_a.shape[1]
    rows_y = pad_rows.shape[0]
    near = lines // 2
    planes = lines // rows_y
    taken = []
    cut = (rows_y + 2) // 2
    for source, state, count in ((hand, state_a, planes), (inner, state_b, planes - 2)):
        for p in range(count):
            for start in (0, cut):
                some = pl.ds(start, cut)
                taken.append(
                    pltpu.make_async_copy(
                        source.at[p, some], state.at[planes + p, some], sems.at[len(taken)]
                    )
                )
                taken[-1].start()
    even, first, last = flags[0], flags[1], flags[2]
    base_a = pl.multiple_of(even * (2 * lines), 8)
    base_b = pl.multiple_of((1 - even) * (2 * lines), 8)
    kappa[...] = jnp.ones(kappa.shape, jnp.float32)
    kappa[pl.ds(lines, lines)] = own_kappa[...]
    for base, part in ((base_a, near_a), (base_b, near_b)):
        marks = part[0][:lines].astype(jnp.float32).astype(jnp.int32)
        kappa[pl.ds(base, lines)] = powers(marks)
    weight_rows(kappa, weights, stiff_rows, lines, first, last, rows_y, rows_z)
    fill(state_a, near_a, 1, near, near + even * (lines + near), pad_rows)
    fill(state_a, near_b, 1, near, near + (1 - even) * (lines + near), pad_rows)
    for copy in taken:
        copy.wait()
    ghost_low = state_a[planes, 0]
    ghost_high = state_a[planes, rows_y + 1]
    for e in range(1, 3 * planes - 1):
        if e not in range(planes, 2 * planes):
            state_a[e, 0] = ghost_low
            state_a[e, rows_y + 1] = ghost_high
        if e not in range(planes + 1, 2 * planes - 1):
            state_b[e - 1, 0] = ghost_low
            state_b[e - 1, rows_y + 1] = ghost_high
    step = functools.partial(relax_lines, weights=weights, rows_y=rows_y, rows_z=rows_z)
    ends = (lines - rows_y, 2 * lines - rows_y)
    step(state_a, state_b, first_lines=ends, count=2 * rows_y, keep=True)
    step(state_b, state_a, first_lines=(lines,), count=lines, keep=True)
    inner = (lines + rows_y,)
    step(state_a, state_b, first_lines=inner, count=lines - 2 * rows_y, keep=False)
    inside = range(planes + 1, 2 * planes - 1)
    blank = jnp.zeros(gram.shape, jnp.float32)
    gram[...] = gram_terms(state_b, inside, planes, stiff_rows, snap, both, blank)


def advance(buffers, weights, low_line, count, total, rows_y, rows_z):
    for sweep in range(1, SWEEPS + 1):
        src, dst = buffers[(sweep - 1) % 2], buffers[sweep % 2]
        low = low_line + sweep * rows_y
        ends = (low, total - low - count)
        relax_lines(src, dst, weights, ends, count, rows_y, rows_z, sweep < SWEEPS)


def far_kernel(
    flags,
    far_a,
    far_b,
    weights,
    stiff_rows,
    pad_rows,
    near_gram,
    old_a,
    old_b,
    state_a,
    state_b,
    snap,
    gram,
    both,
):
    del old_a, old_b
    width = snap.shape[1]
    rows_y = pad_rows.shape[0]
    count, rows_z = far_a.shape[:2]
    planes = stiff_rows.shape[1] // rows_y
    lines = weights.shape[1]
    half = rows_y // 2
    shift = flags[0] * (lines - 2 * half - count)
    fill(state_a, far_a, 0, count, half + shift, pad_rows)
    fill(state_a, far_b, 0, count, lines - half - count - shift, pad_rows)
    buffers = (state_a, state_b)
    advance(buffers, weights, half, count, lines, rows_y, rows_z)
    final = buffers[SWEEPS % 2]
    outer = (planes, 2 * planes - 1)
    total = gram_terms(final, outer, planes, stiff_rows, snap, both, near_gram[...])
    mass = total[:, :width]
    stiff = total[:, width:]
    stiff = stiff + stiff.T
    row = lax.broadcasted_iota(jnp.int32, (width, width), 0)
    col = lax.broadcasted_iota(jnp.int32, (width, width), 1)
    gram[pl.ds(0, width)] = jnp.where(row > col, stiff, mass)
    diagonal = jnp.sum(jnp.where(row == col, stiff, 0.0), axis=0, keepdims=True)
    gram[pl.ds(width, 8)] = jnp.broadcast_to(diagonal, (8, width))


def swap(array, start):
    count = lax.axis_size("sub")
    pairs = [(i, i + 1) for i in range(start, count - 1, 2)]
    return lax.ppermute(array, "sub", pairs + [(j, i) for i, j in pairs])


def relax(initial, classes, y_vals, z_vals, face_ids):
    planes, rows_y, rows_z, width = initial.shape
    index = lax.axis_index("sub")
    subs = lax.axis_size("sub")
    even = (index + 1) % 2
    flags = jnp.stack([even, index == 0, index == subs - 1, 0]).astype(jnp.int32)
    lines = initial.reshape(planes * rows_y, rows_z, width)
    count = planes * rows_y
    near, half = 2 * rows_y, rows_y // 2
    flat_classes = classes.reshape(count, rows_z)
    part = functools.partial(jax.ShapeDtypeStruct, dtype=initial.dtype)
    vmem = pl.BlockSpec(memory_space=pltpu.VMEM)
    smem = pl.BlockSpec(memory_space=pltpu.SMEM)
    hbm = pl.BlockSpec(memory_space=pltpu.HBM)
    first_state = pltpu.VMEM((3 * planes, rows_y + 2, width, LANES), jnp.float32)
    second_state = pltpu.VMEM((3 * planes - 2, rows_y + 2, width, LANES), jnp.float32)
    kappa = pltpu.VMEM((3 * count, LANES), jnp.float32)
    both = pltpu.VMEM((2 * width, rows_y * LANES), jnp.bfloat16)
    params = pltpu.CompilerParams(vmem_limit_bytes=8 * 2**20)

    def kept(depth):
        return jax.ShapeDtypeStruct((depth, width, rows_y * LANES), jnp.bfloat16)

    def in_hbm(item):
        return pltpu.with_memory_space_constraint(item, pltpu.HBM)

    def held(item):
        return pltpu.with_memory_space_constraint(item, pltpu.VMEM)

    rows = [
        jax.ShapeDtypeStruct((6, 3 * count, LANES), jnp.float32),
        jax.ShapeDtypeStruct((8, count, LANES), jnp.float32),
    ]
    near_a, near_b = pl.pallas_call(
        pack_kernel,
        out_shape=[part((near + 1, rows_z, width))] * 2,
        in_specs=[smem] + [hbm] * 2,
        out_specs=[vmem] * 2,
        scratch_shapes=[
            pltpu.VMEM((count, rows_z), jnp.int32),
            pltpu.SemaphoreType.DMA((17,)),
        ],
        compiler_params=params,
    )(flags, in_hbm(flat_classes), in_hbm(lines))
    near_a = swap(near_a, 0)
    near_b = swap(near_b, 1)
    hand, inner, pad_rows, far_a, far_b, own_kappa = pl.pallas_call(
        own_kernel,
        out_shape=[
            pltpu.HBM((planes,) + first_state.shape[1:], jnp.float32),
            pltpu.HBM((planes - 2,) + first_state.shape[1:], jnp.float32),
            part((rows_y, LANES - rows_z, width)),
            part((rows_y + half, rows_z, width)),
            part((rows_y + half, rows_z, width)),
            jax.ShapeDtypeStruct((count, LANES), jnp.float32),
        ],
        in_specs=[smem] + [vmem] * 5,
        out_specs=[hbm] * 2 + [vmem] * 4,
        scratch_shapes=[first_state, second_state, kappa]
        + [pltpu.VMEM(item.shape, item.dtype) for item in rows]
        + [pltpu.SemaphoreType.DMA((2 * planes - 2,))],
        compiler_params=pltpu.CompilerParams(vmem_limit_bytes=40 * 2**20),
    )(flags, lines, flat_classes, y_vals, z_vals, face_ids[None])
    far_a = swap(far_a, 0)
    far_b = swap(far_b, 1)
    state_a, state_b, weights, stiff_rows, snap_near, gram_near = pl.pallas_call(
        near_kernel,
        out_shape=[
            first_state,
            second_state,
            *rows,
            kept(planes - 2),
            jax.ShapeDtypeStruct((width, 2 * width), jnp.float32),
        ],
        in_specs=[smem] + [vmem] * 4 + [hbm] * 2,
        out_specs=[vmem] * 6,
        scratch_shapes=[kappa, both, pltpu.SemaphoreType.DMA((4 * planes - 4,))],
        compiler_params=params,
    )(flags, near_a, near_b, own_kappa, pad_rows, in_hbm(hand), in_hbm(inner))
    _, _, snap_far, gram = pl.pallas_call(
        far_kernel,
        out_shape=[
            first_state,
            second_state,
            kept(2),
            jax.ShapeDtypeStruct((width + 8, width), jnp.float32),
        ],
        in_specs=[smem] + [vmem] * 8,
        out_specs=[vmem] * 4,
        scratch_shapes=[both],
        input_output_aliases={7: 0, 8: 1},
        compiler_params=params,
    )(
        flags,
        far_a,
        far_b,
        weights,
        stiff_rows,
        pad_rows,
        gram_near,
        held(state_a),
        held(state_b),
    )
    return snap_near, snap_far, gram


def lane_copy(tile, lane):
    return jnp.broadcast_to(tile[:, lane : lane + 1], (8, 128))


def row_copy(tile, row):
    return jnp.broadcast_to(tile[row : row + 1, :], (8, tile.shape[1]))


def pivot_block(left, right, first_lane):
    sub = lax.broadcasted_iota(jnp.int32, (8, 128), 0)
    cols = [lane_copy(left, first_lane + j) for j in range(8)]
    for j in range(8):
        recip = pl.reciprocal(row_copy(cols[j], j), approx=True)
        here = sub == j
        mult = jnp.where(here, recip, -cols[j] * recip)
        for l in range(j + 1, 8):
            cols[l] = jnp.where(here, 0.0, cols[l]) + mult * row_copy(cols[l], j)
        left = jnp.where(here, 0.0, left) + mult * row_copy(left, j)
        right = jnp.where(here, 0.0, right) + mult * row_copy(right, j)
        yield left, right


def solve_spd(left, right):
    size = left.shape[0]
    count = size // 8
    lhs = [left[8 * t : 8 * t + 8] for t in range(count)]
    rhs = [right[8 * t : 8 * t + 8] for t in range(count)]
    for panel in pivot_block(lhs[0], rhs[0], 0):
        lhs[0], rhs[0] = panel
    for k in range(count):
        rows_l = [row_copy(lhs[k], j) for j in range(8)]
        rows_r = [row_copy(rhs[k], j) for j in range(8)]

        def update(t, k=k, rows_l=rows_l, rows_r=rows_r):
            tile_cols = [lane_copy(lhs[t], 8 * k + j) for j in range(8)]
            if k + 1 < count:
                lhs[t] = lhs[t] - tree([tile_cols[j] * rows_l[j] for j in range(8)])
            rhs[t] = rhs[t] - tree([tile_cols[j] * rows_r[j] for j in range(8)])

        others = [t for t in range(count) if t not in (k, k + 1)]
        if k + 1 < count:
            update(k + 1)
            panel = None
            for panel in pivot_block(lhs[k + 1], rhs[k + 1], 8 * (k + 1)):
                for t in others[:2]:
                    update(t)
                others = others[2:]
            lhs[k + 1], rhs[k + 1] = panel
        for t in others:
            update(t)
    return jnp.concatenate(rhs, axis=0)


def tree(terms):
    while len(terms) > 1:
        terms = [a + b for a, b in zip(terms[::2], terms[1::2])] + terms[len(terms) & ~1 :]
    return terms[0]


def whiten(inner, block):
    size = inner.shape[0]
    count = size // 8
    sub = lax.broadcasted_iota(jnp.int32, (8, 128), 0)
    lhs = [inner[8 * t : 8 * t + 8] for t in range(count)]
    rhs = [block[8 * t : 8 * t + 8] for t in range(count)]
    done = []
    for k in range(count):
        live = range(k, count)
        cols = {t: [lane_copy(lhs[t], 8 * k + j) for j in range(8)] for t in live}
        scale = None
        for j in range(8):
            pivot = row_copy(cols[k][j], j)
            recip = pl.reciprocal(pivot, approx=True)
            root = lax.rsqrt(pivot)
            scale = root if scale is None else jnp.where(sub >= j, root, scale)
            head = {l: row_copy(cols[k][l], j) for l in range(j + 1, 8)}
            row_l, row_r = row_copy(lhs[k], j), row_copy(rhs[k], j)
            for t in live:
                mult = cols[t][j] * recip
                if t == k:
                    mult = jnp.where(sub > j, mult, 0.0)
                for l in range(j + 1, 8):
                    cols[t][l] = cols[t][l] - mult * head[l]
                lhs[t] = lhs[t] - mult[:, : row_l.shape[1]] * row_l
                rhs[t] = rhs[t] - mult * row_r
        done.append(rhs[k] * scale)
    return jnp.concatenate(done, axis=0)


def pieces_of(value):
    high = value.astype(jnp.bfloat16)
    return high, (value - high.astype(jnp.float32)).astype(jnp.bfloat16)


def dot_rows(left, right):
    left_high, left_low = pieces_of(left)
    right_high, right_low = pieces_of(right)
    return lax.dot_general(
        jnp.concatenate([left_high, left_high, left_low], axis=1),
        jnp.concatenate([right_high, right_low, right_high], axis=1),
        (((1,), (1,)), ((), ())),
        preferred_element_type=jnp.float32,
    )


def order_kernel(rows_z, near_ref, far_ref, out_ref):
    planes = near_ref.shape[0] + 2
    rows_y = near_ref.shape[2] // LANES
    piece_rows = planes * rows_y // out_ref.shape[0]
    for p in range(planes):
        inside = 0 < p < planes - 1
        source, at = (near_ref, p - 1) if inside else (far_ref, min(p, 1))
        for y in range(rows_y):
            piece, spot = divmod(p * rows_y + y, piece_rows)
            out_ref[piece, :, pl.ds(spot * rows_z, rows_z)] = source[
                at, :, pl.ds(y * LANES, rows_z)
            ]


def modes_kernel(cell_count, *refs):
    mask_ref, *part_refs, start_ref, snap_hbm, out_ref, snap_ref, sem = refs
    fetch = pltpu.make_async_copy(snap_hbm, snap_ref, sem)
    fetch.start()
    total = part_refs[0][...]
    for part in part_refs[1:]:
        total = total + part[...]
    width = total.shape[1]
    row = lax.broadcasted_iota(jnp.int32, (width, width), 0)
    col = lax.broadcasted_iota(jnp.int32, (width, width), 1)
    packed = total[:width]
    turned = packed.T
    mass = jnp.where(row <= col, packed, turned) * (1.0 / cell_count)
    stiff = jnp.where(row > col, packed, jnp.where(row < col, turned, total[width : width + 1]))
    stiff = stiff * (0.5 / cell_count)
    step = solve_spd(stiff, mass)
    turned_step = step.T
    form = dot_rows(turned_step, dot_rows(turned_step, mass))
    both = jnp.concatenate([form, step], axis=0)
    block = start_ref[...]
    for _ in range(ITERS):
        products = dot_rows(block, both)
        inner = dot_rows(products[:, :width], block)
        block = whiten(inner, products[:, width:])
    modes = block.astype(jnp.bfloat16)
    fetch.wait()
    for piece in range(out_ref.shape[0]):
        basis = jnp.dot(modes, snap_ref[piece], preferred_element_type=jnp.float32)
        wanted = mask_ref[piece] != 0
        out_ref[piece] = jnp.where(wanted, basis.astype(jnp.bfloat16), 0.0)


def on_device(snap_init, channel_map, yface_vals, zface_vals, face_of, start_block, correlation):
    subs = lax.axis_size("sub")
    owner_count = lax.axis_size("nbhd")
    planes, rows_y, rows_z, width = snap_init.shape[1:]
    snap_near, snap_far, own = relax(
        snap_init[0], channel_map[0], yface_vals[0], zface_vals[0], face_of[0]
    )
    parts = [own] + [
        lax.ppermute(own, "sub", [(i, (i + shift) % subs) for i in range(subs)])
        for shift in range(1, subs)
    ]
    cells = planes * rows_y * rows_z
    ordered = pl.pallas_call(
        functools.partial(order_kernel, rows_z),
        out_shape=jax.ShapeDtypeStruct((owner_count, width, cells // owner_count), jnp.bfloat16),
        compiler_params=pltpu.CompilerParams(vmem_limit_bytes=8 * 2**20),
    )(snap_near, snap_far)
    modes = start_block.shape[-1]
    mask = lax.dynamic_slice_in_dim(correlation, lax.axis_index("nbhd"), 1, axis=0)[0]
    pieces = pl.pallas_call(
        functools.partial(modes_kernel, float(subs * cells)),
        out_shape=jax.ShapeDtypeStruct((owner_count, modes, cells // owner_count), jnp.bfloat16),
        in_specs=[pl.BlockSpec(memory_space=pltpu.SMEM)]
        + [pl.BlockSpec(memory_space=pltpu.VMEM)] * (subs + 1)
        + [pl.BlockSpec(memory_space=pltpu.HBM)],
        scratch_shapes=[
            pltpu.VMEM(ordered.shape, ordered.dtype),
            pltpu.SemaphoreType.DMA,
        ],
        compiler_params=pltpu.CompilerParams(vmem_limit_bytes=24 * 2**20),
    )(mask, *parts, start_block[0].T, ordered)
    received = lax.all_to_all(pieces, "nbhd", split_axis=0, concat_axis=0, tiled=True)
    return received[None, None]


def solution(mesh):
    return jax.shard_map(
        on_device,
        mesh=mesh,
        in_specs=(
            P("nbhd", "sub", None, None, None),
            P("nbhd", "sub", None, None),
            P("nbhd", None, None),
            P("nbhd", None, None),
            P("nbhd", None),
            P("nbhd", None, None),
            P(),
        ),
        out_specs=P("nbhd", "sub", None, None, None),
        check_vma=False,
    )
```

```python
import functools

import jax
import jax.numpy as jnp
from jax import lax
from jax.experimental import pallas as pl
from jax.experimental.pallas import tpu as pltpu
from jax.sharding import PartitionSpec as P

SWEEPS = 3
ITERS = 4


def harmonic(left_k, right_k):
    return 2.0 * left_k * right_k / (left_k + right_k)


LANES = 128


def weight_rows(kappa_ref, weights, stiff_rows, lines, first, last, rows_y, rows_z):
    total = kappa_ref.shape[0]
    depth = (total - lines) // 2
    kappa = kappa_ref[...]
    shape = kappa.shape
    line = lax.broadcasted_iota(jnp.int32, shape, 0)
    row_z = lax.broadcasted_iota(jnp.int32, shape, 1)
    row_y = lax.rem(line, rows_y)

    def face(other, edge):
        return jnp.where(edge, kappa, harmonic(kappa, other))

    top = depth + lines
    faces = [
        face(pltpu.roll(kappa, rows_y, 0), (line >= depth) & (line < depth + rows_y * first)),
        face(pltpu.roll(kappa, total - rows_y, 0), (line >= top - rows_y * last) & (line < top)),
        face(pltpu.roll(kappa, 1, 0), row_y == 0),
        face(pltpu.roll(kappa, total - 1, 0), row_y == rows_y - 1),
        face(pltpu.roll(kappa, 1, 1), row_z == 0),
        face(pltpu.roll(kappa, LANES - 1, 1), row_z == rows_z - 1),
    ]
    denom = faces[0] + faces[1] + faces[2] + faces[3] + faces[4] + faces[5]
    outside = (line < depth * first) | (line >= total - depth * last) | (row_z >= rows_z)
    scale = jnp.where(outside, 0.0, 1.0 / denom)
    for k in range(6):
        weights[k] = faces[k] * scale
    upper = row_y >= rows_y // 2
    plane = lax.div(line - depth, rows_y)
    planes = lines // rows_y
    low_cross = jnp.where(upper, 2.0 - 2.0 * first.astype(jnp.float32), 0.0)
    high_cross = jnp.where(upper, 0.0, 2.0 - 2.0 * last.astype(jnp.float32))
    shares = [
        jnp.where(plane == 0, low_cross, jnp.where(plane == 1, 0.0, 1.0)),
        jnp.where(plane == planes - 1, high_cross, jnp.where(plane == planes - 2, 0.0, 1.0)),
        jnp.where(row_y == 0, 0.0, 1.0),
        jnp.where(row_y == rows_y - 1, 0.0, 1.0),
        jnp.where(row_z == 0, 0.0, 1.0),
        jnp.where(row_z == rows_z - 1, 0.0, 1.0),
    ]
    shares[0] = jnp.where(plane == planes - 1, 2.0, shares[0])
    shares[1] = jnp.where(plane == 0, 2.0, shares[1])
    rows = [item * share for item, share in zip(faces, shares)] + [denom, kappa * (1.0 / 16.0)]
    inside = (row_z < rows_z)[depth:top]
    for k in range(8):
        stiff_rows[k] = jnp.where(inside, rows[k][depth:top], 0.0)


def turned(lines):
    width = lines.shape[1]
    row = lax.broadcasted_iota(jnp.int32, (width, width), 0)
    col = lax.broadcasted_iota(jnp.int32, (width, width), 1)
    eye = jnp.where(row == col, 1.0, 0.0).astype(jnp.bfloat16)
    return lax.dot_general(eye, lines, (((1,), (1,)), ((), ())), preferred_element_type=jnp.float32)


def place(line, rows_y):
    return lax.div(line, rows_y), lax.rem(line, rows_y)


def fill(state, source, skip, count, first_line, pad_rows):
    rows_y = pad_rows.shape[0]
    group = 16 if count % 16 == 0 else 8

    def body(i, carry):
        waiting = []

        def store(e, y, both):
            state[e, y + 1] = both[:, :LANES]
            state[e, y + 2] = both[:, LANES:]

        for j in range(0, group, 2):
            at = i * group + j
            e, y = place(first_line + at, rows_y)
            lines = [source[skip + at], pad_rows[y], source[skip + at + 1], pad_rows[y + 1]]
            waiting.append((e, y, turned(jnp.concatenate(lines, axis=0))))
            if len(waiting) > 1:
                store(*waiting.pop(0))
        for item in waiting:
            store(*item)
        return carry

    lax.fori_loop(0, count // group, body, 0)


def neighbour_sum(src, e, y, rows, some, middle):
    return (
        rows[0] * src[e - 1, y + 1, some]
        + rows[1] * src[e + 1, y + 1, some]
        + rows[2] * src[e, y, some]
        + rows[3] * src[e, y + 2, some]
        + rows[4] * pltpu.roll(middle, 1, 1)
        + rows[5] * pltpu.roll(middle, LANES - 1, 1)
    )


PART = 64


def relax_lines(src, dst, weights, first_lines, count, rows_y, rows_z, keep):
    width = src.shape[2]
    group = 8
    total = weights.shape[1] // rows_y
    src_skip = (total - src.shape[0]) // 2
    dst_skip = (total - dst.shape[0]) // 2
    valid = lax.broadcasted_iota(jnp.int32, (PART, LANES), 1) < rows_z

    def body(i, carry):
        waiting = []
        for j in range(group * len(first_lines)):
            line = first_lines[j // group] + i * group + j % group
            e, y = place(line, rows_y)
            rows = [weights[k, pl.ds(line, 1)] for k in range(6)]
            for start in range(0, width, PART):
                some = pl.ds(start, PART)
                middle = src[e - src_skip, y + 1, some]
                fresh = neighbour_sum(src, e - src_skip, y, rows, some, middle)
                fresh = fresh.astype(jnp.bfloat16).astype(jnp.float32)
                if keep:
                    fresh = jnp.where(valid, fresh, middle)
                waiting.append((e - dst_skip, y, some, fresh))
                if len(waiting) > 1:
                    e0, y0, some0, value = waiting.pop(0)
                    dst[e0, y0 + 1, some0] = value
        for e0, y0, some0, value in waiting:
            dst[e0, y0 + 1, some0] = value
        return carry

    lax.fori_loop(0, count // group, body, 0)


def gram_terms(final, places, planes, stiff_rows, snap, both, total):
    _, width, columns = snap.shape
    rows_y = columns // LANES
    for item, e in enumerate(places):
        p = e - planes
        e = e - (3 * planes - final.shape[0]) // 2
        waiting = []

        def store(y, some, below, values, item=item):
            spot = pl.ds(y * LANES, LANES)
            snap[item, some, spot] = values[0]
            both[some, spot] = values[1]
            both[below, spot] = values[2]

        for y in range(rows_y):
            rows = [stiff_rows[k, pl.ds(p * rows_y + y, 1)] for k in range(8)]
            for start in range(0, width, PART):
                some = pl.ds(start, PART)
                middle = final[e, y + 1, some]
                numer = neighbour_sum(final, e, y, rows, some, middle)
                values = [middle, rows[7] * middle, rows[6] * middle - numer]
                values = [value.astype(jnp.bfloat16) for value in values]
                waiting.append((y, some, pl.ds(width + start, PART), values))
                if len(waiting) > 1:
                    store(*waiting.pop(0))
        for entry in waiting:
            store(*entry)
        total = total + lax.dot_general(
            snap[item], both[...], (((1,), (1,)), ((), ())), preferred_element_type=jnp.float32
        )
    return total


def powers(marks):
    return jnp.left_shift(jnp.int32(1), 2 * marks).astype(jnp.float32)


def pack_kernel(flags, class_map, lines, near_a, near_b, mid_a, mid_b, classes, sems):
    count, rows_z = classes.shape
    size = mid_a.shape[0]
    upward = flags[0]
    fetch = pltpu.make_async_copy(class_map, classes, sems.at[4])
    fetch.start()
    copies = []
    for out, skip, start in (
        (near_a, 1, upward * (count - size)),
        (near_b, 1, (1 - upward) * (count - size)),
        (mid_a, 0, size + upward * (count - 3 * size)),
        (mid_b, 0, size + (1 - upward) * (count - 3 * size)),
    ):
        copies.append(
            pltpu.make_async_copy(
                lines.at[pl.ds(start, size)], out.at[pl.ds(skip, size)], sems.at[len(copies)]
            )
        )
        copies[-1].start()
    fetch.wait()
    marks = classes[...].astype(jnp.float32).astype(jnp.bfloat16)
    width = near_a.shape[2]
    marks = jnp.concatenate([marks, jnp.zeros((count, width - rows_z), jnp.bfloat16)], axis=1)
    for out in (near_a, near_b):
        out[0, pl.ds(0, count)] = marks
        out[0, pl.ds(count, rows_z - count)] = jnp.zeros((rows_z - count, width), jnp.bfloat16)
    for copy in copies:
        copy.wait()


def own_kernel(
    flags,
    own,
    classes,
    y_vals,
    z_vals,
    face_ids,
    hand,
    inner,
    pad_rows,
    far_a,
    far_b,
    own_kappa,
    state_a,
    state_b,
    kappa,
    weights,
    stiff_rows,
    sems,
):
    lines, rows_z, width = own.shape
    rows_y = pad_rows.shape[0]
    planes = lines // rows_y
    bf16 = jnp.bfloat16
    ids = face_ids[...]
    picks = [(ids == side).astype(jnp.float32) for side in range(4)]
    spare = LANES - rows_z
    spot = lax.broadcasted_iota(jnp.int32, (spare, width), 0)
    z_all = z_vals[...].astype(jnp.float32)
    z_low = z_all * picks[2]
    z_high = z_all * picks[3]
    for y in range(rows_y):
        rows = jnp.where(spot == 0, z_high[y : y + 1], 0.0)
        pad_rows[y] = jnp.where(spot == spare - 1, z_low[y : y + 1], rows).astype(bf16)
    y_all = y_vals[...].astype(jnp.float32)
    blank = jnp.zeros((spare, width), bf16)
    ghost_low = turned(jnp.concatenate([(y_all * picks[0]).astype(bf16), blank], axis=0))
    ghost_high = turned(jnp.concatenate([(y_all * picks[1]).astype(bf16), blank], axis=0))

    def edges(e, carry):
        for state, at in ((state_a, e), (state_b, e - 1)):
            state[at, 0] = ghost_low
            state[at, rows_y + 1] = ghost_high
        return carry

    lax.fori_loop(planes, 2 * planes, edges, 0)
    fill(state_a, own, 0, lines, lines, pad_rows)
    sends = [
        pltpu.make_async_copy(state_a.at[planes + p], hand.at[p], sems.at[p])
        for p in range(planes)
    ]
    for copy in sends:
        copy.start()
    kappa[...] = jnp.ones(kappa.shape, jnp.float32)
    kappa[pl.ds(lines, lines), pl.ds(0, rows_z)] = powers(classes[...])
    own_kappa[...] = kappa[pl.ds(lines, lines)]
    weight_rows(kappa, weights, stiff_rows, lines, flags[1], flags[2], rows_y, rows_z)
    inside = lines - 2 * rows_y
    relax_lines(state_a, state_b, weights, (lines + rows_y,), inside, rows_y, rows_z, True)
    for p in range(planes - 2):
        sends.append(
            pltpu.make_async_copy(state_b.at[planes + p], inner.at[p], sems.at[planes + p])
        )
        sends[-1].start()
    half = rows_y // 2
    far = far_a.shape[0]
    for out, upward in ((far_a, flags[0]), (far_b, 1 - flags[0])):
        out[...] = own[pl.ds(upward * half + (1 - upward) * (lines - half - far), far)]
    for copy in sends:
        copy.wait()


def near_kernel(
    flags,
    near_a,
    near_b,
    own_kappa,
    pad_rows,
    hand,
    inner,
    state_a,
    state_b,
    weights,
    stiff_rows,
    kappa,
    sems,
):
    lines = own_kappa.shape[0]
    rows_z = near_a.shape[1]
    rows_y = pad_rows.shape[0]
    gap = lines + rows_y
    planes = lines // rows_y
    taken = []
    cut = (rows_y + 2) // 2
    for source, state, count in ((hand, state_a, planes), (inner, state_b, planes - 2)):
        for p in range(count):
            for start in (0, cut):
                some = pl.ds(start, cut)
                taken.append(
                    pltpu.make_async_copy(
                        source.at[p, some], state.at[planes + p, some], sems.at[len(taken)]
                    )
                )
                taken[-1].start()
    even, first, last = flags[0], flags[1], flags[2]
    base_a = pl.multiple_of(even * (2 * lines), 8)
    base_b = pl.multiple_of((1 - even) * (2 * lines), 8)
    kappa[...] = jnp.ones(kappa.shape, jnp.float32)
    kappa[pl.ds(lines, lines)] = own_kappa[...]
    for base, part in ((base_a, near_a), (base_b, near_b)):
        marks = part[0][:lines].astype(jnp.float32).astype(jnp.int32)
        kappa[pl.ds(base, lines)] = powers(marks)
    weight_rows(kappa, weights, stiff_rows, lines, first, last, rows_y, rows_z)
    low = lines - rows_y
    fill(state_a, near_a, 1, rows_y, low + even * gap, pad_rows)
    fill(state_a, near_b, 1, rows_y, low + (1 - even) * gap, pad_rows)
    for copy in taken:
        copy.wait()
    ghost_low = state_a[planes, 0]
    ghost_high = state_a[planes, rows_y + 1]
    for e in range(1, 3 * planes - 1):
        if e not in range(planes, 2 * planes):
            state_a[e, 0] = ghost_low
            state_a[e, rows_y + 1] = ghost_high
        if e not in range(planes + 1, 2 * planes - 1):
            state_b[e - 1, 0] = ghost_low
            state_b[e - 1, rows_y + 1] = ghost_high
    step = functools.partial(relax_lines, weights=weights, rows_y=rows_y, rows_z=rows_z)
    step(state_a, state_b, first_lines=(lines, 2 * lines - rows_y), count=rows_y, keep=True)
    inner = (lines + rows_y,)
    step(state_b, state_a, first_lines=inner, count=lines - 2 * rows_y, keep=True)


def mid_kernel(
    flags,
    mid_a,
    mid_b,
    weights,
    stiff_rows,
    pad_rows,
    old_a,
    old_b,
    state_a,
    state_b,
    snap,
    gram,
    both,
):
    del old_a, old_b
    rows_y = pad_rows.shape[0]
    rows_z = mid_a.shape[1]
    lines = stiff_rows.shape[1]
    planes = lines // rows_y
    even = flags[0]
    low = lines - 2 * rows_y
    gap = lines + 3 * rows_y
    fill(state_a, mid_a, 0, rows_y, low + even * gap, pad_rows)
    fill(state_a, mid_b, 0, rows_y, low + (1 - even) * gap, pad_rows)
    step = functools.partial(relax_lines, weights=weights, rows_y=rows_y, rows_z=rows_z)
    step(state_a, state_b, first_lines=(lines - rows_y, 2 * lines), count=rows_y, keep=True)
    step(state_b, state_a, first_lines=(lines, 2 * lines - rows_y), count=rows_y, keep=True)
    inner = (lines + rows_y,)
    step(state_a, state_b, first_lines=inner, count=lines - 2 * rows_y, keep=False)
    inside = range(planes + 1, 2 * planes - 1)
    blank = jnp.zeros(gram.shape, jnp.float32)
    gram[...] = gram_terms(state_b, inside, planes, stiff_rows, snap, both, blank)


def advance(buffers, weights, low_line, count, total, rows_y, rows_z):
    for sweep in range(1, SWEEPS + 1):
        src, dst = buffers[(sweep - 1) % 2], buffers[sweep % 2]
        low = low_line + sweep * rows_y
        ends = (low, total - low - count)
        relax_lines(src, dst, weights, ends, count, rows_y, rows_z, sweep < SWEEPS)


def far_kernel(
    flags,
    far_a,
    far_b,
    weights,
    stiff_rows,
    pad_rows,
    near_gram,
    old_a,
    old_b,
    state_a,
    state_b,
    snap,
    gram,
    both,
):
    del old_a, old_b
    width = snap.shape[1]
    rows_y = pad_rows.shape[0]
    count, rows_z = far_a.shape[:2]
    planes = stiff_rows.shape[1] // rows_y
    lines = weights.shape[1]
    half = rows_y // 2
    shift = flags[0] * (lines - 2 * half - count)
    fill(state_a, far_a, 0, count, half + shift, pad_rows)
    fill(state_a, far_b, 0, count, lines - half - count - shift, pad_rows)
    buffers = (state_a, state_b)
    advance(buffers, weights, half, count, lines, rows_y, rows_z)
    final = buffers[SWEEPS % 2]
    outer = (planes, 2 * planes - 1)
    total = gram_terms(final, outer, planes, stiff_rows, snap, both, near_gram[...])
    mass = total[:, :width]
    stiff = total[:, width:]
    stiff = stiff + stiff.T
    row = lax.broadcasted_iota(jnp.int32, (width, width), 0)
    col = lax.broadcasted_iota(jnp.int32, (width, width), 1)
    gram[pl.ds(0, width)] = jnp.where(row > col, stiff, mass)
    diagonal = jnp.sum(jnp.where(row == col, stiff, 0.0), axis=0, keepdims=True)
    gram[pl.ds(width, 8)] = jnp.broadcast_to(diagonal, (8, width))


def swap(array, start):
    count = lax.axis_size("sub")
    pairs = [(i, i + 1) for i in range(start, count - 1, 2)]
    return lax.ppermute(array, "sub", pairs + [(j, i) for i, j in pairs])


def relax(initial, classes, y_vals, z_vals, face_ids):
    planes, rows_y, rows_z, width = initial.shape
    index = lax.axis_index("sub")
    subs = lax.axis_size("sub")
    even = (index + 1) % 2
    flags = jnp.stack([even, index == 0, index == subs - 1, 0]).astype(jnp.int32)
    lines = initial.reshape(planes * rows_y, rows_z, width)
    count = planes * rows_y
    half = rows_y // 2
    flat_classes = classes.reshape(count, rows_z)
    part = functools.partial(jax.ShapeDtypeStruct, dtype=initial.dtype)
    vmem = pl.BlockSpec(memory_space=pltpu.VMEM)
    smem = pl.BlockSpec(memory_space=pltpu.SMEM)
    hbm = pl.BlockSpec(memory_space=pltpu.HBM)
    first_state = pltpu.VMEM((3 * planes, rows_y + 2, width, LANES), jnp.float32)
    second_state = pltpu.VMEM((3 * planes - 2, rows_y + 2, width, LANES), jnp.float32)
    kappa = pltpu.VMEM((3 * count, LANES), jnp.float32)
    both = pltpu.VMEM((2 * width, rows_y * LANES), jnp.bfloat16)
    params = pltpu.CompilerParams(vmem_limit_bytes=8 * 2**20)

    def kept(depth):
        return jax.ShapeDtypeStruct((depth, width, rows_y * LANES), jnp.bfloat16)

    def in_hbm(item):
        return pltpu.with_memory_space_constraint(item, pltpu.HBM)

    def held(item):
        return pltpu.with_memory_space_constraint(item, pltpu.VMEM)

    rows = [
        jax.ShapeDtypeStruct((6, 3 * count, LANES), jnp.float32),
        jax.ShapeDtypeStruct((8, count, LANES), jnp.float32),
    ]
    near_a, near_b, mid_a, mid_b = pl.pallas_call(
        pack_kernel,
        out_shape=[part((rows_y + 1, rows_z, width))] * 2 + [part((rows_y, rows_z, width))] * 2,
        in_specs=[smem] + [hbm] * 2,
        out_specs=[vmem] * 4,
        scratch_shapes=[
            pltpu.VMEM((count, rows_z), jnp.int32),
            pltpu.SemaphoreType.DMA((5,)),
        ],
        compiler_params=params,
    )(flags, in_hbm(flat_classes), in_hbm(lines))
    near_a = swap(near_a, 0)
    near_b = swap(near_b, 1)
    mid_a = swap(mid_a, 0)
    mid_b = swap(mid_b, 1)
    hand, inner, pad_rows, far_a, far_b, own_kappa = pl.pallas_call(
        own_kernel,
        out_shape=[
            pltpu.HBM((planes,) + first_state.shape[1:], jnp.float32),
            pltpu.HBM((planes - 2,) + first_state.shape[1:], jnp.float32),
            part((rows_y, LANES - rows_z, width)),
            part((rows_y + half, rows_z, width)),
            part((rows_y + half, rows_z, width)),
            jax.ShapeDtypeStruct((count, LANES), jnp.float32),
        ],
        in_specs=[smem] + [vmem] * 5,
        out_specs=[hbm] * 2 + [vmem] * 4,
        scratch_shapes=[first_state, second_state, kappa]
        + [pltpu.VMEM(item.shape, item.dtype) for item in rows]
        + [pltpu.SemaphoreType.DMA((2 * planes - 2,))],
        compiler_params=pltpu.CompilerParams(vmem_limit_bytes=40 * 2**20),
    )(flags, lines, flat_classes, y_vals, z_vals, face_ids[None])
    far_a = swap(far_a, 0)
    far_b = swap(far_b, 1)
    state_a, state_b, weights, stiff_rows = pl.pallas_call(
        near_kernel,
        out_shape=[first_state, second_state, *rows],
        in_specs=[smem] + [vmem] * 4 + [hbm] * 2,
        out_specs=[vmem] * 4,
        scratch_shapes=[kappa, pltpu.SemaphoreType.DMA((4 * planes - 4,))],
        compiler_params=params,
    )(flags, near_a, near_b, own_kappa, pad_rows, in_hbm(hand), in_hbm(inner))
    state_a, state_b, snap_near, gram_near = pl.pallas_call(
        mid_kernel,
        out_shape=[
            first_state,
            second_state,
            kept(planes - 2),
            jax.ShapeDtypeStruct((width, 2 * width), jnp.float32),
        ],
        in_specs=[smem] + [vmem] * 7,
        out_specs=[vmem] * 4,
        scratch_shapes=[both],
        input_output_aliases={6: 0, 7: 1},
        compiler_params=params,
    )(flags, mid_a, mid_b, weights, stiff_rows, pad_rows, held(state_a), held(state_b))
    _, _, snap_far, gram = pl.pallas_call(
        far_kernel,
        out_shape=[
            first_state,
            second_state,
            kept(2),
            jax.ShapeDtypeStruct((width + 8, width), jnp.float32),
        ],
        in_specs=[smem] + [vmem] * 8,
        out_specs=[vmem] * 4,
        scratch_shapes=[both],
        input_output_aliases={7: 0, 8: 1},
        compiler_params=params,
    )(
        flags,
        far_a,
        far_b,
        weights,
        stiff_rows,
        pad_rows,
        gram_near,
        held(state_a),
        held(state_b),
    )
    return snap_near, snap_far, gram


def lane_copy(tile, lane):
    return jnp.broadcast_to(tile[:, lane : lane + 1], (8, 128))


def row_copy(tile, row):
    return jnp.broadcast_to(tile[row : row + 1, :], (8, tile.shape[1]))


def pivot_block(left, right, first_lane):
    sub = lax.broadcasted_iota(jnp.int32, (8, 128), 0)
    cols = [lane_copy(left, first_lane + j) for j in range(8)]
    for j in range(8):
        recip = pl.reciprocal(row_copy(cols[j], j), approx=True)
        here = sub == j
        mult = jnp.where(here, recip, -cols[j] * recip)
        for l in range(j + 1, 8):
            cols[l] = jnp.where(here, 0.0, cols[l]) + mult * row_copy(cols[l], j)
        left = jnp.where(here, 0.0, left) + mult * row_copy(left, j)
        right = jnp.where(here, 0.0, right) + mult * row_copy(right, j)
        yield left, right


def solve_spd(left, right):
    size = left.shape[0]
    count = size // 8
    lhs = [left[8 * t : 8 * t + 8] for t in range(count)]
    rhs = [right[8 * t : 8 * t + 8] for t in range(count)]
    for panel in pivot_block(lhs[0], rhs[0], 0):
        lhs[0], rhs[0] = panel
    for k in range(count):
        rows_l = [row_copy(lhs[k], j) for j in range(8)]
        rows_r = [row_copy(rhs[k], j) for j in range(8)]

        def update(t, k=k, rows_l=rows_l, rows_r=rows_r):
            tile_cols = [lane_copy(lhs[t], 8 * k + j) for j in range(8)]
            if k + 1 < count:
                lhs[t] = lhs[t] - tree([tile_cols[j] * rows_l[j] for j in range(8)])
            rhs[t] = rhs[t] - tree([tile_cols[j] * rows_r[j] for j in range(8)])

        others = [t for t in range(count) if t not in (k, k + 1)]
        if k + 1 < count:
            update(k + 1)
            panel = None
            for panel in pivot_block(lhs[k + 1], rhs[k + 1], 8 * (k + 1)):
                for t in others[:2]:
                    update(t)
                others = others[2:]
            lhs[k + 1], rhs[k + 1] = panel
        for t in others:
            update(t)
    return jnp.concatenate(rhs, axis=0)


def tree(terms):
    while len(terms) > 1:
        terms = [a + b for a, b in zip(terms[::2], terms[1::2])] + terms[len(terms) & ~1 :]
    return terms[0]


def whiten(inner, block):
    size = inner.shape[0]
    count = size // 8
    sub = lax.broadcasted_iota(jnp.int32, (8, 128), 0)
    lhs = [inner[8 * t : 8 * t + 8] for t in range(count)]
    rhs = [block[8 * t : 8 * t + 8] for t in range(count)]
    done = []
    for k in range(count):
        live = range(k, count)
        cols = {t: [lane_copy(lhs[t], 8 * k + j) for j in range(8)] for t in live}
        scale = None
        for j in range(8):
            pivot = row_copy(cols[k][j], j)
            recip = pl.reciprocal(pivot, approx=True)
            root = lax.rsqrt(pivot)
            scale = root if scale is None else jnp.where(sub >= j, root, scale)
            head = {l: row_copy(cols[k][l], j) for l in range(j + 1, 8)}
            row_l, row_r = row_copy(lhs[k], j), row_copy(rhs[k], j)
            for t in live:
                mult = cols[t][j] * recip
                if t == k:
                    mult = jnp.where(sub > j, mult, 0.0)
                for l in range(j + 1, 8):
                    cols[t][l] = cols[t][l] - mult * head[l]
                lhs[t] = lhs[t] - mult[:, : row_l.shape[1]] * row_l
                rhs[t] = rhs[t] - mult * row_r
        done.append(rhs[k] * scale)
    return jnp.concatenate(done, axis=0)


def pieces_of(value):
    high = value.astype(jnp.bfloat16)
    return high, (value - high.astype(jnp.float32)).astype(jnp.bfloat16)


def dot_rows(left, right):
    left_high, left_low = pieces_of(left)
    right_high, right_low = pieces_of(right)
    return lax.dot_general(
        jnp.concatenate([left_high, left_high, left_low], axis=1),
        jnp.concatenate([right_high, right_low, right_high], axis=1),
        (((1,), (1,)), ((), ())),
        preferred_element_type=jnp.float32,
    )


def order_kernel(rows_z, near_ref, far_ref, out_ref):
    planes = near_ref.shape[0] + 2
    rows_y = near_ref.shape[2] // LANES
    piece_rows = planes * rows_y // out_ref.shape[0]
    for p in range(planes):
        inside = 0 < p < planes - 1
        source, at = (near_ref, p - 1) if inside else (far_ref, min(p, 1))
        for y in range(rows_y):
            piece, spot = divmod(p * rows_y + y, piece_rows)
            out_ref[piece, :, pl.ds(spot * rows_z, rows_z)] = source[
                at, :, pl.ds(y * LANES, rows_z)
            ]


def modes_kernel(cell_count, *refs):
    mask_ref, *part_refs, start_ref, snap_hbm, out_ref, snap_ref, sem = refs
    fetch = pltpu.make_async_copy(snap_hbm, snap_ref, sem)
    fetch.start()
    total = part_refs[0][...]
    for part in part_refs[1:]:
        total = total + part[...]
    width = total.shape[1]
    row = lax.broadcasted_iota(jnp.int32, (width, width), 0)
    col = lax.broadcasted_iota(jnp.int32, (width, width), 1)
    packed = total[:width]
    turned = packed.T
    mass = jnp.where(row <= col, packed, turned) * (1.0 / cell_count)
    stiff = jnp.where(row > col, packed, jnp.where(row < col, turned, total[width : width + 1]))
    stiff = stiff * (0.5 / cell_count)
    step = solve_spd(stiff, mass)
    turned_step = step.T
    form = dot_rows(turned_step, dot_rows(turned_step, mass))
    both = jnp.concatenate([form, step], axis=0)
    block = start_ref[...]
    for _ in range(ITERS):
        products = dot_rows(block, both)
        inner = dot_rows(products[:, :width], block)
        block = whiten(inner, products[:, width:])
    modes = block.astype(jnp.bfloat16)
    fetch.wait()
    for piece in range(out_ref.shape[0]):
        basis = jnp.dot(modes, snap_ref[piece], preferred_element_type=jnp.float32)
        wanted = mask_ref[piece] != 0
        out_ref[piece] = jnp.where(wanted, basis.astype(jnp.bfloat16), 0.0)


def on_device(snap_init, channel_map, yface_vals, zface_vals, face_of, start_block, correlation):
    subs = lax.axis_size("sub")
    owner_count = lax.axis_size("nbhd")
    planes, rows_y, rows_z, width = snap_init.shape[1:]
    snap_near, snap_far, own = relax(
        snap_init[0], channel_map[0], yface_vals[0], zface_vals[0], face_of[0]
    )
    parts = [own] + [
        lax.ppermute(own, "sub", [(i, (i + shift) % subs) for i in range(subs)])
        for shift in range(1, subs)
    ]
    cells = planes * rows_y * rows_z
    ordered = pl.pallas_call(
        functools.partial(order_kernel, rows_z),
        out_shape=jax.ShapeDtypeStruct((owner_count, width, cells // owner_count), jnp.bfloat16),
        compiler_params=pltpu.CompilerParams(vmem_limit_bytes=8 * 2**20),
    )(snap_near, snap_far)
    modes = start_block.shape[-1]
    mask = lax.dynamic_slice_in_dim(correlation, lax.axis_index("nbhd"), 1, axis=0)[0]
    pieces = pl.pallas_call(
        functools.partial(modes_kernel, float(subs * cells)),
        out_shape=jax.ShapeDtypeStruct((owner_count, modes, cells // owner_count), jnp.bfloat16),
        in_specs=[pl.BlockSpec(memory_space=pltpu.SMEM)]
        + [pl.BlockSpec(memory_space=pltpu.VMEM)] * (subs + 1)
        + [pl.BlockSpec(memory_space=pltpu.HBM)],
        scratch_shapes=[
            pltpu.VMEM(ordered.shape, ordered.dtype),
            pltpu.SemaphoreType.DMA,
        ],
        compiler_params=pltpu.CompilerParams(vmem_limit_bytes=24 * 2**20),
    )(mask, *parts, start_block[0].T, ordered)
    received = lax.all_to_all(pieces, "nbhd", split_axis=0, concat_axis=0, tiled=True)
    return received[None, None]


def solution(mesh):
    return jax.shard_map(
        on_device,
        mesh=mesh,
        in_specs=(
            P("nbhd", "sub", None, None, None),
            P("nbhd", "sub", None, None),
            P("nbhd", None, None),
            P("nbhd", None, None),
            P("nbhd", None),
            P("nbhd", None, None),
            P(),
        ),
        out_specs=P("nbhd", "sub", None, None, None),
        check_vma=False,
    )
```

```python
import functools

import jax
import jax.numpy as jnp
from jax import lax
from jax.experimental import pallas as pl
from jax.experimental.pallas import tpu as pltpu
from jax.sharding import PartitionSpec as P

SWEEPS = 3
ITERS = 4


def harmonic(left_k, right_k):
    return 2.0 * left_k * right_k / (left_k + right_k)


LANES = 128


def weight_rows(kappa_ref, weights, stiff_rows, lines, first, last, rows_y, rows_z):
    total = kappa_ref.shape[0]
    depth = (total - lines) // 2
    kappa = kappa_ref[...]
    shape = kappa.shape
    line = lax.broadcasted_iota(jnp.int32, shape, 0)
    row_z = lax.broadcasted_iota(jnp.int32, shape, 1)
    row_y = lax.rem(line, rows_y)

    def face(other, edge):
        return jnp.where(edge, kappa, harmonic(kappa, other))

    top = depth + lines
    faces = [
        face(pltpu.roll(kappa, rows_y, 0), (line >= depth) & (line < depth + rows_y * first)),
        face(pltpu.roll(kappa, total - rows_y, 0), (line >= top - rows_y * last) & (line < top)),
        face(pltpu.roll(kappa, 1, 0), row_y == 0),
        face(pltpu.roll(kappa, total - 1, 0), row_y == rows_y - 1),
        face(pltpu.roll(kappa, 1, 1), row_z == 0),
        face(pltpu.roll(kappa, LANES - 1, 1), row_z == rows_z - 1),
    ]
    denom = faces[0] + faces[1] + faces[2] + faces[3] + faces[4] + faces[5]
    outside = (line < depth * first) | (line >= total - depth * last) | (row_z >= rows_z)
    scale = jnp.where(outside, 0.0, 1.0 / denom)
    for k in range(6):
        weights[k] = faces[k] * scale
    upper = row_y >= rows_y // 2
    plane = lax.div(line - depth, rows_y)
    planes = lines // rows_y
    low_cross = jnp.where(upper, 2.0 - 2.0 * first.astype(jnp.float32), 0.0)
    high_cross = jnp.where(upper, 0.0, 2.0 - 2.0 * last.astype(jnp.float32))
    shares = [
        jnp.where(plane == 0, low_cross, jnp.where(plane == 1, 0.0, 1.0)),
        jnp.where(plane == planes - 1, high_cross, jnp.where(plane == planes - 2, 0.0, 1.0)),
        jnp.where(row_y == 0, 0.0, 1.0),
        jnp.where(row_y == rows_y - 1, 0.0, 1.0),
        jnp.where(row_z == 0, 0.0, 1.0),
        jnp.where(row_z == rows_z - 1, 0.0, 1.0),
    ]
    shares[0] = jnp.where(plane == planes - 1, 2.0, shares[0])
    shares[1] = jnp.where(plane == 0, 2.0, shares[1])
    rows = [item * share for item, share in zip(faces, shares)] + [denom, kappa * (1.0 / 16.0)]
    inside = (row_z < rows_z)[depth:top]
    for k in range(8):
        stiff_rows[k] = jnp.where(inside, rows[k][depth:top], 0.0)


def turned(lines):
    width = lines.shape[1]
    row = lax.broadcasted_iota(jnp.int32, (width, width), 0)
    col = lax.broadcasted_iota(jnp.int32, (width, width), 1)
    eye = jnp.where(row == col, 1.0, 0.0).astype(jnp.bfloat16)
    return lax.dot_general(eye, lines, (((1,), (1,)), ((), ())), preferred_element_type=jnp.float32)


def place(line, rows_y):
    return lax.div(line, rows_y), lax.rem(line, rows_y)


def fill(state, source, skip, count, first_line, pad_rows):
    rows_y = pad_rows.shape[0]
    group = 16 if count % 16 == 0 else 8

    def body(i, carry):
        waiting = []

        def store(e, y, both):
            state[e, y + 1] = both[:, :LANES]
            state[e, y + 2] = both[:, LANES:]

        for j in range(0, group, 2):
            at = i * group + j
            e, y = place(first_line + at, rows_y)
            lines = [source[skip + at], pad_rows[y], source[skip + at + 1], pad_rows[y + 1]]
            waiting.append((e, y, turned(jnp.concatenate(lines, axis=0))))
            if len(waiting) > 1:
                store(*waiting.pop(0))
        for item in waiting:
            store(*item)
        return carry

    lax.fori_loop(0, count // group, body, 0)


def neighbour_sum(src, e, y, rows, some, middle):
    return (
        rows[0] * src[e - 1, y + 1, some]
        + rows[1] * src[e + 1, y + 1, some]
        + rows[2] * src[e, y, some]
        + rows[3] * src[e, y + 2, some]
        + rows[4] * pltpu.roll(middle, 1, 1)
        + rows[5] * pltpu.roll(middle, LANES - 1, 1)
    )


PART = 64


def relax_lines(src, dst, weights, first_lines, count, rows_y, rows_z, keep):
    width = src.shape[2]
    group = 8
    total = weights.shape[1] // rows_y
    src_skip = (total - src.shape[0]) // 2
    dst_skip = (total - dst.shape[0]) // 2
    valid = lax.broadcasted_iota(jnp.int32, (PART, LANES), 1) < rows_z

    def body(i, carry):
        waiting = []
        for j in range(group * len(first_lines)):
            line = first_lines[j // group] + i * group + j % group
            e, y = place(line, rows_y)
            rows = [weights[k, pl.ds(line, 1)] for k in range(6)]
            for start in range(0, width, PART):
                some = pl.ds(start, PART)
                middle = src[e - src_skip, y + 1, some]
                fresh = neighbour_sum(src, e - src_skip, y, rows, some, middle)
                fresh = fresh.astype(jnp.bfloat16).astype(jnp.float32)
                if keep:
                    fresh = jnp.where(valid, fresh, middle)
                waiting.append((e - dst_skip, y, some, fresh))
                if len(waiting) > 1:
                    e0, y0, some0, value = waiting.pop(0)
                    dst[e0, y0 + 1, some0] = value
        for e0, y0, some0, value in waiting:
            dst[e0, y0 + 1, some0] = value
        return carry

    lax.fori_loop(0, count // group, body, 0)


def gram_terms(final, places, planes, stiff_rows, snap, both, total):
    _, width, columns = snap.shape
    rows_y = columns // LANES
    for item, e in enumerate(places):
        p = e - planes
        e = e - (3 * planes - final.shape[0]) // 2
        waiting = []

        def store(y, some, below, values, item=item):
            spot = pl.ds(y * LANES, LANES)
            snap[item, some, spot] = values[0]
            both[some, spot] = values[1]
            both[below, spot] = values[2]

        for y in range(rows_y):
            rows = [stiff_rows[k, pl.ds(p * rows_y + y, 1)] for k in range(8)]
            for start in range(0, width, PART):
                some = pl.ds(start, PART)
                middle = final[e, y + 1, some]
                numer = neighbour_sum(final, e, y, rows, some, middle)
                values = [middle, rows[7] * middle, rows[6] * middle - numer]
                values = [value.astype(jnp.bfloat16) for value in values]
                waiting.append((y, some, pl.ds(width + start, PART), values))
                if len(waiting) > 1:
                    store(*waiting.pop(0))
        for entry in waiting:
            store(*entry)
        total = total + lax.dot_general(
            snap[item], both[...], (((1,), (1,)), ((), ())), preferred_element_type=jnp.float32
        )
    return total


def powers(marks):
    return jnp.left_shift(jnp.int32(1), 2 * marks).astype(jnp.float32)


def pack_kernel(flags, class_map, lines, near_a, near_b, classes, sems):
    count, rows_z = classes.shape
    near = near_a.shape[0] - 1
    upward = flags[0]
    fetch = pltpu.make_async_copy(class_map, classes, sems.at[16])
    fetch.start()
    copies = []
    chunk = near // 8
    for out, start in (
        (near_a, upward * (count - near)),
        (near_b, (1 - upward) * (count - near)),
    ):
        for at in range(0, near, chunk):
            copies.append(
                pltpu.make_async_copy(
                    lines.at[pl.ds(start + at, chunk)],
                    out.at[pl.ds(1 + at, chunk)],
                    sems.at[len(copies)],
                )
            )
            copies[-1].start()
    fetch.wait()
    marks = classes[...].astype(jnp.float32).astype(jnp.bfloat16)
    width = near_a.shape[2]
    marks = jnp.concatenate([marks, jnp.zeros((count, width - rows_z), jnp.bfloat16)], axis=1)
    for out in (near_a, near_b):
        out[0, pl.ds(0, count)] = marks
        out[0, pl.ds(count, rows_z - count)] = jnp.zeros((rows_z - count, width), jnp.bfloat16)
    for copy in copies:
        copy.wait()


def own_kernel(
    flags,
    own,
    classes,
    y_vals,
    z_vals,
    face_ids,
    hand,
    inner,
    pad_rows,
    far_a,
    far_b,
    own_kappa,
    state_a,
    state_b,
    kappa,
    weights,
    stiff_rows,
    sems,
):
    lines, rows_z, width = own.shape
    rows_y = pad_rows.shape[0]
    planes = lines // rows_y
    bf16 = jnp.bfloat16
    ids = face_ids[...]
    picks = [(ids == side).astype(jnp.float32) for side in range(4)]
    spare = LANES - rows_z
    spot = lax.broadcasted_iota(jnp.int32, (spare, width), 0)
    z_all = z_vals[...].astype(jnp.float32)
    z_low = z_all * picks[2]
    z_high = z_all * picks[3]
    for y in range(rows_y):
        rows = jnp.where(spot == 0, z_high[y : y + 1], 0.0)
        pad_rows[y] = jnp.where(spot == spare - 1, z_low[y : y + 1], rows).astype(bf16)
    y_all = y_vals[...].astype(jnp.float32)
    blank = jnp.zeros((spare, width), bf16)
    ghost_low = turned(jnp.concatenate([(y_all * picks[0]).astype(bf16), blank], axis=0))
    ghost_high = turned(jnp.concatenate([(y_all * picks[1]).astype(bf16), blank], axis=0))

    def edges(e, carry):
        for state, at in ((state_a, e), (state_b, e - 1)):
            state[at, 0] = ghost_low
            state[at, rows_y + 1] = ghost_high
        return carry

    lax.fori_loop(planes, 2 * planes, edges, 0)
    fill(state_a, own, 0, lines, lines, pad_rows)
    sends = [
        pltpu.make_async_copy(state_a.at[planes + p], hand.at[p], sems.at[p])
        for p in range(planes)
    ]
    for copy in sends:
        copy.start()
    kappa[...] = jnp.ones(kappa.shape, jnp.float32)
    kappa[pl.ds(lines, lines), pl.ds(0, rows_z)] = powers(classes[...])
    own_kappa[...] = kappa[pl.ds(lines, lines)]
    weight_rows(kappa, weights, stiff_rows, lines, flags[1], flags[2], rows_y, rows_z)
    inside = lines - 2 * rows_y
    relax_lines(state_a, state_b, weights, (lines + rows_y,), inside, rows_y, rows_z, True)
    for p in range(planes - 2):
        sends.append(
            pltpu.make_async_copy(state_b.at[planes + p], inner.at[p], sems.at[planes + p])
        )
        sends[-1].start()
    half = rows_y // 2
    far = far_a.shape[0]
    for out, upward in ((far_a, flags[0]), (far_b, 1 - flags[0])):
        out[...] = own[pl.ds(upward * half + (1 - upward) * (lines - half - far), far)]
    for copy in sends:
        copy.wait()


def near_kernel(
    flags,
    near_a,
    near_b,
    own_kappa,
    pad_rows,
    hand,
    inner,
    state_a,
    state_b,
    weights,
    stiff_rows,
    snap,
    gram,
    kappa,
    both,
    sems,
):
    lines = own_kappa.shape[0]
    rows_z = near_a.shape[1]
    rows_y = pad_rows.shape[0]
    near = lines // 2
    planes = lines // rows_y
    taken = []
    cut = (rows_y + 2) // 2
    for source, state, count in ((hand, state_a, planes), (inner, state_b, planes - 2)):
        for p in range(count):
            for start in (0, cut):
                some = pl.ds(start, cut)
                taken.append(
                    pltpu.make_async_copy(
                        source.at[p, some], state.at[planes + p, some], sems.at[len(taken)]
                    )
                )
                taken[-1].start()
    even, first, last = flags[0], flags[1], flags[2]
    base_a = pl.multiple_of(even * (2 * lines), 8)
    base_b = pl.multiple_of((1 - even) * (2 * lines), 8)
    kappa[...] = jnp.ones(kappa.shape, jnp.float32)
    kappa[pl.ds(lines, lines)] = own_kappa[...]
    for base, part in ((base_a, near_a), (base_b, near_b)):
        marks = part[0][:lines].astype(jnp.float32).astype(jnp.int32)
        kappa[pl.ds(base, lines)] = powers(marks)
    weight_rows(kappa, weights, stiff_rows, lines, first, last, rows_y, rows_z)
    fill(state_a, near_a, 1, near, near + even * (lines + near), pad_rows)
    fill(state_a, near_b, 1, near, near + (1 - even) * (lines + near), pad_rows)
    for copy in taken:
        copy.wait()
    ghost_low = state_a[planes, 0]
    ghost_high = state_a[planes, rows_y + 1]
    for e in range(1, 3 * planes - 1):
        if e not in range(planes, 2 * planes):
            state_a[e, 0] = ghost_low
            state_a[e, rows_y + 1] = ghost_high
        if e not in range(planes + 1, 2 * planes - 1):
            state_b[e - 1, 0] = ghost_low
            state_b[e - 1, rows_y + 1] = ghost_high
    step = functools.partial(relax_lines, weights=weights, rows_y=rows_y, rows_z=rows_z)
    ends = (lines - rows_y, 2 * lines - rows_y)
    step(state_a, state_b, first_lines=ends, count=2 * rows_y, keep=True)
    step(state_b, state_a, first_lines=(lines,), count=lines, keep=True)
    inner = (lines + rows_y,)
    step(state_a, state_b, first_lines=inner, count=lines - 2 * rows_y, keep=False)
    inside = range(planes + 1, 2 * planes - 1)
    blank = jnp.zeros(gram.shape, jnp.float32)
    gram[...] = gram_terms(state_b, inside, planes, stiff_rows, snap, both, blank)


def advance(buffers, weights, low_line, count, total, rows_y, rows_z):
    for sweep in range(1, SWEEPS + 1):
        src, dst = buffers[(sweep - 1) % 2], buffers[sweep % 2]
        low = low_line + sweep * rows_y
        ends = (low, total - low - count)
        relax_lines(src, dst, weights, ends, count, rows_y, rows_z, sweep < SWEEPS)


def far_kernel(
    flags,
    far_a,
    far_b,
    weights,
    stiff_rows,
    pad_rows,
    near_gram,
    old_a,
    old_b,
    state_a,
    state_b,
    snap,
    gram,
    both,
):
    del old_a, old_b
    width = snap.shape[1]
    rows_y = pad_rows.shape[0]
    count, rows_z = far_a.shape[:2]
    planes = stiff_rows.shape[1] // rows_y
    lines = weights.shape[1]
    half = rows_y // 2
    shift = flags[0] * (lines - 2 * half - count)
    fill(state_a, far_a, 0, count, half + shift, pad_rows)
    fill(state_a, far_b, 0, count, lines - half - count - shift, pad_rows)
    buffers = (state_a, state_b)
    advance(buffers, weights, half, count, lines, rows_y, rows_z)
    final = buffers[SWEEPS % 2]
    outer = (planes, 2 * planes - 1)
    total = gram_terms(final, outer, planes, stiff_rows, snap, both, near_gram[...])
    mass = total[:, :width]
    stiff = total[:, width:]
    stiff = stiff + stiff.T
    row = lax.broadcasted_iota(jnp.int32, (width, width), 0)
    col = lax.broadcasted_iota(jnp.int32, (width, width), 1)
    gram[pl.ds(0, width)] = jnp.where(row > col, stiff, mass)
    diagonal = jnp.sum(jnp.where(row == col, stiff, 0.0), axis=0, keepdims=True)
    gram[pl.ds(width, 8)] = jnp.broadcast_to(diagonal, (8, width))


def swap(array, start):
    count = lax.axis_size("sub")
    pairs = [(i, i + 1) for i in range(start, count - 1, 2)]
    return lax.ppermute(array, "sub", pairs + [(j, i) for i, j in pairs])


def relax(initial, classes, y_vals, z_vals, face_ids):
    planes, rows_y, rows_z, width = initial.shape
    index = lax.axis_index("sub")
    subs = lax.axis_size("sub")
    even = (index + 1) % 2
    flags = jnp.stack([even, index == 0, index == subs - 1, 0]).astype(jnp.int32)
    lines = initial.reshape(planes * rows_y, rows_z, width)
    count = planes * rows_y
    near, half = 2 * rows_y, rows_y // 2
    flat_classes = classes.reshape(count, rows_z)
    part = functools.partial(jax.ShapeDtypeStruct, dtype=initial.dtype)
    vmem = pl.BlockSpec(memory_space=pltpu.VMEM)
    smem = pl.BlockSpec(memory_space=pltpu.SMEM)
    hbm = pl.BlockSpec(memory_space=pltpu.HBM)
    first_state = pltpu.VMEM((3 * planes, rows_y + 2, width, LANES), jnp.float32)
    second_state = pltpu.VMEM((3 * planes - 2, rows_y + 2, width, LANES), jnp.float32)
    kappa = pltpu.VMEM((3 * count, LANES), jnp.float32)
    both = pltpu.VMEM((2 * width, rows_y * LANES), jnp.bfloat16)
    params = pltpu.CompilerParams(vmem_limit_bytes=8 * 2**20)

    def kept(depth):
        return jax.ShapeDtypeStruct((depth, width, rows_y * LANES), jnp.bfloat16)

    def in_hbm(item):
        return pltpu.with_memory_space_constraint(item, pltpu.HBM)

    def held(item):
        return pltpu.with_memory_space_constraint(item, pltpu.VMEM)

    rows = [
        jax.ShapeDtypeStruct((6, 3 * count, LANES), jnp.float32),
        jax.ShapeDtypeStruct((8, count, LANES), jnp.float32),
    ]
    near_a, near_b = pl.pallas_call(
        pack_kernel,
        out_shape=[part((near + 1, rows_z, width))] * 2,
        in_specs=[smem] + [hbm] * 2,
        out_specs=[vmem] * 2,
        scratch_shapes=[
            pltpu.VMEM((count, rows_z), jnp.int32),
            pltpu.SemaphoreType.DMA((17,)),
        ],
        compiler_params=params,
    )(flags, in_hbm(flat_classes), in_hbm(lines))
    near_a = swap(near_a, 0)
    near_b = swap(near_b, 1)
    hand, inner, pad_rows, far_a, far_b, own_kappa = pl.pallas_call(
        own_kernel,
        out_shape=[
            pltpu.HBM((planes,) + first_state.shape[1:], jnp.float32),
            pltpu.HBM((planes - 2,) + first_state.shape[1:], jnp.float32),
            part((rows_y, LANES - rows_z, width)),
            part((rows_y + half, rows_z, width)),
            part((rows_y + half, rows_z, width)),
            jax.ShapeDtypeStruct((count, LANES), jnp.float32),
        ],
        in_specs=[smem] + [vmem] * 5,
        out_specs=[hbm] * 2 + [vmem] * 4,
        scratch_shapes=[first_state, second_state, kappa]
        + [pltpu.VMEM(item.shape, item.dtype) for item in rows]
        + [pltpu.SemaphoreType.DMA((2 * planes - 2,))],
        compiler_params=pltpu.CompilerParams(vmem_limit_bytes=40 * 2**20),
    )(flags, lines, flat_classes, y_vals, z_vals, face_ids[None])
    far_a = swap(far_a, 0)
    far_b = swap(far_b, 1)
    state_a, state_b, weights, stiff_rows, snap_near, gram_near = pl.pallas_call(
        near_kernel,
        out_shape=[
            first_state,
            second_state,
            *rows,
            kept(planes - 2),
            jax.ShapeDtypeStruct((width, 2 * width), jnp.float32),
        ],
        in_specs=[smem] + [vmem] * 4 + [hbm] * 2,
        out_specs=[vmem] * 6,
        scratch_shapes=[kappa, both, pltpu.SemaphoreType.DMA((4 * planes - 4,))],
        compiler_params=params,
    )(flags, near_a, near_b, own_kappa, pad_rows, in_hbm(hand), in_hbm(inner))
    _, _, snap_far, gram = pl.pallas_call(
        far_kernel,
        out_shape=[
            first_state,
            second_state,
            kept(2),
            jax.ShapeDtypeStruct((width + 8, width), jnp.float32),
        ],
        in_specs=[smem] + [vmem] * 8,
        out_specs=[vmem] * 4,
        scratch_shapes=[both],
        input_output_aliases={7: 0, 8: 1},
        compiler_params=params,
    )(
        flags,
        far_a,
        far_b,
        weights,
        stiff_rows,
        pad_rows,
        gram_near,
        held(state_a),
        held(state_b),
    )
    return snap_near, snap_far, gram


def lane_copy(tile, lane):
    return jnp.broadcast_to(tile[:, lane : lane + 1], (8, 128))


def row_copy(tile, row):
    return jnp.broadcast_to(tile[row : row + 1, :], (8, tile.shape[1]))


def pivot_pairs(left, right, first_lane, heads):
    sub = lax.broadcasted_iota(jnp.int32, (8, 128), 0)
    cols = [lane_copy(left, first_lane + j) for j in range(8)]
    for j in range(0, 8, 2):
        first, second = cols[j], cols[j + 1]
        p, q, s = row_copy(first, j), row_copy(second, j), row_copy(second, j + 1)
        det = p * s - q * q
        recip = pl.reciprocal(det, approx=True)
        a, b, c = s * recip, q * recip, p * recip
        first = first - jnp.where(sub == j, 1.0, 0.0)
        second = second - jnp.where(sub == j + 1, 1.0, 0.0)

        def reduce(tile, j=j, a=a, b=b, c=c, first=first, second=second):
            w = tile.shape[1]
            r0, r1 = row_copy(tile, j), row_copy(tile, j + 1)
            x0 = a[:, :w] * r0 - b[:, :w] * r1
            x1 = c[:, :w] * r1 - b[:, :w] * r0
            return tile - (first[:, :w] * x0 + second[:, :w] * x1)

        if heads is not None:
            r0, r1 = row_copy(right, j), row_copy(right, j + 1)
            inverse = pl.reciprocal(p, approx=True)
            heads.append(r0 * lax.rsqrt(p))
            heads.append((r1 - (q * inverse) * r0) * lax.rsqrt(det * inverse))
        for l in range(j + 2, 8):
            cols[l] = reduce(cols[l])
        left, right = reduce(left), reduce(right)
        yield left, right


def gather_rows(rows):
    sub = lax.broadcasted_iota(jnp.int32, rows[0].shape, 0)
    out = rows[0]
    for i in range(1, 8):
        out = jnp.where(sub == i, rows[i], out)
    return out


def unit_diagonal(matrix):
    row = lax.broadcasted_iota(jnp.int32, matrix.shape, 0)
    col = lax.broadcasted_iota(jnp.int32, matrix.shape, 1)
    diagonal = jnp.where(row == col, matrix, 0.0)
    across = lax.rsqrt(jnp.sum(diagonal, axis=0, keepdims=True))
    down = lax.rsqrt(jnp.sum(diagonal, axis=1, keepdims=True))
    return across, down


def solve_spd(left, right):
    size = left.shape[0]
    count = size // 8
    across, down = unit_diagonal(left)
    left = left * across * down
    right = right * down
    lhs = [left[8 * t : 8 * t + 8] for t in range(count)]
    rhs = [right[8 * t : 8 * t + 8] for t in range(count)]
    for panel in pivot_pairs(lhs[0], rhs[0], 0, None):
        lhs[0], rhs[0] = panel
    for k in range(count):
        rows_l = [row_copy(lhs[k], j) for j in range(8)]
        rows_r = [row_copy(rhs[k], j) for j in range(8)]

        def update(t, k=k, rows_l=rows_l, rows_r=rows_r):
            tile_cols = [lane_copy(lhs[t], 8 * k + j) for j in range(8)]
            if k + 1 < count:
                lhs[t] = lhs[t] - tree([tile_cols[j] * rows_l[j] for j in range(8)])
            rhs[t] = rhs[t] - tree([tile_cols[j] * rows_r[j] for j in range(8)])

        others = [t for t in range(count) if t not in (k, k + 1)]
        if k + 1 < count:
            update(k + 1)
            panel = None
            for panel in pivot_pairs(lhs[k + 1], rhs[k + 1], 8 * (k + 1), None):
                for t in others[:4]:
                    update(t)
                others = others[4:]
            lhs[k + 1], rhs[k + 1] = panel
        for t in others:
            update(t)
    return jnp.concatenate(rhs, axis=0) * down


def tree(terms):
    while len(terms) > 1:
        terms = [a + b for a, b in zip(terms[::2], terms[1::2])] + terms[len(terms) & ~1 :]
    return terms[0]


def whiten(inner, block):
    size = inner.shape[0]
    count = size // 8
    across, down = unit_diagonal(inner)
    inner = inner * across * down
    block = block * down
    lhs = [inner[8 * t : 8 * t + 8] for t in range(count)]
    rhs = [block[8 * t : 8 * t + 8] for t in range(count)]
    done = []
    for k in range(count):
        heads = []
        panel = None
        for panel in pivot_pairs(lhs[k], rhs[k], 8 * k, heads):
            pass
        done.append(gather_rows(heads))
        rows_l = [row_copy(panel[0], j) for j in range(8)]
        rows_r = [row_copy(panel[1], j) for j in range(8)]
        for t in range(k + 1, count):
            tile_cols = [lane_copy(lhs[t], 8 * k + j) for j in range(8)]
            lhs[t] = lhs[t] - tree([tile_cols[j][:, :size] * rows_l[j] for j in range(8)])
            rhs[t] = rhs[t] - tree([tile_cols[j] * rows_r[j] for j in range(8)])
    return jnp.concatenate(done, axis=0)


def pieces_of(value):
    high = value.astype(jnp.bfloat16)
    return high, (value - high.astype(jnp.float32)).astype(jnp.bfloat16)


def dot_rows(left, right):
    left_high, left_low = pieces_of(left)
    right_high, right_low = pieces_of(right)
    return lax.dot_general(
        jnp.concatenate([left_high, left_high, left_low], axis=1),
        jnp.concatenate([right_high, right_low, right_high], axis=1),
        (((1,), (1,)), ((), ())),
        preferred_element_type=jnp.float32,
    )


def order_kernel(rows_z, near_ref, far_ref, out_ref):
    planes = near_ref.shape[0] + 2
    rows_y = near_ref.shape[2] // LANES
    piece_rows = planes * rows_y // out_ref.shape[0]
    for p in range(planes):
        inside = 0 < p < planes - 1
        source, at = (near_ref, p - 1) if inside else (far_ref, min(p, 1))
        for y in range(rows_y):
            piece, spot = divmod(p * rows_y + y, piece_rows)
            out_ref[piece, :, pl.ds(spot * rows_z, rows_z)] = source[
                at, :, pl.ds(y * LANES, rows_z)
            ]


def modes_kernel(cell_count, *refs):
    mask_ref, *part_refs, start_ref, snap_hbm, out_ref, snap_ref, sem = refs
    fetch = pltpu.make_async_copy(snap_hbm, snap_ref, sem)
    fetch.start()
    total = part_refs[0][...]
    for part in part_refs[1:]:
        total = total + part[...]
    width = total.shape[1]
    row = lax.broadcasted_iota(jnp.int32, (width, width), 0)
    col = lax.broadcasted_iota(jnp.int32, (width, width), 1)
    packed = total[:width]
    turned = packed.T
    mass = jnp.where(row <= col, packed, turned) * (1.0 / cell_count)
    stiff = jnp.where(row > col, packed, jnp.where(row < col, turned, total[width : width + 1]))
    stiff = stiff * (0.5 / cell_count)
    step = solve_spd(stiff, mass)
    turned_step = step.T
    form = dot_rows(turned_step, dot_rows(turned_step, mass))
    both = jnp.concatenate([form, step], axis=0)
    block = start_ref[...]
    for _ in range(ITERS):
        products = dot_rows(block, both)
        inner = dot_rows(products[:, :width], block)
        block = whiten(inner, products[:, width:])
    modes = block.astype(jnp.bfloat16)
    fetch.wait()
    for piece in range(out_ref.shape[0]):
        basis = jnp.dot(modes, snap_ref[piece], preferred_element_type=jnp.float32)
        wanted = mask_ref[piece] != 0
        out_ref[piece] = jnp.where(wanted, basis.astype(jnp.bfloat16), 0.0)


def on_device(snap_init, channel_map, yface_vals, zface_vals, face_of, start_block, correlation):
    subs = lax.axis_size("sub")
    owner_count = lax.axis_size("nbhd")
    planes, rows_y, rows_z, width = snap_init.shape[1:]
    snap_near, snap_far, own = relax(
        snap_init[0], channel_map[0], yface_vals[0], zface_vals[0], face_of[0]
    )
    parts = [own] + [
        lax.ppermute(own, "sub", [(i, (i + shift) % subs) for i in range(subs)])
        for shift in range(1, subs)
    ]
    cells = planes * rows_y * rows_z
    ordered = pl.pallas_call(
        functools.partial(order_kernel, rows_z),
        out_shape=jax.ShapeDtypeStruct((owner_count, width, cells // owner_count), jnp.bfloat16),
        compiler_params=pltpu.CompilerParams(vmem_limit_bytes=8 * 2**20),
    )(snap_near, snap_far)
    modes = start_block.shape[-1]
    mask = lax.dynamic_slice_in_dim(correlation, lax.axis_index("nbhd"), 1, axis=0)[0]
    pieces = pl.pallas_call(
        functools.partial(modes_kernel, float(subs * cells)),
        out_shape=jax.ShapeDtypeStruct((owner_count, modes, cells // owner_count), jnp.bfloat16),
        in_specs=[pl.BlockSpec(memory_space=pltpu.SMEM)]
        + [pl.BlockSpec(memory_space=pltpu.VMEM)] * (subs + 1)
        + [pl.BlockSpec(memory_space=pltpu.HBM)],
        scratch_shapes=[
            pltpu.VMEM(ordered.shape, ordered.dtype),
            pltpu.SemaphoreType.DMA,
        ],
        compiler_params=pltpu.CompilerParams(vmem_limit_bytes=24 * 2**20),
    )(mask, *parts, start_block[0].T, ordered)
    received = lax.all_to_all(pieces, "nbhd", split_axis=0, concat_axis=0, tiled=True)
    return received[None, None]


def solution(mesh):
    return jax.shard_map(
        on_device,
        mesh=mesh,
        in_specs=(
            P("nbhd", "sub", None, None, None),
            P("nbhd", "sub", None, None),
            P("nbhd", None, None),
            P("nbhd", None, None),
            P("nbhd", None),
            P("nbhd", None, None),
            P(),
        ),
        out_specs=P("nbhd", "sub", None, None, None),
        check_vma=False,
    )
```
